32 devices in a mesh: rep: 4 (over y, core), shard: 8 (over z, x).
Axes of the slice: x: 2, y: 2, z: 4, core: 2. Of those that a mesh axis runs over, the one named last changes fastest.
Arguments:
- tokens: bfloat16 [8192, 1024], P(('rep', 'shard')), may hold values from -6 to 6
- cotangent: bfloat16 [8192, 1024], P(('rep', 'shard')), may hold values from -6 to 6
- qkv_weight: float32 [1024, 3072], P('shard'), may hold values from -0.1875 to 0.1875
- out_weight: float32 [1024, 1024], P('shard'), may hold values from -3 to 3
- up_weight: float32 [1024, 4096], P('shard'), may hold values from -0.1875 to 0.1875
- down_weight: float32 [4096, 1024], P('shard'), may hold values from -0.09375 to 0.09375
- gain_attn: float32 [1024], P('shard'), may hold values from 0.5 to 1.5
- gain_ffn: float32 [1024], P('shard'), may hold values from 0.5 to 1.5
- parents: int32 [4, 16], P('rep'), may hold values from 0 to 11, as said below
- slot_ids: int32 [64], P('rep'), may hold values from 0 to 15, as said below
Outputs:
- layer_out: bfloat16 [8192, 1024], P(('rep', 'shard'))
- input_grad: float32 [8192, 1024], P(('rep', 'shard'))
- qkv_grad: float32 [1024, 3072], P('shard')
- out_grad: float32 [1024, 1024], P('shard')
- up_grad: float32 [1024, 4096], P('shard')
- down_grad: float32 [4096, 1024], P('shard')
- attn_gain_grad: float32 [1024], P('shard')
- ffn_gain_grad: float32 [1024], P('shard')
The draws below stay inside these ranges and needn't reach their ends.
Inputs may be any that keep to these rules, and one draw needn't show every extreme that they name: parents[t, 0] = 0; segment s of the trunk (1 <= s < 10) has parent s - 1; the 2 branch segments 10 .. 11 have parent 10 - 1; every later segment is a leaf whose parent is one of the branches, the last segment's parent being the last branch. `slot_ids`: each aligned block of 16 slots (one group) holds each number 0 .. 15 exactly once.
All inputs are finite; a program needn't handle non-finite values.
Results may differ from the reference program's by a relative error of at most 0.019.
Values may be sent and summed in bfloat16 or wider, within the bound.
A program may use at most 384 MiB of HBM per device.

```python
import jax
import jax.numpy as jnp
from jax import lax

D = 1024
FF = 4096
HEADS = 16
HEAD = 64
TRUNK = 10
BRANCHES = 2
SEG = 128
TREE_SEGS = 16
GROUP_SEGS = 16
TREES = 4
TOKENS = 8192
SLOTS = 64


def draw_parents(key, part):
    seg_range = jnp.arange(TREE_SEGS, dtype=jnp.int32)[None, :]
    trunk_parent = jnp.maximum(seg_range - 1, 0)
    leaf_parent = TRUNK + jax.random.randint(key, (TREES, TREE_SEGS), 0, BRANCHES, dtype=jnp.int32)
    leaf_parent = jnp.where(seg_range == TREE_SEGS - 1, TRUNK + BRANCHES - 1, leaf_parent)
    chosen = jnp.where(seg_range < TRUNK, trunk_parent, jnp.where(seg_range < TRUNK + BRANCHES, TRUNK - 1, leaf_parent))
    return chosen.astype(jnp.int32)


def draw_slot_ids(key, part):
    groups = SLOTS // GROUP_SEGS
    scores = jax.random.randint(key, (groups, GROUP_SEGS), 0, 1 << 20, dtype=jnp.int32) * GROUP_SEGS
    scores = scores + jnp.arange(GROUP_SEGS, dtype=jnp.int32)[None, :]
    ranking = jnp.argsort(scores, axis=1, stable=True)
    return ranking.reshape(-1).astype(jnp.int32)


def with_spikes(drawn, rng, source, target, blocks, factor):
    owner, partner = [(jnp.arange(drawn.shape[dim]) // (drawn.shape[dim] // blocks)).reshape([-1 if axis == dim else 1 for axis in range(drawn.ndim)]) for dim in (source, target)]
    chosen = jax.random.permutation(rng, blocks)[partner]
    strong = (owner == chosen) | (owner == (partner + blocks // 2) % blocks)
    return jnp.where(strong, factor * drawn, drawn)


def block_scale(key, extent, split, smallest, high):
    def one(dim, parts):
        draws = jax.random.uniform(jax.random.fold_in(jax.random.fold_in(key, 6), dim), (parts,), jnp.float32, smallest / len(split), high / len(split))
        return jnp.repeat(jnp.exp(draws), extent[dim] // parts).reshape((-1,) + (1,) * (len(extent) - dim - 1))

    loudness = one(*split[0])
    for cut in split[1:]:
        loudness = loudness * one(*cut)
    return loudness


def bell_draw(stream_key, shape, spread, bound, split=(), kind=jnp.bfloat16):
    gain = block_scale(stream_key, shape, split, -0.22, 0.18) if split else 1.0
    drawn = jax.random.normal(stream_key, shape, jnp.float32) * spread * gain
    return jnp.minimum(jnp.maximum(drawn, -bound), bound).astype(kind)


def heavy_noise(own_key, extent, spread, bound, shards, heavy, held_as=jnp.bfloat16):
    drawn = spread * jax.random.normal(own_key, extent, jnp.float32)
    if shards:
        drawn = drawn * block_scale(own_key, extent, shards, -0.22, 0.18)
    return jnp.clip(with_spikes(drawn, jax.random.fold_in(own_key, 3), *heavy), -bound, bound).astype(held_as)


def setup_inputs(seed: int = 0) -> dict:
    seeds = jax.random.split(jax.random.key(seed), 11)
    tokens = bell_draw(seeds[0], (TOKENS, D), 1.0, 6.0, ((0, 32),))
    cotangent = heavy_noise(seeds[1], (TOKENS, D), 1.0, 6.0, ((0, 32),), (0, 1, 32, 2.75))
    qkv_weight = bell_draw(seeds[2], (D, 3 * D), D ** -0.5, 0.1875, ((0, 8),), jnp.float32)
    out_weight = bell_draw(seeds[3], (D, D), (max(1, D // 256)) ** -0.5, 3.0, ((0, 8),), jnp.float32)
    up_weight = bell_draw(seeds[4], (D, FF), D ** -0.5, 0.1875, ((0, 8),), jnp.float32)
    down_weight = bell_draw(seeds[5], (FF, D), FF ** -0.5, 0.09375, ((0, 8),), jnp.float32)
    gain_attn = jnp.clip(1.0 + 0.1 * jax.random.normal(seeds[6], (D,), jnp.float32), 0.5, 1.5)
    gain_ffn = jnp.clip(1.0 + 0.1 * jax.random.normal(seeds[7], (D,), jnp.float32), 0.5, 1.5)
    parents = draw_parents(jax.random.fold_in(seeds[10], 71), 0)
    slot_ids = draw_slot_ids(jax.random.fold_in(seeds[10], 71), 0)
    return {"tokens": tokens, "cotangent": cotangent, "qkv_weight": qkv_weight, "out_weight": out_weight, "up_weight": up_weight, "down_weight": down_weight, "gain_attn": gain_attn, "gain_ffn": gain_ffn, "parents": parents, "slot_ids": slot_ids}


@jax.custom_vjp
def low(v):
    return lax.optimization_barrier(v.astype(jnp.bfloat16)).astype(jnp.float32)

@jax.custom_vjp
def low_back(v):
    return v

def low_keep(v):
    return (low(v), None)

def low_pass(kept, grad):
    return (grad,)

def back_keep(v):
    return (v, None)

def back_low(kept, grad):
    return (low(grad),)
low.defvjp(low_keep, low_pass)
low_back.defvjp(back_keep, back_low)

def normalize(values):
    average = lax.optimization_barrier(jnp.mean(values, axis=-1, keepdims=True))
    centered = values - average
    variance = lax.optimization_barrier(jnp.mean(centered * centered, axis=-1, keepdims=True))
    return centered * lax.rsqrt(variance + 1e-05)

def gelu_exact(values):
    return 0.5 * values * (1.0 + lax.erf(values * 0.7071067811865476))

def matmul(left_side, right_side):
    return jnp.dot(left_side, right_side, precision=lax.Precision.HIGHEST, preferred_element_type=jnp.float32)

def ancestors(parent_row):
    seg_range = jnp.arange(TREE_SEGS, dtype=jnp.int32)
    walker = seg_range
    reached = walker[:, None] == seg_range[None, :]
    for repeat in range(TREE_SEGS):
        walker = parent_row[walker]
        reached = reached | (walker[:, None] == seg_range[None, :])
    return reached

def attend_tree(packed):
    qkv_tree, allowed_seg = packed
    tree_rows = qkv_tree.shape[0]
    queries = qkv_tree[:, :D].reshape(tree_rows, HEADS, HEAD)
    keys_all = qkv_tree[:, D:2 * D].reshape(tree_rows, HEADS, HEAD)
    values_all = qkv_tree[:, 2 * D:].reshape(tree_rows, HEADS, HEAD)
    scores = low_back(0.125 * jnp.einsum('qhd,khd->hqk', queries, keys_all, precision=lax.Precision.HIGHEST))
    rows_index = jnp.arange(tree_rows, dtype=jnp.int32)
    seg_index = rows_index // SEG
    visible = allowed_seg[seg_index][:, seg_index]
    visible = visible & ((seg_index[:, None] != seg_index[None, :]) | (rows_index[None, :] <= rows_index[:, None]))
    scores = jnp.where(visible[None], scores, -1e+30)
    weights = jax.nn.softmax(scores, axis=-1)
    mixture = jnp.einsum('hqk,khd->qhd', low(weights), values_all, precision=lax.Precision.HIGHEST)
    return mixture.reshape(tree_rows, D)

def reference(tokens, cotangent, qkv_weight, out_weight, up_weight, down_weight, gain_attn, gain_ffn, parents, slot_ids):
    groups = SLOTS // GROUP_SEGS
    slot_order = jnp.argsort(slot_ids.reshape(groups, GROUP_SEGS), axis=1).astype(jnp.int32)
    slot_base = (jnp.arange(groups, dtype=jnp.int32) * GROUP_SEGS)[:, None] + slot_order
    row_index = (slot_base.reshape(-1)[:, None] * SEG + jnp.arange(SEG, dtype=jnp.int32)[None, :]).reshape(-1)
    inverse = jnp.argsort(row_index).astype(jnp.int32)
    allowed = jax.vmap(ancestors)(parents)

    def forward(inputs, qkv_matrix, out_matrix, up_matrix, down_matrix, attn_gain, ffn_gain):
        entered = low(normalize(inputs) * low(attn_gain))
        qkv_all = low(low_back(matmul(entered, low(qkv_matrix))))
        attended = lax.map(jax.checkpoint(attend_tree), (qkv_all.reshape(TREES, -1, 3 * D), allowed))
        attn_out = low(low_back(attended.reshape(-1, D)))
        hidden = inputs + low_back(matmul(attn_out, low(out_matrix)))
        second = low(normalize(hidden) * low(ffn_gain))
        pre_act = low_back(matmul(second, low(up_matrix)))
        active = low(low_back(gelu_exact(pre_act)))
        return hidden + low_back(matmul(active, low(down_matrix)))
    inputs_sorted = tokens.astype(jnp.float32)[row_index]
    cot_sorted = cotangent.astype(jnp.float32)[row_index]
    result, pullback = jax.vjp(forward, inputs_sorted, qkv_weight, out_weight, up_weight, down_weight, gain_attn, gain_ffn)
    gradients = pullback(cot_sorted)
    output = result[inverse].astype(jnp.bfloat16)
    return (output, gradients[0][inverse], gradients[1], gradients[2], gradients[3], gradients[4], gradients[5], gradients[6])
```

```python
import jax
import jax.numpy as jnp
from jax import lax
from jax.experimental import pallas as pl
from jax.experimental.pallas import tpu as pltpu
from jax.sharding import PartitionSpec as P

HEADS = 16
HEAD = 64


masked_score = -1e30


def block_size():
    return 512


def normalize(values):
    average = jnp.mean(values, axis=-1, keepdims=True)
    centered = values - average
    variance = jnp.mean(centered * centered, axis=-1, keepdims=True)
    inv_std = lax.rsqrt(variance + 1e-05)
    return (centered * inv_std, inv_std)


def gelu_exact(values):
    return 0.5 * values * (1.0 + lax.erf(values * 0.7071067811865476))


def gelu_slope(values):
    return (
        0.5 * (1.0 + lax.erf(values * 0.7071067811865476))
        + values * jnp.exp(-0.5 * values * values) * 0.3989422804014327
    )


def norm_back(grad_normed, normed, inv_std):
    first_mean = jnp.mean(grad_normed, axis=-1, keepdims=True)
    second_mean = jnp.mean(grad_normed * normed, axis=-1, keepdims=True)
    return inv_std * (grad_normed - first_mean - normed * second_mean)


def times_t(left_side, right_side):
    return lax.dot_general(
        left_side, right_side, (((1,), (1,)), ((), ())), preferred_element_type=jnp.float32
    )


def t_times(left_side, right_side):
    return lax.dot_general(
        left_side, right_side, (((0,), (0,)), ((), ())), preferred_element_type=jnp.float32
    )


def exact_dot(left_side, right_side):
    return jnp.dot(
        left_side, right_side, precision=lax.Precision.HIGHEST, preferred_element_type=jnp.float32
    )


def slot_table(group_ids, parents):
    tree_segs = parents.shape[1]
    group_segs = group_ids.shape[0]
    seg_range = jnp.arange(tree_segs, dtype=jnp.int32)
    walker = seg_range[None, :]
    reached = walker[:, :, None] == seg_range[None, None, :]

    def climb(step_index, carried):
        walker_now, reached_now = carried
        walker_now = jnp.sum(
            jnp.where(walker_now[:, :, None] == seg_range[None, None, :], parents[:, None, :], 0),
            axis=2,
        )
        return (walker_now, reached_now | (walker_now[:, :, None] == seg_range[None, None, :]))

    walker, reached = lax.fori_loop(0, tree_segs, climb, (walker, reached))
    anc_flat = reached.reshape(group_segs, tree_segs).astype(jnp.float32)
    id_picks = (group_ids[:, None] == jnp.arange(group_segs, dtype=jnp.int32)[None, :]).astype(
        jnp.float32
    )
    seg_rows = exact_dot(id_picks, anc_flat)
    local_pick = ((group_ids % tree_segs)[:, None] == seg_range[None, :]).astype(jnp.float32)
    tree_of = group_ids // tree_segs
    same_tree = (tree_of[:, None] == tree_of[None, :]).astype(jnp.float32)
    return (
        lax.dot_general(
            seg_rows,
            local_pick,
            (((1,), (1,)), ((), ())),
            precision=lax.Precision.HIGHEST,
            preferred_element_type=jnp.float32,
        )
        * same_tree
    )


def visible_mask(allowed, seg_len, query_start, query_rows, key_start, key_rows):
    group_segs = allowed.shape[0]
    query_index = query_start + jnp.arange(query_rows, dtype=jnp.int32)
    key_index = key_start + jnp.arange(key_rows, dtype=jnp.int32)
    query_slot = query_index // seg_len
    key_slot = key_index // seg_len
    seg_range = jnp.arange(group_segs, dtype=jnp.int32)
    query_pick = (query_slot[:, None] == seg_range[None, :]).astype(jnp.float32)
    key_pick = (key_slot[:, None] == seg_range[None, :]).astype(jnp.float32)
    linked = (
        lax.dot_general(
            exact_dot(query_pick, allowed),
            key_pick,
            (((1,), (1,)), ((), ())),
            precision=lax.Precision.HIGHEST,
            preferred_element_type=jnp.float32,
        )
        > 0.5
    )
    return linked & (
        (query_slot[:, None] != key_slot[None, :]) | (key_index[None, :] <= query_index[:, None])
    )


def pair_terms(query_part, grad_part, stat_part, delta_part, key_part, value_part, visible):
    scores = (
        jnp.einsum("qhd,khd->qhk", query_part, key_part, preferred_element_type=jnp.float32) * 0.125
    )
    scores = jnp.where(visible[:, None, :], scores, masked_score)
    probs_full = jnp.exp(scores - stat_part[:, :, None])
    grad_probs = jnp.einsum(
        "qhd,khd->qhk", grad_part, value_part, preferred_element_type=jnp.float32
    )
    grad_scores = (probs_full * (grad_probs - delta_part[:, :, None])).astype(jnp.bfloat16)
    grad_query = None
    grad_key = None
    grad_value = None
    grad_query = (
        jnp.einsum("qhk,khd->qhd", grad_scores, key_part, preferred_element_type=jnp.float32)
        * 0.125
    )
    grad_key = (
        jnp.einsum("qhk,qhd->khd", grad_scores, query_part, preferred_element_type=jnp.float32)
        * 0.125
    )
    grad_value = jnp.einsum(
        "qhk,qhd->khd",
        probs_full.astype(jnp.bfloat16),
        grad_part,
        preferred_element_type=jnp.float32,
    )
    return (grad_query, grad_key, grad_value)


def shards(
    tokens,
    cotangent,
    qkv_weight,
    out_weight,
    up_weight,
    down_weight,
    gain_attn,
    gain_ffn,
    parents,
    slot_ids,
):
    local_rows = tokens.shape[0]
    model_width = tokens.shape[1]
    shard_count = lax.axis_size("shard")
    my_start = lax.axis_index("shard") * local_rows
    seg_len = local_rows * shard_count // slot_ids.shape[0]
    allowed = slot_table(slot_ids, parents)
    qkv_full, out_full, attn_gain = (
        lax.all_gather(qkv_weight.astype(jnp.bfloat16), "shard", axis=0, tiled=True),
        lax.all_gather(out_weight.astype(jnp.bfloat16), "shard", axis=0, tiled=True),
        lax.all_gather(gain_attn.astype(jnp.bfloat16), "shard", axis=0, tiled=True),
    )
    inputs = tokens.astype(jnp.float32)
    normed_one, inv_one = normalize(inputs)
    entered = (normed_one * attn_gain.astype(jnp.float32)).astype(jnp.bfloat16)
    qkv_all = jnp.dot(entered, qkv_full, preferred_element_type=jnp.float32).astype(jnp.bfloat16)
    queries = qkv_all[:, :model_width]
    keys_local = qkv_all[:, model_width : 2 * model_width]
    values_local = qkv_all[:, 2 * model_width :]
    query_heads = queries.reshape(local_rows, HEADS, HEAD)
    start_state = (
        jnp.full((local_rows, HEADS), masked_score, jnp.float32),
        jnp.zeros((local_rows, HEADS), jnp.float32),
        jnp.zeros((local_rows, HEADS, HEAD), jnp.float32),
    )
    carried = start_state
    key_piece = lax.all_gather(keys_local, "shard", axis=0, tiled=True)
    value_piece = lax.all_gather(values_local, "shard", axis=0, tiled=True)
    piece_rows = key_piece.shape[0]
    block_rows = block_size()
    count_blocks = piece_rows // block_rows
    key_blocks = key_piece.reshape(count_blocks, block_rows, HEADS, HEAD)
    value_blocks = value_piece.reshape(count_blocks, block_rows, HEADS, HEAD)

    def attend_block(running, blocks):
        key_block, value_block, block_index = blocks
        run_max, run_sum, run_acc = running
        visible = visible_mask(
            allowed, seg_len, my_start, local_rows, block_index * block_rows, block_rows
        )
        scores = (
            jnp.einsum("qhd,khd->qhk", query_heads, key_block, preferred_element_type=jnp.float32)
            * 0.125
        )
        scores = jnp.where(visible[:, None, :], scores, masked_score)
        new_max = jnp.maximum(run_max, jnp.max(scores, axis=2))
        rescale = jnp.exp(run_max - new_max)
        exp_scores = jnp.exp(scores - new_max[:, :, None])
        run_sum = run_sum * rescale + jnp.sum(exp_scores, axis=2)
        run_acc = run_acc * rescale[:, :, None] + jnp.einsum(
            "qhk,khd->qhd",
            exp_scores.astype(jnp.bfloat16),
            value_block,
            preferred_element_type=jnp.float32,
        )
        return ((new_max, run_sum, run_acc), None)

    carried, unused = lax.scan(
        attend_block, carried, (key_blocks, value_blocks, jnp.arange(count_blocks, dtype=jnp.int32))
    )
    run_max, run_sum, run_acc = carried
    attn_exact = run_acc / run_sum[:, :, None]
    log_sum = run_max + jnp.log(run_sum)
    attended = attn_exact.reshape(local_rows, model_width).astype(jnp.bfloat16)
    hidden = inputs + jnp.dot(attended, out_full, preferred_element_type=jnp.float32)
    up_full, down_full, ffn_gain = (
        lax.all_gather(up_weight.astype(jnp.bfloat16), "shard", axis=0, tiled=True),
        lax.all_gather(down_weight.astype(jnp.bfloat16), "shard", axis=0, tiled=True),
        lax.all_gather(gain_ffn.astype(jnp.bfloat16), "shard", axis=0, tiled=True),
    )
    normed_two, inv_two = normalize(hidden)
    second = (normed_two * ffn_gain.astype(jnp.float32)).astype(jnp.bfloat16)
    pre_act = jnp.dot(second, up_full, preferred_element_type=jnp.float32)
    active = gelu_exact(pre_act).astype(jnp.bfloat16)
    output = (hidden + jnp.dot(active, down_full, preferred_element_type=jnp.float32)).astype(
        jnp.bfloat16
    )
    up_full, down_full, ffn_gain = (
        lax.all_gather(up_weight.astype(jnp.bfloat16), "shard", axis=0, tiled=True),
        lax.all_gather(down_weight.astype(jnp.bfloat16), "shard", axis=0, tiled=True),
        lax.all_gather(gain_ffn.astype(jnp.bfloat16), "shard", axis=0, tiled=True),
    )
    qkv_full, out_full, attn_gain = (
        lax.all_gather(qkv_weight.astype(jnp.bfloat16), "shard", axis=0, tiled=True),
        lax.all_gather(out_weight.astype(jnp.bfloat16), "shard", axis=0, tiled=True),
        lax.all_gather(gain_attn.astype(jnp.bfloat16), "shard", axis=0, tiled=True),
    )
    grad_down = t_times(active, cotangent)
    grad_active = times_t(cotangent, down_full).astype(jnp.bfloat16)
    grad_pre = (grad_active.astype(jnp.float32) * gelu_slope(pre_act)).astype(jnp.bfloat16)
    grad_up = t_times(second, grad_pre)
    grad_second = times_t(grad_pre, up_full)
    grad_gain_ffn = jnp.sum(grad_second * normed_two, axis=0)
    grad_hidden = cotangent.astype(jnp.float32) + norm_back(
        grad_second * ffn_gain.astype(jnp.float32), normed_two, inv_two
    )
    grad_y = grad_hidden.astype(jnp.bfloat16)
    grad_out = t_times(attended, grad_y)
    grad_attn = times_t(grad_y, out_full).astype(jnp.bfloat16)
    grad_heads = grad_attn.reshape(local_rows, HEADS, HEAD)
    row_delta = jnp.sum(grad_heads.astype(jnp.float32) * attn_exact, axis=2)
    start_back = jnp.zeros((local_rows, HEADS, HEAD), jnp.float32)
    carried = start_back
    key_piece = lax.all_gather(keys_local, "shard", axis=0, tiled=True)
    value_piece = lax.all_gather(values_local, "shard", axis=0, tiled=True)
    piece_rows = key_piece.shape[0]
    back_block_rows = block_size()
    count_blocks = piece_rows // back_block_rows
    key_blocks = key_piece.reshape(count_blocks, back_block_rows, HEADS, HEAD)
    value_blocks = value_piece.reshape(count_blocks, back_block_rows, HEADS, HEAD)

    def back_block(running, blocks):
        grad_query = running
        key_block, value_block, block_index = blocks
        block_start = block_index * back_block_rows
        visible = visible_mask(allowed, seg_len, my_start, local_rows, block_start, back_block_rows)
        part_query, part_key, part_value = pair_terms(
            query_heads, grad_heads, log_sum, row_delta, key_block, value_block, visible
        )
        joined = jnp.concatenate(
            (
                part_key.reshape(back_block_rows, model_width),
                part_value.reshape(back_block_rows, model_width),
            ),
            axis=1,
        )
        return (grad_query + part_query, joined.astype(jnp.bfloat16))

    carried, key_terms = lax.scan(
        back_block, carried, (key_blocks, value_blocks, jnp.arange(count_blocks, dtype=jnp.int32))
    )
    grad_query = carried
    key_terms = key_terms.reshape(piece_rows, 2 * model_width)
    key_grads = lax.psum_scatter(key_terms, "shard", scatter_dimension=0, tiled=True)
    grad_qkv = jnp.concatenate(
        (grad_query.reshape(local_rows, model_width), key_grads), axis=1
    ).astype(jnp.bfloat16)
    grad_qkv_weight = t_times(entered, grad_qkv)
    grad_entered = times_t(grad_qkv, qkv_full)
    grad_gain_attn = jnp.sum(grad_entered * normed_one, axis=0)
    input_grad = grad_hidden + norm_back(
        grad_entered * attn_gain.astype(jnp.float32), normed_one, inv_one
    )
    group_sums = (
        lax.psum_scatter(grad_qkv_weight.astype(jnp.bfloat16), "shard", scatter_dimension=0, tiled=True),
        lax.psum_scatter(grad_out.astype(jnp.bfloat16), "shard", scatter_dimension=0, tiled=True),
        lax.psum_scatter(grad_up.astype(jnp.bfloat16), "shard", scatter_dimension=0, tiled=True),
        lax.psum_scatter(grad_down.astype(jnp.bfloat16), "shard", scatter_dimension=0, tiled=True),
        lax.psum_scatter(grad_gain_attn, "shard", scatter_dimension=0, tiled=True),
        lax.psum_scatter(grad_gain_ffn, "shard", scatter_dimension=0, tiled=True),
    )
    totals = (
        lax.psum(group_sums[0].astype(jnp.bfloat16), "rep").astype(jnp.float32),
        lax.psum(group_sums[1].astype(jnp.bfloat16), "rep").astype(jnp.float32),
        lax.psum(group_sums[2].astype(jnp.bfloat16), "rep").astype(jnp.float32),
        lax.psum(group_sums[3].astype(jnp.bfloat16), "rep").astype(jnp.float32),
        lax.psum(group_sums[4].astype(jnp.bfloat16), "rep").astype(jnp.float32),
        lax.psum(group_sums[5].astype(jnp.bfloat16), "rep").astype(jnp.float32),
    )
    return (output, input_grad, totals[0], totals[1], totals[2], totals[3], totals[4], totals[5])


MESH = pl.DeviceIdType.MESH


def ring_place(shard):
    return (1 - shard % 2) * (shard // 2) + (shard % 2) * (7 - shard // 2)


def ring_shard(place):
    upper = place // 4
    return (1 - upper) * 2 * place + upper * (15 - 2 * place)


def remote(source, target, sent, got, device):
    return pltpu.make_async_remote_copy(
        src_ref=source,
        dst_ref=target,
        send_sem=sent,
        recv_sem=got,
        device_id=device,
        device_id_type=MESH,
    )


def around(place, offset):
    return ring_shard(lax.rem(place + offset + 8, 8))


class Where:
    def __init__(self):
        self.rep = lax.axis_index("rep")
        self.me = lax.axis_index("shard")
        self.y = self.rep // 2
        self.core = self.rep % 2
        self.rep_y = (1 - self.y) * 2 + self.core
        self.rep_core = self.y * 2 + 1 - self.core
        self.rep_far = (1 - self.y) * 2 + 1 - self.core
        self.place = ring_place(self.me)
        self.right = around(self.place, 1)
        self.left = around(self.place, -1)

    def other(self, step):
        return lax.rem(self.me + step, 8)

    def back(self, step):
        return lax.rem(self.me + 8 - step, 8)

    def greet(self):
        barrier = pltpu.get_barrier_semaphore()
        for step in range(1, 8):
            pl.semaphore_signal(
                barrier, inc=1, device_id=(self.rep, self.other(step)), device_id_type=MESH
            )
        for rep in (self.rep_y, self.rep_core, self.rep_far):
            pl.semaphore_signal(barrier, inc=1, device_id=(rep, self.me), device_id_type=MESH)
        pl.semaphore_wait(barrier, 10)


RING_UNITS = [(flow, step, piece) for step in range(3) for flow in range(2) for piece in range(3)]
RING_UNITS = RING_UNITS + [(0, 3, 1), (1, 3, 2), (1, 3, 0)]


def normed_rows(values):
    average = jnp.mean(values, axis=-1, keepdims=True)
    centered = values - average
    variance = jnp.mean(centered * centered, axis=-1, keepdims=True)
    inv_std = lax.rsqrt(variance + 1e-05)
    return (centered * inv_std, inv_std)


def gain_row(gains_ref, which):
    return jnp.concatenate(
        [gains_ref[s, which * 8 : which * 8 + 1, :] for s in range(8)], axis=1
    ).astype(jnp.float32)


def head_lanes(values, head):
    lane = lax.broadcasted_iota(jnp.int32, values.shape, 1)
    return jnp.where(lane // HEAD == head, values, jnp.zeros_like(values))


KEY_ROWS = [256, 512, 768, 1024, 1280, 1536, 1536, 1536]


def tile_masks(block, parents_ref):
    key_row = lax.broadcasted_iota(jnp.int32, (256, 256), 0)
    query_row = lax.broadcasted_iota(jnp.int32, (256, 256), 1)
    own = key_row <= query_row
    if block < 5:
        return (own, None)
    own = own & (key_row // 128 == query_row // 128)
    if block == 5:
        return (own, None)
    parent = jnp.where(query_row < 128, parents_ref[2 * block], parents_ref[2 * block + 1])
    return (own, parent == 10 + key_row // 128)


def score_parts(block, keys_ref, queries, masks):
    own_mask, branch_mask = masks
    full = 256 * block if block < 5 else 1280
    spans = [(0, full, None)] if full else []
    if branch_mask is not None:
        spans.append((1280, 256, branch_mask))
    spans.append((256 * block, 256, own_mask))
    parts = []
    for first, rows, mask in spans:
        scores = times_t(keys_ref[pl.ds(first, rows), :], queries)
        if mask is not None:
            scores = jnp.where(mask, scores, masked_score)
        parts.append((first, rows, scores))
    return parts


def forward_kernel(
    place_ref, ids_ref, parents_ref, tok_ref, wq_ref, gain_ref, out_ref, up_ref, down_ref,
    att_ref, ent_ref, qkv_ref, mixed_ref, log_ref, gains_ref, slice_ref, out_all, up_all, down_all,
    tok_all, qkv_slots, value_t, tree_rows, slot_rows,
    small_s, small_r, tok_s, tok_r, ring_s, ring_r, y_s, y_r, core_s, core_r, mix_s, mix_r, local_s,
):
    at = Where()
    rep, me = at.rep, at.me
    at.greet()
    ring_device = ((rep, at.right), (rep, at.left))

    small = []
    for step in range(1, 8):
        to = at.other(step)
        small.append(
            remote(
                gain_ref, gains_ref.at[me], small_s.at[0, step], small_r.at[0, step], (rep, to)
            )
        )
        small.append(
            remote(
                wq_ref.at[to],
                slice_ref.at[me],
                small_s.at[1, step],
                small_r.at[1, step],
                (rep, to),
            )
        )

    def token_copy(flow, step, half):
        origin = around(at.place, step if flow else -step)
        source = tok_ref if step == 0 else tok_all.at[origin]
        rows = pl.ds(half * 128, 128)
        return remote(
            source.at[rows, :],
            tok_all.at[origin, rows, :],
            tok_s.at[flow, step, half],
            tok_r.at[flow, step, half],
            ring_device[flow],
        )

    def piece_rows(piece, origin, quarter):
        whole = (out_all, up_all, down_all)[piece]
        if piece < 2:
            return whole.at[pl.ds(origin * 128 + quarter * 32, 32), :]
        return whole.at[pl.ds(origin * 512 + quarter * 128, 128), :]

    def ring_copy(unit):
        flow, step, piece = unit
        origin = around(at.place, step if flow else -step)
        index = RING_UNITS.index(unit)
        target = piece_rows(piece, origin, rep)
        if step == 0:
            source = (out_ref, up_ref, down_ref)[piece]
            rows = 32 if piece < 2 else 128
            source = source.at[pl.ds(rep * rows, rows), :]
        else:
            source = target
        return remote(source, target, ring_s.at[index], ring_r.at[index], ring_device[flow])

    def unit_origin(unit):
        flow, step, _ = unit
        return around(at.place, (step + 1) if flow else -(step + 1))

    def share_y(unit):
        index = RING_UNITS.index(unit)
        block = piece_rows(unit[2], unit_origin(unit), rep)
        return remote(block, block, y_s.at[index], y_r.at[index], (at.rep_y, me))

    def share_core(unit, own):
        index = RING_UNITS.index(unit)
        block = piece_rows(unit[2], unit_origin(unit), rep if own else at.rep_y)
        return remote(
            block, block, core_s.at[own, index], core_r.at[own, index], (at.rep_core, me)
        )

    for copy in small:
        copy.start()
    for half in range(2):
        for flow in range(2):
            token_copy(flow, 0, half).start()
    for unit in RING_UNITS:
        if unit[1] == 0:
            ring_copy(unit).start()
    kept = [
        pltpu.make_async_copy(out_ref, out_all.at[pl.ds(me * 128, 128), :], local_s.at[0]),
        pltpu.make_async_copy(up_ref, up_all.at[pl.ds(me * 128, 128), :], local_s.at[1]),
        pltpu.make_async_copy(down_ref, down_all.at[pl.ds(me * 512, 512), :], local_s.at[2]),
    ]
    for copy in kept:
        copy.start()
    gains_ref[me] = gain_ref[...]
    slice_ref[me] = wq_ref[me]
    for copy in small:
        copy.wait_recv()
    gain = gain_row(gains_ref, 0)

    def enter(rows, origin):
        normed, _ = normed_rows(rows.astype(jnp.float32))
        entered = (normed * gain).astype(jnp.bfloat16)
        ent_ref[origin] = entered
        weights = slice_ref[...].reshape(1024, 384)
        made = jnp.dot(entered, weights, preferred_element_type=jnp.float32).astype(jnp.bfloat16)
        qkv_slots[2 * origin] = made[:128]
        qkv_slots[2 * origin + 1] = made[128:]

    enter(tok_ref[...], me)

    for step in range(4):
        halves = [(half, flow) for half in range(2) for flow in range(2)]
        if step == 3:
            halves = [(0, 0), (1, 1)]
        for half, flow in halves:
            token_copy(flow, step, half).wait_recv()
            if step < 2 or (step == 2 and half == flow):
                token_copy(flow, step + 1, half).start()
        for unit in RING_UNITS:
            if unit[1] == step:
                ring_copy(unit).wait_recv()
                after = (unit[0], step + 1, unit[2])
                if after in RING_UNITS:
                    ring_copy(after).start()
                share_y(unit).start()
                share_core(unit, 1).start()
        for flow in range(2 if step < 3 else 1):
            origin = around(at.place, (step + 1) if flow else -(step + 1))
            enter(tok_all[origin], origin)

    for seg in range(16):
        rows = qkv_slots[place_ref[seg]]
        qkv_ref[seg * 128 : seg * 128 + 128, :] = rows
    for block in range(8):
        rows = pl.ds(block * 256, 256)
        value_t[:, block * 256 : block * 256 + 256] = qkv_ref[rows, 256:384].T

    for block in range(8):
        masks = tile_masks(block, parents_ref)
        rows = pl.ds(block * 256, 256)

        def one_head(head, unused):
            queries = head_lanes(qkv_ref[rows, 0:128], head) * jnp.bfloat16(0.125)
            parts = score_parts(block, qkv_ref.at[:, pl.ds(128, 128)], queries, masks)
            top = None
            for _, _, scores in parts:
                part = jnp.max(scores, axis=0, keepdims=True)
                top = part if top is None else jnp.maximum(top, part)
            total = None
            mixed = None
            head_rows = pl.ds(pl.multiple_of(head * HEAD, HEAD), HEAD)
            for first, count, scores in parts:
                weights = jnp.exp(scores - top)
                part = jnp.sum(weights, axis=0, keepdims=True)
                total = part if total is None else total + part
                term = jnp.dot(
                    value_t[head_rows, pl.ds(first, count)],
                    weights.astype(jnp.bfloat16),
                    preferred_element_type=jnp.float32,
                )
                mixed = term if mixed is None else mixed + term
            mixed_ref[head_rows, block * 256 : block * 256 + 256] = mixed / total
            log_ref[pl.ds(pl.multiple_of(head * 8, 8), 8), block * 256 : block * 256 + 256] = (
                jnp.broadcast_to(top + jnp.log(total), (8, 256))
            )
            return unused

        lax.fori_loop(0, 2, one_head, 0)
        tree = mixed_ref[:, block * 256 : block * 256 + 256].T.astype(jnp.bfloat16)
        tree_rows[2 * block] = tree[:128]
        tree_rows[2 * block + 1] = tree[128:]

    for slot in range(16):
        slot_rows[slot // 2, (slot % 2) * 128 : (slot % 2) * 128 + 128, :] = tree_rows[
            ids_ref[slot]
        ]

    columns = pl.ds(pl.multiple_of(me * 128, 128), 128)
    mix = []
    for step in range(1, 8):
        to = at.other(step)
        mix.append(
            remote(
                slot_rows.at[to],
                att_ref.at[:, columns],
                mix_s.at[step],
                mix_r.at[step],
                (rep, to),
            )
        )
    for copy in mix:
        copy.start()
    att_ref[:, columns] = slot_rows[me]

    for unit in RING_UNITS:
        share_y(unit).wait_recv()
        share_core(unit, 0).start()
    for copy in mix:
        copy.wait()
    for copy in kept:
        copy.wait()
    for unit in RING_UNITS:
        share_core(unit, 1).wait()
        share_core(unit, 0).wait()
        share_y(unit).wait_send()
        ring_copy(unit).wait_send()
    for copy in small:
        copy.wait_send()
    for step in range(4):
        for half in range(2):
            for flow in range(2):
                if step < 3 or half == flow:
                    token_copy(flow, step, half).wait_send()


def forward_part(places, slot_ids, parents, tokens, wq, gains, out_b, up_b, down_b):
    smem = pl.BlockSpec(memory_space=pltpu.SMEM)
    vmem = pl.BlockSpec(memory_space=pltpu.VMEM)
    anywhere = pl.BlockSpec(memory_space=pl.ANY)
    units = len(RING_UNITS)
    dma = pltpu.SemaphoreType.DMA
    return pl.pallas_call(
        forward_kernel,
        out_shape=[
            jax.ShapeDtypeStruct((256, 1024), jnp.bfloat16),
            jax.ShapeDtypeStruct((8, 256, 1024), jnp.bfloat16),
            jax.ShapeDtypeStruct((2048, 384), jnp.bfloat16),
            jax.ShapeDtypeStruct((128, 2048), jnp.float32),
            jax.ShapeDtypeStruct((16, 2048), jnp.float32),
            jax.ShapeDtypeStruct((8, 16, 128), jnp.bfloat16),
            jax.ShapeDtypeStruct((8, 128, 384), jnp.bfloat16),
            jax.ShapeDtypeStruct((1024, 1024), jnp.bfloat16),
            jax.ShapeDtypeStruct((1024, 4096), jnp.bfloat16),
            jax.ShapeDtypeStruct((4096, 1024), jnp.bfloat16),
        ],
        in_specs=[smem] * 3 + [vmem] * 3 + [anywhere] * 3,
        out_specs=[vmem] * 7 + [anywhere] * 3,
        scratch_shapes=[
            pltpu.VMEM((8, 256, 1024), jnp.bfloat16),
            pltpu.VMEM((16, 128, 384), jnp.bfloat16),
            pltpu.VMEM((128, 2048), jnp.bfloat16),
            pltpu.VMEM((16, 128, 128), jnp.bfloat16),
            pltpu.VMEM((8, 256, 128), jnp.bfloat16),
            dma((2, 8)), dma((2, 8)), dma((2, 4, 2)), dma((2, 4, 2)),
            dma((units,)), dma((units,)), dma((units,)), dma((units,)),
            dma((2, units)), dma((2, units)), dma((8,)), dma((8,)), dma((3,)),
        ],
        compiler_params=pltpu.CompilerParams(
            collective_id=1, has_side_effects=True, vmem_limit_bytes=56 * 2**20
        ),
    )(places, slot_ids, parents, tokens, wq, gains, out_b, up_b, down_b)


BLOCK_ORDER = [4, 3, -3, 2, -2, 1, -1, 0]


def summed(*parts):
    total = parts[0].astype(jnp.float32)
    for part in parts[1:]:
        total = total + part.astype(jnp.float32)
    return total


def backward_kernel(
    place_ref, ids_ref, parents_ref, tok_ref, gh_ref, ga_ref, ent_ref, qkv_ref, mixed_ref, log_ref,
    gains_ref, slice_ref, gfg_ref, out_ref, up_ref, down_ref,
    in_ref, qkv_out, out_out, up_out, down_out, gain_out,
    own_out, own_up, own_down, cr_out, cr_up, cr_down, yr_out, yr_up, yr_down, rr_out, rr_up, rr_down,
    do_slots, do_tree, key_t, dq_t, dk, dv, gq_tree, gq_slots, gq_t, ge_recv,
    qs_send, qs_recv, qs_core, qs_half, qs_y, gp, gp_recv, gp_rep,
    do_s, do_r, load_s, core_s, core_r, y_s, y_r, ring_s, ring_r, fin_s, fin_r, ge_s, ge_r,
    qs_s, qs_r, qr_s, qr_r, gp_s, gp_r, gr_s, gr_r,
):
    at = Where()
    rep, me, y, core = at.rep, at.me, at.y, at.core
    at.greet()
    ring_device = ((rep, at.right), (rep, at.left))
    whole = (out_ref, up_ref, down_ref)
    own = (own_out, own_up, own_down)
    from_core = (cr_out, cr_up, cr_down)
    from_y = (yr_out, yr_up, yr_down)
    from_ring = (rr_out, rr_up, rr_down)
    result = (out_out, up_out, down_out)
    order = [around(at.place, offset) for offset in BLOCK_ORDER]

    grads = []
    for step in range(1, 8):
        to = at.other(step)
        grads.append(
            remote(
                ga_ref.at[:, pl.ds(pl.multiple_of(to * 128, 128), 128)],
                do_slots.at[me],
                do_s.at[step],
                do_r.at[step],
                (rep, to),
            )
        )
    for copy in grads:
        copy.start()
    loads = [
        pltpu.make_async_copy(whole[i].at[:, :, core], own[i], load_s.at[i]) for i in range(3)
    ]
    for copy in loads:
        copy.start()

    def core_copy(index, piece):
        block = order[index]
        return remote(
            whole[piece].at[block, :, 1 - core],
            from_core[piece].at[block],
            core_s.at[index, piece],
            core_r.at[index, piece],
            (at.rep_core, me),
        )

    def y_copy(index, piece):
        block = order[index]
        return remote(
            own[piece].at[block, 1 - y],
            from_y[piece].at[block],
            y_s.at[index, piece],
            y_r.at[index, piece],
            (at.rep_y, me),
        )

    for index in range(8):
        for piece in range(3):
            core_copy(index, piece).start()
    do_slots[me] = ga_ref[:, pl.ds(pl.multiple_of(me * 128, 128), 128)]
    for copy in loads:
        copy.wait()
    for index in range(8):
        block = order[index]
        for piece in range(3):
            core_copy(index, piece).wait_recv()
            own[piece][block, 1 - y] = summed(
                own[piece][block, 1 - y], from_core[piece][block, 1 - y]
            ).astype(jnp.bfloat16)
            y_copy(index, piece).start()
            own[piece][block, y] = summed(
                own[piece][block, y], from_core[piece][block, y]
            ).astype(jnp.bfloat16)

    def ring_pieces(flow, step):
        return ((1,), (2, 0))[flow] if step == 0 else (0, 1, 2)

    def ring_copy(flow, step, piece):
        block = around(at.place, (-1 if flow else 1) * (4 - step))
        return remote(
            own[piece].at[block, y],
            from_ring[piece].at[flow, step],
            ring_s.at[flow, step, piece],
            ring_r.at[flow, step, piece],
            ring_device[flow],
        )

    def ring_step(step):
        for flow in range(2):
            block = around(at.place, (-1 if flow else 1) * (4 - step))
            offset = (-1 if flow else 1) * (4 - step)
            index = BLOCK_ORDER.index(4 if step == 0 else offset)
            for piece in ring_pieces(flow, step):
                y_copy(index, piece).wait_recv()
                terms = [own[piece][block, y], from_y[piece][block]]
                if step > 0 and piece in ring_pieces(flow, step - 1):
                    ring_copy(flow, step - 1, piece).wait_recv()
                    terms.append(from_ring[piece][flow, step - 1])
                own[piece][block, y] = summed(*terms).astype(jnp.bfloat16)
                ring_copy(flow, step, piece).start()

    for copy in grads:
        copy.wait_recv()
    for seg in range(16):
        slot = place_ref[seg]
        do_tree[seg * 128 : seg * 128 + 128, :] = do_slots.reshape(16, 128, 128)[slot]
    for block in range(8):
        rows = pl.ds(block * 256, 256)
        key_t[:, block * 256 : block * 256 + 256] = qkv_ref[rows, 128:256].T
    dk[...] = jnp.zeros_like(dk)
    dv[...] = jnp.zeros_like(dv)

    for block in range(8):
        masks = tile_masks(block, parents_ref)
        rows = pl.ds(block * 256, 256)
        across = pl.ds(block * 256, 256)

        def one_head(head, unused):
            head_rows = pl.ds(pl.multiple_of(head * HEAD, HEAD), HEAD)
            queries = head_lanes(qkv_ref[rows, 0:128], head) * jnp.bfloat16(0.125)
            grad_rows = head_lanes(do_tree[rows, :], head)
            lse = log_ref[pl.ds(pl.multiple_of(head * 8, 8), 8), across][0:1]
            grad_t = do_tree[rows, :].T.astype(jnp.float32)
            both = grad_t * mixed_ref[:, across]
            delta0 = jnp.sum(both[:HEAD], axis=0, keepdims=True)
            delta1 = jnp.sum(both[HEAD:], axis=0, keepdims=True)
            delta = jnp.where(head == 0, delta0, delta1)
            grad_query = None
            for first, count, scores in score_parts(
                block, qkv_ref.at[:, pl.ds(128, 128)], queries, masks
            ):
                keys = pl.ds(first, count)
                weights = jnp.exp(scores - lse)
                grad_weights = times_t(qkv_ref[keys, 256:384], grad_rows)
                grad_scores = (weights * (grad_weights - delta)).astype(jnp.bfloat16)
                dk[keys, :] += jnp.dot(grad_scores, queries, preferred_element_type=jnp.float32)
                dv[keys, :] += jnp.dot(
                    weights.astype(jnp.bfloat16), grad_rows, preferred_element_type=jnp.float32
                )
                term = jnp.dot(
                    key_t[head_rows, keys], grad_scores, preferred_element_type=jnp.float32
                )
                grad_query = term if grad_query is None else grad_query + term
            dq_t[head_rows, across] = grad_query * 0.125
            return unused

        lax.fori_loop(0, 2, one_head, 0)
        if block == 4:
            ring_step(0)

    for seg in range(16):
        rows = pl.ds(seg * 128, 128)
        gq_tree[seg, :, 0:128] = dq_t[:, seg * 128 : seg * 128 + 128].T.astype(jnp.bfloat16)
        gq_tree[seg, :, 128:256] = dk[rows, :].astype(jnp.bfloat16)
        gq_tree[seg, :, 256:384] = dv[rows, :].astype(jnp.bfloat16)
    for slot in range(16):
        gq_slots[slot // 2, (slot % 2) * 128 : (slot % 2) * 128 + 128, :] = gq_tree[ids_ref[slot]]

    def ge_copy(flow, step):
        source, target = cr_down.at[flow * 4 + step], ge_recv.at[flow, step]
        if step == 0:
            source, target = source.at[flow], target.at[flow]
        return remote(
            source, target, ge_s.at[flow, step], ge_r.at[flow, step], ring_device[flow]
        )

    def ge_part(block):
        weights = slice_ref[...].reshape(1024, 384)
        return times_t(gq_slots[block], weights)

    def ge_step(step):
        for flow in range(2):
            block = around(at.place, (-1 if flow else 1) * (4 - step))
            part = ge_part(block)
            if step > 0:
                ge_copy(flow, step - 1).wait_recv()
            for half in range(2):
                if step == 0 and half != flow:
                    continue
                rows = part[half * 128 : half * 128 + 128]
                if step > 1 or (step == 1 and half == flow):
                    rows = rows + ge_recv[flow, step - 1, half].astype(jnp.float32)
                cr_down[flow * 4 + step, half] = rows.astype(jnp.bfloat16)
            ge_copy(flow, step).start()

    ge_step(0)
    for block in range(8):
        gq_t[:, block * 256 : block * 256 + 256] = gq_slots[block].T

    slices = []
    for step in range(1, 8):
        to = at.other(step)
        slices.append(
            remote(qs_send.at[to], qs_recv.at[me], qs_s.at[step], qs_r.at[step], (rep, to))
        )
    for step in range(8):
        to = at.other(step)
        entered = ent_ref[:, :, pl.ds(pl.multiple_of(to * 128, 128), 128)].reshape(2048, 128)
        made = jnp.dot(gq_t[...], entered, preferred_element_type=jnp.float32)
        made = made.T.astype(jnp.bfloat16).reshape(2, 2, 32, 384)
        if step == 0:
            qs_recv[me] = made
        else:
            qs_send[to] = made
            slices[step - 1].start()
    ge_step(1)
    ring_step(1)
    for copy in slices:
        copy.wait_recv()
    qs_over_core = remote(
        qs_recv.at[:, :, 1 - core], qs_core, qr_s.at[0], qr_r.at[0], (at.rep_core, me)
    )
    qs_over_core.start()
    ge_step(2)
    qs_over_core.wait_recv()
    qs_half[...] = summed(qs_recv[:, :, core], qs_core[...]).astype(jnp.bfloat16)
    qs_over_y = remote(qs_half.at[:, 1 - y], qs_y, qr_s.at[1], qr_r.at[1], (at.rep_y, me))
    qs_over_y.start()
    ring_step(2)
    qs_over_y.wait_recv()
    qkv_out[:, rep] = summed(qs_half[:, y], qs_y[...]).astype(jnp.bfloat16)
    back_y = remote(
        qkv_out.at[:, rep], qkv_out.at[:, rep], qr_s.at[2], qr_r.at[2], (at.rep_y, me)
    )
    back_core = remote(
        qkv_out.at[:, rep], qkv_out.at[:, rep], qr_s.at[3], qr_r.at[3], (at.rep_core, me)
    )
    back_y.start()
    back_core.start()
    ge_step(3)
    ring_step(3)
    back_y.wait_recv()
    back_far = remote(
        qkv_out.at[:, at.rep_y], qkv_out.at[:, at.rep_y], qr_s.at[4], qr_r.at[4], (at.rep_core, me)
    )
    back_far.start()

    for flow in range(2):
        ge_copy(flow, 3).wait_recv()
    grad_entered = ge_part(me)
    for flow in range(2):
        grad_entered = grad_entered + ge_recv[flow, 3].reshape(256, 1024).astype(jnp.float32)
    normed, inv_std = normed_rows(tok_ref[...].astype(jnp.float32))
    gain_sum = jnp.sum(grad_entered * normed, axis=0, keepdims=True)
    in_ref[...] = gh_ref[...] + norm_back(grad_entered * gain_row(gains_ref, 0), normed, inv_std)
    for s in range(8):
        gp[s, 0:8, :] = jnp.broadcast_to(gain_sum[:, s * 128 : s * 128 + 128], (8, 128))
        gp[s, 8:16, :] = jnp.broadcast_to(gfg_ref[:, s * 128 : s * 128 + 128], (8, 128))
    gain_sends = []
    for step in range(1, 8):
        to = at.other(step)
        gain_sends.append(
            remote(gp.at[to], gp_recv.at[me], gp_s.at[step], gp_r.at[step], (rep, to))
        )
    for copy in gain_sends:
        copy.start()
    gp_recv[me] = gp[me]

    def final_copy(piece, leg):
        quarter = at.rep_y if leg == 2 else rep
        rows = 32 if piece < 2 else 128
        spot = result[piece].at[pl.ds(quarter * rows, rows), :]
        device = (at.rep_y if leg == 0 else at.rep_core, me)
        return remote(spot, spot, fin_s.at[piece, leg], fin_r.at[piece, leg], device)

    for piece in range(3):
        y_copy(7, piece).wait_recv()
        terms = [own[piece][me, y], from_y[piece][me]]
        for flow in range(2):
            ring_copy(flow, 3, piece).wait_recv()
            terms.append(from_ring[piece][flow, 3])
        rows = 32 if piece < 2 else 128
        result[piece][pl.ds(rep * rows, rows), :] = summed(*terms).astype(jnp.bfloat16)
        final_copy(piece, 0).start()
        final_copy(piece, 1).start()
    for copy in gain_sends:
        copy.wait_recv()
    total = gp_recv[0]
    for s in range(1, 8):
        total = total + gp_recv[s]
    gp_rep[rep] = total
    rep_sends = [
        remote(gp_rep.at[rep], gp_rep.at[rep], gr_s.at[i], gr_r.at[i], (to, me))
        for i, to in enumerate((at.rep_y, at.rep_core, at.rep_far))
    ]
    for copy in rep_sends:
        copy.start()
    for piece in range(3):
        final_copy(piece, 0).wait_recv()
        final_copy(piece, 2).start()
    for copy in rep_sends:
        copy.wait()
    gain_out[...] = gp_rep[0] + gp_rep[1] + gp_rep[2] + gp_rep[3]
    for piece in range(3):
        final_copy(piece, 1).wait()
        final_copy(piece, 2).wait()
        final_copy(piece, 0).wait_send()
    back_core.wait()
    back_far.wait()
    back_y.wait_send()
    qs_over_y.wait_send()
    qs_over_core.wait_send()
    for copy in slices + gain_sends + grads:
        copy.wait_send()
    for index in range(8):
        for piece in range(3):
            core_copy(index, piece).wait_send()
            y_copy(index, piece).wait_send()
    for step in range(4):
        for flow in range(2):
            ge_copy(flow, step).wait_send()
            for piece in ring_pieces(flow, step):
                ring_copy(flow, step, piece).wait_send()


def backward_part(
    places, slot_ids, parents, tokens, grad_hidden, grad_attn, entered, qkv, mixed, logs, gains,
    slices, grad_gain_ffn, grad_out, grad_up, grad_down,
):
    smem = pl.BlockSpec(memory_space=pltpu.SMEM)
    vmem = pl.BlockSpec(memory_space=pltpu.VMEM)
    anywhere = pl.BlockSpec(memory_space=pl.ANY)
    dma = pltpu.SemaphoreType.DMA
    low, full = jnp.bfloat16, jnp.float32

    def pieces(*lead):
        return [
            pltpu.VMEM(lead + (32, 1024), low),
            pltpu.VMEM(lead + (32, 4096), low),
            pltpu.VMEM(lead + (128, 1024), low),
        ]

    in_grad, qkv_part, out_part, up_part, down_part, gain_part = pl.pallas_call(
        backward_kernel,
        out_shape=[
            jax.ShapeDtypeStruct((256, 1024), full),
            jax.ShapeDtypeStruct((8, 4, 32, 384), low),
            jax.ShapeDtypeStruct((128, 1024), low),
            jax.ShapeDtypeStruct((128, 4096), low),
            jax.ShapeDtypeStruct((512, 1024), low),
            jax.ShapeDtypeStruct((16, 128), full),
        ],
        in_specs=[smem] * 3 + [vmem] * 10 + [anywhere] * 3,
        out_specs=[vmem] * 6,
        scratch_shapes=pieces(8, 2) + pieces(8, 2) + pieces(8) + pieces(2, 4) + [
            pltpu.VMEM((8, 256, 128), low),
            pltpu.VMEM((2048, 128), low),
            pltpu.VMEM((128, 2048), low),
            pltpu.VMEM((128, 2048), full),
            pltpu.VMEM((2048, 128), full),
            pltpu.VMEM((2048, 128), full),
            pltpu.VMEM((16, 128, 384), low),
            pltpu.VMEM((8, 256, 384), low),
            pltpu.VMEM((384, 2048), low),
            pltpu.VMEM((2, 4, 2, 128, 1024), low),
            pltpu.VMEM((8, 2, 2, 32, 384), low),
            pltpu.VMEM((8, 2, 2, 32, 384), low),
            pltpu.VMEM((8, 2, 32, 384), low),
            pltpu.VMEM((8, 2, 32, 384), low),
            pltpu.VMEM((8, 32, 384), low),
            pltpu.VMEM((8, 16, 128), full),
            pltpu.VMEM((8, 16, 128), full),
            pltpu.VMEM((4, 16, 128), full),
            dma((8,)), dma((8,)), dma((3,)), dma((8, 3)), dma((8, 3)), dma((8, 3)), dma((8, 3)),
            dma((2, 4, 3)), dma((2, 4, 3)), dma((3, 3)), dma((3, 3)), dma((2, 4)), dma((2, 4)),
            dma((8,)), dma((8,)), dma((5,)), dma((5,)), dma((8,)), dma((8,)), dma((3,)), dma((3,)),
        ],
        compiler_params=pltpu.CompilerParams(
            collective_id=2, has_side_effects=True, vmem_limit_bytes=62 * 2**20
        ),
    )(
        places, slot_ids, parents, tokens, grad_hidden, grad_attn, entered, qkv, mixed, logs, gains,
        slices, grad_gain_ffn.reshape(1, 1024), grad_out.reshape(8, 2, 2, 32, 1024),
        grad_up.reshape(8, 2, 2, 32, 4096), grad_down.reshape(8, 2, 2, 128, 1024),
    )
    qkv_part = qkv_part.reshape(8, 128, 3, 128).transpose(1, 2, 0, 3).reshape(128, 3072)
    return (in_grad, qkv_part, out_part, up_part, down_part, gain_part)


def fast_shards(
    tokens, cotangent, qkv_weight, out_weight, up_weight, down_weight, gain_attn, gain_ffn, parents, slot_ids
):
    seg_range = jnp.arange(16, dtype=jnp.int32)
    places = jnp.sum(
        jnp.where(slot_ids[None, :] == seg_range[:, None], seg_range[None, :], 0), axis=1
    )
    parents = parents.reshape(16)
    wq = qkv_weight.astype(jnp.bfloat16).reshape(128, 3, 8, 128).transpose(2, 0, 1, 3)
    wq = wq.reshape(8, 128, 384)
    out_b = out_weight.astype(jnp.bfloat16)
    up_b = up_weight.astype(jnp.bfloat16)
    down_b = down_weight.astype(jnp.bfloat16)
    gains = jnp.concatenate(
        [jnp.broadcast_to(g.astype(jnp.bfloat16)[None], (8, 128)) for g in (gain_attn, gain_ffn)]
    )
    attended, entered, qkv, mixed, logs, gains, slices, out_full, up_full, down_full = forward_part(
        places, slot_ids, parents, tokens, wq, gains, out_b, up_b, down_b
    )
    attn_gain = gains[:, 0, :].reshape(1, 1024).astype(jnp.float32)
    ffn_gain = gains[:, 8, :].reshape(1, 1024).astype(jnp.float32)
    hidden = tokens.astype(jnp.float32) + jnp.dot(
        attended, out_full, preferred_element_type=jnp.float32
    )
    normed_two, inv_two = normalize(hidden)
    second = (normed_two * ffn_gain).astype(jnp.bfloat16)
    pre_act = jnp.dot(second, up_full, preferred_element_type=jnp.float32)
    active = gelu_exact(pre_act).astype(jnp.bfloat16)
    output = (hidden + jnp.dot(active, down_full, preferred_element_type=jnp.float32)).astype(
        jnp.bfloat16
    )
    grad_down = t_times(active, cotangent).astype(jnp.bfloat16)
    grad_active = times_t(cotangent, down_full).astype(jnp.bfloat16)
    grad_pre = (grad_active.astype(jnp.float32) * gelu_slope(pre_act)).astype(jnp.bfloat16)
    grad_up = t_times(second, grad_pre).astype(jnp.bfloat16)
    grad_second = times_t(grad_pre, up_full)
    grad_gain_ffn = jnp.sum(grad_second * normed_two, axis=0)
    grad_hidden = cotangent.astype(jnp.float32) + norm_back(
        grad_second * ffn_gain, normed_two, inv_two
    )
    grad_y = grad_hidden.astype(jnp.bfloat16)
    grad_out = t_times(attended, grad_y).astype(jnp.bfloat16)
    grad_attn = times_t(grad_y, out_full).astype(jnp.bfloat16)
    input_grad, qkv_part, out_part, up_part, down_part, gain_part = backward_part(
        places, slot_ids, parents, tokens, grad_hidden, grad_attn, entered, qkv, mixed, logs, gains,
        slices, grad_gain_ffn, grad_out, grad_up, grad_down,
    )
    return (
        output,
        input_grad,
        qkv_part.astype(jnp.float32),
        out_part.astype(jnp.float32),
        up_part.astype(jnp.float32),
        down_part.astype(jnp.float32),
        gain_part[0],
        gain_part[8],
    )


def solution(mesh):
    in_specs = (
        P(("rep", "shard"), None),
        P(("rep", "shard"), None),
        P("shard", None),
        P("shard", None),
        P("shard", None),
        P("shard", None),
        P("shard"),
        P("shard"),
        P("rep", None),
        P("rep"),
    )
    out_specs = (
        P(("rep", "shard"), None),
        P(("rep", "shard"), None),
        P("shard", None),
        P("shard", None),
        P("shard", None),
        P("shard", None),
        P("shard"),
        P("shard"),
    )

    def fits(*args):
        shapes = [a.shape for a in args]
        return shapes[0] == (8192, 1024) and shapes[4] == (1024, 4096) and shapes[8] == (4, 16)

    small = mesh.shape["rep"] == 4 and mesh.shape["shard"] == 8

    def whole(*args):
        run = fast_shards if small and fits(*args) else shards
        return jax.shard_map(
            run, mesh=mesh, in_specs=in_specs, out_specs=out_specs, check_vma=False
        )(*args)

    return whole
```

```python
import jax
import jax.numpy as jnp
from jax import lax
from jax.experimental import pallas as pl
from jax.experimental.pallas import tpu as pltpu
from jax.sharding import PartitionSpec as P

HEADS = 16
HEAD = 64


masked_score = -1e30


def block_size():
    return 512


def normalize(values):
    average = jnp.mean(values, axis=-1, keepdims=True)
    centered = values - average
    variance = jnp.mean(centered * centered, axis=-1, keepdims=True)
    inv_std = lax.rsqrt(variance + 1e-05)
    return (centered * inv_std, inv_std)


def gelu_exact(values):
    return 0.5 * values * (1.0 + lax.erf(values * 0.7071067811865476))


def gelu_slope(values):
    return (
        0.5 * (1.0 + lax.erf(values * 0.7071067811865476))
        + values * jnp.exp(-0.5 * values * values) * 0.3989422804014327
    )


def norm_back(grad_normed, normed, inv_std):
    first_mean = jnp.mean(grad_normed, axis=-1, keepdims=True)
    second_mean = jnp.mean(grad_normed * normed, axis=-1, keepdims=True)
    return inv_std * (grad_normed - first_mean - normed * second_mean)


def times_t(left_side, right_side):
    return lax.dot_general(
        left_side, right_side, (((1,), (1,)), ((), ())), preferred_element_type=jnp.float32
    )


def t_times(left_side, right_side):
    return lax.dot_general(
        left_side, right_side, (((0,), (0,)), ((), ())), preferred_element_type=jnp.float32
    )


def exact_dot(left_side, right_side):
    return jnp.dot(
        left_side, right_side, precision=lax.Precision.HIGHEST, preferred_element_type=jnp.float32
    )


def slot_table(group_ids, parents):
    tree_segs = parents.shape[1]
    group_segs = group_ids.shape[0]
    seg_range = jnp.arange(tree_segs, dtype=jnp.int32)
    walker = seg_range[None, :]
    reached = walker[:, :, None] == seg_range[None, None, :]

    def climb(step_index, carried):
        walker_now, reached_now = carried
        walker_now = jnp.sum(
            jnp.where(walker_now[:, :, None] == seg_range[None, None, :], parents[:, None, :], 0),
            axis=2,
        )
        return (walker_now, reached_now | (walker_now[:, :, None] == seg_range[None, None, :]))

    walker, reached = lax.fori_loop(0, tree_segs, climb, (walker, reached))
    anc_flat = reached.reshape(group_segs, tree_segs).astype(jnp.float32)
    id_picks = (group_ids[:, None] == jnp.arange(group_segs, dtype=jnp.int32)[None, :]).astype(
        jnp.float32
    )
    seg_rows = exact_dot(id_picks, anc_flat)
    local_pick = ((group_ids % tree_segs)[:, None] == seg_range[None, :]).astype(jnp.float32)
    tree_of = group_ids // tree_segs
    same_tree = (tree_of[:, None] == tree_of[None, :]).astype(jnp.float32)
    return (
        lax.dot_general(
            seg_rows,
            local_pick,
            (((1,), (1,)), ((), ())),
            precision=lax.Precision.HIGHEST,
            preferred_element_type=jnp.float32,
        )
        * same_tree
    )


def visible_mask(allowed, seg_len, query_start, query_rows, key_start, key_rows):
    group_segs = allowed.shape[0]
    query_index = query_start + jnp.arange(query_rows, dtype=jnp.int32)
    key_index = key_start + jnp.arange(key_rows, dtype=jnp.int32)
    query_slot = query_index // seg_len
    key_slot = key_index // seg_len
    seg_range = jnp.arange(group_segs, dtype=jnp.int32)
    query_pick = (query_slot[:, None] == seg_range[None, :]).astype(jnp.float32)
    key_pick = (key_slot[:, None] == seg_range[None, :]).astype(jnp.float32)
    linked = (
        lax.dot_general(
            exact_dot(query_pick, allowed),
            key_pick,
            (((1,), (1,)), ((), ())),
            precision=lax.Precision.HIGHEST,
            preferred_element_type=jnp.float32,
        )
        > 0.5
    )
    return linked & (
        (query_slot[:, None] != key_slot[None, :]) | (key_index[None, :] <= query_index[:, None])
    )


def pair_terms(query_part, grad_part, stat_part, delta_part, key_part, value_part, visible):
    scores = (
        jnp.einsum("qhd,khd->qhk", query_part, key_part, preferred_element_type=jnp.float32) * 0.125
    )
    scores = jnp.where(visible[:, None, :], scores, masked_score)
    probs_full = jnp.exp(scores - stat_part[:, :, None])
    grad_probs = jnp.einsum(
        "qhd,khd->qhk", grad_part, value_part, preferred_element_type=jnp.float32
    )
    grad_scores = (probs_full * (grad_probs - delta_part[:, :, None])).astype(jnp.bfloat16)
    grad_query = None
    grad_key = None
    grad_value = None
    grad_query = (
        jnp.einsum("qhk,khd->qhd", grad_scores, key_part, preferred_element_type=jnp.float32)
        * 0.125
    )
    grad_key = (
        jnp.einsum("qhk,qhd->khd", grad_scores, query_part, preferred_element_type=jnp.float32)
        * 0.125
    )
    grad_value = jnp.einsum(
        "qhk,qhd->khd",
        probs_full.astype(jnp.bfloat16),
        grad_part,
        preferred_element_type=jnp.float32,
    )
    return (grad_query, grad_key, grad_value)


def shards(
    tokens,
    cotangent,
    qkv_weight,
    out_weight,
    up_weight,
    down_weight,
    gain_attn,
    gain_ffn,
    parents,
    slot_ids,
):
    local_rows = tokens.shape[0]
    model_width = tokens.shape[1]
    shard_count = lax.axis_size("shard")
    my_start = lax.axis_index("shard") * local_rows
    seg_len = local_rows * shard_count // slot_ids.shape[0]
    allowed = slot_table(slot_ids, parents)
    qkv_full, out_full, attn_gain = (
        lax.all_gather(qkv_weight.astype(jnp.bfloat16), "shard", axis=0, tiled=True),
        lax.all_gather(out_weight.astype(jnp.bfloat16), "shard", axis=0, tiled=True),
        lax.all_gather(gain_attn.astype(jnp.bfloat16), "shard", axis=0, tiled=True),
    )
    inputs = tokens.astype(jnp.float32)
    normed_one, inv_one = normalize(inputs)
    entered = (normed_one * attn_gain.astype(jnp.float32)).astype(jnp.bfloat16)
    qkv_all = jnp.dot(entered, qkv_full, preferred_element_type=jnp.float32).astype(jnp.bfloat16)
    queries = qkv_all[:, :model_width]
    keys_local = qkv_all[:, model_width : 2 * model_width]
    values_local = qkv_all[:, 2 * model_width :]
    query_heads = queries.reshape(local_rows, HEADS, HEAD)
    start_state = (
        jnp.full((local_rows, HEADS), masked_score, jnp.float32),
        jnp.zeros((local_rows, HEADS), jnp.float32),
        jnp.zeros((local_rows, HEADS, HEAD), jnp.float32),
    )
    carried = start_state
    key_piece = lax.all_gather(keys_local, "shard", axis=0, tiled=True)
    value_piece = lax.all_gather(values_local, "shard", axis=0, tiled=True)
    piece_rows = key_piece.shape[0]
    block_rows = block_size()
    count_blocks = piece_rows // block_rows
    key_blocks = key_piece.reshape(count_blocks, block_rows, HEADS, HEAD)
    value_blocks = value_piece.reshape(count_blocks, block_rows, HEADS, HEAD)

    def attend_block(running, blocks):
        key_block, value_block, block_index = blocks
        run_max, run_sum, run_acc = running
        visible = visible_mask(
            allowed, seg_len, my_start, local_rows, block_index * block_rows, block_rows
        )
        scores = (
            jnp.einsum("qhd,khd->qhk", query_heads, key_block, preferred_element_type=jnp.float32)
            * 0.125
        )
        scores = jnp.where(visible[:, None, :], scores, masked_score)
        new_max = jnp.maximum(run_max, jnp.max(scores, axis=2))
        rescale = jnp.exp(run_max - new_max)
        exp_scores = jnp.exp(scores - new_max[:, :, None])
        run_sum = run_sum * rescale + jnp.sum(exp_scores, axis=2)
        run_acc = run_acc * rescale[:, :, None] + jnp.einsum(
            "qhk,khd->qhd",
            exp_scores.astype(jnp.bfloat16),
            value_block,
            preferred_element_type=jnp.float32,
        )
        return ((new_max, run_sum, run_acc), None)

    carried, unused = lax.scan(
        attend_block, carried, (key_blocks, value_blocks, jnp.arange(count_blocks, dtype=jnp.int32))
    )
    run_max, run_sum, run_acc = carried
    attn_exact = run_acc / run_sum[:, :, None]
    log_sum = run_max + jnp.log(run_sum)
    attended = attn_exact.reshape(local_rows, model_width).astype(jnp.bfloat16)
    hidden = inputs + jnp.dot(attended, out_full, preferred_element_type=jnp.float32)
    up_full, down_full, ffn_gain = (
        lax.all_gather(up_weight.astype(jnp.bfloat16), "shard", axis=0, tiled=True),
        lax.all_gather(down_weight.astype(jnp.bfloat16), "shard", axis=0, tiled=True),
        lax.all_gather(gain_ffn.astype(jnp.bfloat16), "shard", axis=0, tiled=True),
    )
    normed_two, inv_two = normalize(hidden)
    second = (normed_two * ffn_gain.astype(jnp.float32)).astype(jnp.bfloat16)
    pre_act = jnp.dot(second, up_full, preferred_element_type=jnp.float32)
    active = gelu_exact(pre_act).astype(jnp.bfloat16)
    output = (hidden + jnp.dot(active, down_full, preferred_element_type=jnp.float32)).astype(
        jnp.bfloat16
    )
    up_full, down_full, ffn_gain = (
        lax.all_gather(up_weight.astype(jnp.bfloat16), "shard", axis=0, tiled=True),
        lax.all_gather(down_weight.astype(jnp.bfloat16), "shard", axis=0, tiled=True),
        lax.all_gather(gain_ffn.astype(jnp.bfloat16), "shard", axis=0, tiled=True),
    )
    qkv_full, out_full, attn_gain = (
        lax.all_gather(qkv_weight.astype(jnp.bfloat16), "shard", axis=0, tiled=True),
        lax.all_gather(out_weight.astype(jnp.bfloat16), "shard", axis=0, tiled=True),
        lax.all_gather(gain_attn.astype(jnp.bfloat16), "shard", axis=0, tiled=True),
    )
    grad_down = t_times(active, cotangent)
    grad_active = times_t(cotangent, down_full).astype(jnp.bfloat16)
    grad_pre = (grad_active.astype(jnp.float32) * gelu_slope(pre_act)).astype(jnp.bfloat16)
    grad_up = t_times(second, grad_pre)
    grad_second = times_t(grad_pre, up_full)
    grad_gain_ffn = jnp.sum(grad_second * normed_two, axis=0)
    grad_hidden = cotangent.astype(jnp.float32) + norm_back(
        grad_second * ffn_gain.astype(jnp.float32), normed_two, inv_two
    )
    grad_y = grad_hidden.astype(jnp.bfloat16)
    grad_out = t_times(attended, grad_y)
    grad_attn = times_t(grad_y, out_full).astype(jnp.bfloat16)
    grad_heads = grad_attn.reshape(local_rows, HEADS, HEAD)
    row_delta = jnp.sum(grad_heads.astype(jnp.float32) * attn_exact, axis=2)
    start_back = jnp.zeros((local_rows, HEADS, HEAD), jnp.float32)
    carried = start_back
    key_piece = lax.all_gather(keys_local, "shard", axis=0, tiled=True)
    value_piece = lax.all_gather(values_local, "shard", axis=0, tiled=True)
    piece_rows = key_piece.shape[0]
    back_block_rows = block_size()
    count_blocks = piece_rows // back_block_rows
    key_blocks = key_piece.reshape(count_blocks, back_block_rows, HEADS, HEAD)
    value_blocks = value_piece.reshape(count_blocks, back_block_rows, HEADS, HEAD)

    def back_block(running, blocks):
        grad_query = running
        key_block, value_block, block_index = blocks
        block_start = block_index * back_block_rows
        visible = visible_mask(allowed, seg_len, my_start, local_rows, block_start, back_block_rows)
        part_query, part_key, part_value = pair_terms(
            query_heads, grad_heads, log_sum, row_delta, key_block, value_block, visible
        )
        joined = jnp.concatenate(
            (
                part_key.reshape(back_block_rows, model_width),
                part_value.reshape(back_block_rows, model_width),
            ),
            axis=1,
        )
        return (grad_query + part_query, joined.astype(jnp.bfloat16))

    carried, key_terms = lax.scan(
        back_block, carried, (key_blocks, value_blocks, jnp.arange(count_blocks, dtype=jnp.int32))
    )
    grad_query = carried
    key_terms = key_terms.reshape(piece_rows, 2 * model_width)
    key_grads = lax.psum_scatter(key_terms, "shard", scatter_dimension=0, tiled=True)
    grad_qkv = jnp.concatenate(
        (grad_query.reshape(local_rows, model_width), key_grads), axis=1
    ).astype(jnp.bfloat16)
    grad_qkv_weight = t_times(entered, grad_qkv)
    grad_entered = times_t(grad_qkv, qkv_full)
    grad_gain_attn = jnp.sum(grad_entered * normed_one, axis=0)
    input_grad = grad_hidden + norm_back(
        grad_entered * attn_gain.astype(jnp.float32), normed_one, inv_one
    )
    group_sums = (
        lax.psum_scatter(grad_qkv_weight.astype(jnp.bfloat16), "shard", scatter_dimension=0, tiled=True),
        lax.psum_scatter(grad_out.astype(jnp.bfloat16), "shard", scatter_dimension=0, tiled=True),
        lax.psum_scatter(grad_up.astype(jnp.bfloat16), "shard", scatter_dimension=0, tiled=True),
        lax.psum_scatter(grad_down.astype(jnp.bfloat16), "shard", scatter_dimension=0, tiled=True),
        lax.psum_scatter(grad_gain_attn, "shard", scatter_dimension=0, tiled=True),
        lax.psum_scatter(grad_gain_ffn, "shard", scatter_dimension=0, tiled=True),
    )
    totals = (
        lax.psum(group_sums[0].astype(jnp.bfloat16), "rep").astype(jnp.float32),
        lax.psum(group_sums[1].astype(jnp.bfloat16), "rep").astype(jnp.float32),
        lax.psum(group_sums[2].astype(jnp.bfloat16), "rep").astype(jnp.float32),
        lax.psum(group_sums[3].astype(jnp.bfloat16), "rep").astype(jnp.float32),
        lax.psum(group_sums[4].astype(jnp.bfloat16), "rep").astype(jnp.float32),
        lax.psum(group_sums[5].astype(jnp.bfloat16), "rep").astype(jnp.float32),
    )
    return (output, input_grad, totals[0], totals[1], totals[2], totals[3], totals[4], totals[5])


MESH = pl.DeviceIdType.MESH


def ring_place(shard):
    return (1 - shard % 2) * (shard // 2) + (shard % 2) * (7 - shard // 2)


def ring_shard(place):
    upper = place // 4
    return (1 - upper) * 2 * place + upper * (15 - 2 * place)


def remote(source, target, sent, got, device):
    return pltpu.make_async_remote_copy(
        src_ref=source,
        dst_ref=target,
        send_sem=sent,
        recv_sem=got,
        device_id=device,
        device_id_type=MESH,
    )


def around(place, offset):
    return ring_shard(lax.rem(place + offset + 8, 8))


class Where:
    def __init__(self):
        self.rep = lax.axis_index("rep")
        self.me = lax.axis_index("shard")
        self.y = self.rep // 2
        self.core = self.rep % 2
        self.rep_y = (1 - self.y) * 2 + self.core
        self.rep_core = self.y * 2 + 1 - self.core
        self.rep_far = (1 - self.y) * 2 + 1 - self.core
        self.place = ring_place(self.me)
        self.right = around(self.place, 1)
        self.left = around(self.place, -1)

    def other(self, step):
        return lax.rem(self.me + step, 8)

    def back(self, step):
        return lax.rem(self.me + 8 - step, 8)

    def greet(self):
        barrier = pltpu.get_barrier_semaphore()
        for step in range(1, 8):
            pl.semaphore_signal(
                barrier, inc=1, device_id=(self.rep, self.other(step)), device_id_type=MESH
            )
        for rep in (self.rep_y, self.rep_core, self.rep_far):
            pl.semaphore_signal(barrier, inc=1, device_id=(rep, self.me), device_id_type=MESH)
        pl.semaphore_wait(barrier, 10)


def normed_rows(values):
    average = jnp.mean(values, axis=-1, keepdims=True)
    centered = values - average
    variance = jnp.mean(centered * centered, axis=-1, keepdims=True)
    inv_std = lax.rsqrt(variance + 1e-05)
    return (centered * inv_std, inv_std)


def gain_row(gains_ref, which):
    return jnp.concatenate(
        [gains_ref[s, which * 8 : which * 8 + 1, :] for s in range(8)], axis=1
    ).astype(jnp.float32)


def head_lanes(values, head):
    lane = lax.broadcasted_iota(jnp.int32, values.shape, 1)
    return jnp.where(lane // HEAD == head, values, jnp.zeros_like(values))


def tile_masks(block, parents_ref):
    key_row = lax.broadcasted_iota(jnp.int32, (256, 256), 0)
    query_row = lax.broadcasted_iota(jnp.int32, (256, 256), 1)
    own = key_row <= query_row
    if block < 5:
        return (own, None)
    own = own & (key_row // 128 == query_row // 128)
    if block == 5:
        return (own, None)
    parent = jnp.where(query_row < 128, parents_ref[2 * block], parents_ref[2 * block + 1])
    return (own, parent == 10 + key_row // 128)


def score_parts(block, keys_ref, queries, masks):
    own_mask, branch_mask = masks
    full = 256 * block if block < 5 else 1280
    spans = [(0, full, None)] if full else []
    if branch_mask is not None:
        spans.append((1280, 256, branch_mask))
    spans.append((256 * block, 256, own_mask))
    parts = []
    for first, rows, mask in spans:
        scores = times_t(keys_ref[pl.ds(first, rows), :], queries)
        if mask is not None:
            scores = jnp.where(mask, scores, masked_score)
        parts.append((first, rows, scores))
    return parts


def summed(*parts):
    total = parts[0].astype(jnp.float32)
    for part in parts[1:]:
        total = total + part.astype(jnp.float32)
    return total


BLOCK_ORDER = [4, 3, -3, 2, -2, 1, -1, 0]


def layer_kernel(
    ids_ref, parents_ref, tok_ref, cot_ref, gain_ref, qkv_w, out_w, up_w, down_w,
    layer_ref, in_ref, qkv_out, out_out, up_out, down_out, gain_out, ent_hbm,
    stage, wq_send, slices, gains_ref, tok_all, qkv_slots, qkv, side_t, tree_rows, slot_rows,
    mixed, logs, att, out_all, w_all, xch, acts, parts, gw, rr, rr_out, cr_out, yr_out,
    do_slots, dk, dv, gq_t, qs_core, qs_half, qs_recv, qs_y, fin_up, gp, gp_recv, gp_rep,
    load_s, small_s, small_r, slc_s, slc_r, tok_s, tok_r, o_s, o_r, oy_s, oy_r, oc_s, oc_r, w_s, w_r,
    keep_s, mix_s, mix_r, cot_s, cot_r, sec_s, sec_r, part_s, part_r, do_s, do_r,
    go_s, go_r, rs_s, rs_r, ro_s, ro_r, fin_s, fin_r, ge_s, ge_r, qs_s, qs_r, qr_s, qr_r,
    gp_s, gp_r, gr_s, gr_r,
):
    low, full = jnp.bfloat16, jnp.float32
    dq_t, gq_slots = mixed, qkv.reshape(8, 256, 384)
    at = Where()
    rep, me, y, core = at.rep, at.me, at.y, at.core
    ring_device = ((rep, at.right), (rep, at.left))
    over_y, over_core = (at.rep_y, me), (at.rep_core, me)
    places = []
    for seg in range(16):
        place = jnp.int32(0)
        for slot in range(1, 16):
            place = jnp.where(ids_ref[slot] == seg, slot, place)
        places.append(place)

    loads = [
        pltpu.make_async_copy(qkv_w.at[:, pl.ds(j * 1024, 1024)], stage.at[j], load_s.at[j])
        for j in range(3)
    ]
    loads.append(pltpu.make_async_copy(out_w, stage.at[3], load_s.at[3]))
    loads.append(
        pltpu.make_async_copy(down_w.at[pl.ds(rep * 128, 128), :], stage.at[5], load_s.at[4])
    )
    for s in range(8):
        columns = pl.ds(pl.multiple_of(s * 512 + rep * 128, 128), 128)
        loads.append(
            pltpu.make_async_copy(
                up_w.at[:, columns], stage.at[4, :, pl.ds(s * 128, 128)], load_s.at[5 + s]
            )
        )
    for copy in loads:
        copy.start()
    at.greet()

    def flow_block(flow, offset):
        return around(at.place, -offset if flow else offset)

    def token_copy(flow, step, half):
        origin = flow_block(flow, -step)
        source = tok_ref if step == 0 else tok_all.at[origin]
        rows = pl.ds(half * 128, 128)
        return remote(
            source.at[rows, :],
            tok_all.at[origin, rows, :],
            tok_s.at[flow, step, half],
            tok_r.at[flow, step, half],
            ring_device[flow],
        )

    def step_halves(step):
        if step == 3:
            return [(0, 0), (1, 1)]
        return [(half, flow) for half in range(2) for flow in range(2)]

    def out_copy(flow, step):
        spot = out_all.at[flow_block(flow, -step), rep]
        return remote(spot, spot, o_s.at[flow, step], o_r.at[flow, step], ring_device[flow])

    def out_flows(step):
        return (0, 1) if step < 3 else (0,)

    def out_over_y(flow, step):
        spot = out_all.at[flow_block(flow, -step - 1), rep]
        return remote(spot, spot, oy_s.at[flow, step], oy_r.at[flow, step], over_y)

    def out_over_core(flow, step, own):
        spot = out_all.at[flow_block(flow, -step - 1), rep if own else at.rep_y]
        return remote(spot, spot, oc_s.at[own, flow, step], oc_r.at[own, flow, step], over_core)

    def w_copy(flow, step, half):
        spot = w_all.at[flow_block(flow, -step), half]
        return remote(spot, spot, w_s.at[flow, step, half], w_r.at[flow, step, half], ring_device[flow])

    def w_step(step):
        for half, flow in step_halves(step):
            w_copy(flow, step, half).wait_recv()
            if step < 2 or (step == 2 and half == flow):
                w_copy(flow, step + 1, half).start()

    small = [
        remote(
            gain_ref,
            gains_ref.at[me],
            small_s.at[0, step],
            small_r.at[0, step],
            (rep, at.other(step)),
        )
        for step in range(1, 8)
    ]
    small += [
        remote(
            wq_send.at[at.other(step), :, core],
            slices.at[me, :, core],
            small_s.at[1, step],
            small_r.at[1, step],
            (rep, at.other(step)),
        )
        for step in range(1, 8)
    ]
    slice_core = remote(
        slices.at[:, :, core], slices.at[:, :, core], slc_s.at[0], slc_r.at[0], over_core
    )
    cot_y = remote(cot_ref, xch.at[6], cot_s.at[0], cot_r.at[0], over_y)
    cot_core = remote(cot_ref, xch.at[5], cot_s.at[1], cot_r.at[1], over_core)
    cot_far = remote(xch.at[6], xch.at[7], cot_s.at[2], cot_r.at[2], over_core)

    for copy in small[:7]:
        copy.start()
    for half in range(2):
        for flow in range(2):
            token_copy(flow, 0, half).start()
    cot_y.start()
    cot_core.start()
    for copy in loads[:3]:
        copy.wait()
    for s in range(8):
        for j in range(3):
            wq_send[s, :, :, :, j * 128 : j * 128 + 128] = (
                stage[j, :, s * 128 : s * 128 + 128].astype(low).reshape(2, 2, 32, 128)
            )
    for copy in small[7:]:
        copy.start()
    gains_ref[me] = gain_ref[...]
    slices[me, :, core] = wq_send[me, :, core]
    loads[3].wait()
    out_all[me] = stage[3].astype(low).reshape(4, 32, 1024)
    for flow in range(2):
        out_copy(flow, 0).start()
    for copy in loads[4:]:
        copy.wait()
    w_all[me, 0] = stage[4].astype(low)
    w_all[me, 1] = stage[5].astype(low)
    xch[4] = cot_ref[...]
    for copy in small:
        copy.wait_recv()
    slice_core.start()
    slice_core.wait_recv()
    gain = gain_row(gains_ref, 0)

    kept = {}

    def enter(rows, origin, count):
        slot = 4 + count % 2
        if count > 1:
            kept[count - 2].wait()
        normed, _ = normed_rows(rows.astype(full))
        entered = (normed * gain).astype(low)
        parts[slot] = entered
        kept[count] = pltpu.make_async_copy(parts.at[slot], ent_hbm.at[origin], keep_s.at[slot - 4])
        kept[count].start()
        weights = slices[...].reshape(1024, 384)
        made = jnp.dot(entered, weights, preferred_element_type=full).astype(low)
        qkv_slots[2 * origin] = made[:128]
        qkv_slots[2 * origin + 1] = made[128:]

    enter(tok_ref[...], me, 0)
    count = 1
    for step in range(4):
        for half, flow in step_halves(step):
            token_copy(flow, step, half).wait_recv()
            if step < 2 or (step == 2 and half == flow):
                token_copy(flow, step + 1, half).start()
        for flow in out_flows(step):
            out_copy(flow, step).wait_recv()
            if step < 2 or (step == 2 and flow == 0):
                out_copy(flow, step + 1).start()
            out_over_y(flow, step).start()
            out_over_core(flow, step, 1).start()
        if step == W_START:
            for half in range(2):
                for flow in range(2):
                    w_copy(flow, 0, half).start()
        for flow in out_flows(step):
            origin = flow_block(flow, -step - 1)
            enter(tok_all[origin], origin, count)
            count += 1
    cot_y.wait_recv()
    cot_far.start()
    kept[6].wait()
    kept[7].wait()

    for seg in range(16):
        qkv[seg * 128 : seg * 128 + 128, :] = qkv_slots[places[seg]]
    for block in range(8):
        side_t[:, block * 256 : block * 256 + 256] = qkv[block * 256 : block * 256 + 256, 256:384].T

    for block in range(8):
        masks = tile_masks(block, parents_ref)
        rows = pl.ds(block * 256, 256)

        def one_head(head, unused):
            queries = head_lanes(qkv[rows, 0:128], head) * low(0.125)
            tiles = score_parts(block, qkv.at[:, pl.ds(128, 128)], queries, masks)
            top = None
            for _, _, scores in tiles:
                part = jnp.max(scores, axis=0, keepdims=True)
                top = part if top is None else jnp.maximum(top, part)
            total = None
            mix = None
            head_rows = pl.ds(pl.multiple_of(head * HEAD, HEAD), HEAD)
            for first, number, scores in tiles:
                weights = jnp.exp(scores - top)
                part = jnp.sum(weights, axis=0, keepdims=True)
                total = part if total is None else total + part
                term = jnp.dot(
                    side_t[head_rows, pl.ds(first, number)],
                    weights.astype(low),
                    preferred_element_type=full,
                )
                mix = term if mix is None else mix + term
            mixed[head_rows, block * 256 : block * 256 + 256] = mix / total
            logs[pl.ds(pl.multiple_of(head * 8, 8), 8), block * 256 : block * 256 + 256] = (
                jnp.broadcast_to(top + jnp.log(total), (8, 256))
            )
            return unused

        lax.fori_loop(0, 2, one_head, 0)
        tree = mixed[:, block * 256 : block * 256 + 256].T.astype(low)
        tree_rows[2 * block] = tree[:128]
        tree_rows[2 * block + 1] = tree[128:]
        if block in W_BLOCKS:
            w_step(W_BLOCKS.index(block))

    for slot in range(16):
        slot_rows[slot // 2, (slot % 2) * 128 : (slot % 2) * 128 + 128, :] = tree_rows[
            ids_ref[slot]
        ]
    my_columns = pl.ds(pl.multiple_of(me * 128, 128), 128)
    mix_sends = [
        remote(
            slot_rows.at[at.other(step)],
            att.at[:, my_columns],
            mix_s.at[step],
            mix_r.at[step],
            (rep, at.other(step)),
        )
        for step in range(1, 8)
    ]
    for copy in mix_sends:
        copy.start()
    att[:, my_columns] = slot_rows[me]
    for step in range(4):
        for flow in out_flows(step):
            out_over_y(flow, step).wait_recv()
            out_over_core(flow, step, 0).start()
    for step in range(4):
        for flow in out_flows(step):
            out_over_core(flow, step, 1).wait_recv()
            out_over_core(flow, step, 0).wait_recv()
    for step in range(len(W_BLOCKS), 3):
        w_step(step)
    for copy in mix_sends:
        copy.wait_recv()

    out_full = out_all[...].reshape(1024, 1024)
    hidden = tok_ref[...].astype(full) + jnp.dot(att[...], out_full, preferred_element_type=full)
    ffn_gain = gain_row(gains_ref, 1)
    normed_two, _ = normed_rows(hidden)
    xch[0] = (normed_two * ffn_gain).astype(low)
    sec_y = remote(xch.at[0], xch.at[2], sec_s.at[0], sec_r.at[0], over_y)
    sec_core = remote(xch.at[0], xch.at[1], sec_s.at[1], sec_r.at[1], over_core)
    sec_far = remote(xch.at[2], xch.at[3], sec_s.at[2], sec_r.at[2], over_core)
    sec_y.start()
    sec_core.start()
    stage[0] = hidden[:128]
    stage[1] = hidden[128:]
    for step in range(4):
        for half, flow in step_halves(step):
            token_copy(flow, step, half).wait_send()
    w_step(3)
    sec_y.wait_recv()
    sec_far.start()
    cot_core.wait_recv()
    cot_far.wait_recv()

    up = w_all[:, 0].reshape(1024, 1024)
    down = w_all[:, 1].reshape(1024, 1024)

    def ffn(first):
        second = xch[first : first + 2].reshape(512, 1024)
        cots = xch[4 + first : 6 + first].reshape(512, 1024)
        pre = jnp.dot(second, up, preferred_element_type=full)
        bell = 1.0 + lax.erf(pre * 0.7071067811865476)
        acts[first : first + 2] = (0.5 * pre * bell).astype(low).reshape(2, 2, 128, 1024)
        slope = 0.5 * bell + pre * jnp.exp(-0.5 * pre * pre) * 0.3989422804014327
        grad_act = times_t(cots, down).astype(low).astype(full)
        grad_pre = (grad_act * slope).astype(low)
        acts[4 + first : 6 + first] = grad_pre.reshape(2, 2, 128, 1024)
        return times_t(grad_pre, up)

    def part_copy(kind, leg):
        index = kind * 3 + leg
        return remote(
            tok_all.at[index],
            parts.at[index],
            part_s.at[index],
            part_r.at[index],
            over_y if leg == 1 else over_core,
        )

    sec_core.wait_recv()
    sec_far.wait_recv()
    grad_far = ffn(2)
    tok_all[0] = grad_far[256:].astype(low)
    part_copy(0, 0).start()
    stage[2] = grad_far[:128]
    stage[3] = grad_far[128:256]
    part_copy(0, 0).wait_recv()
    tok_all[1] = summed(stage[2:4].reshape(256, 1024), parts[0]).astype(low)
    part_copy(0, 1).start()
    grad_near = ffn(0)
    tok_all[2] = grad_near[256:].astype(low)
    part_copy(0, 2).start()
    stage[2] = grad_near[:128]
    stage[3] = grad_near[128:256]

    def outputs(first):
        active = acts[first : first + 2].reshape(512, 1024)
        return jnp.dot(active, down, preferred_element_type=full)

    made = outputs(2)
    tok_all[3] = made[256:].astype(low)
    part_copy(1, 0).start()
    stage[4] = made[:128]
    stage[5] = made[128:256]
    part_copy(1, 0).wait_recv()
    tok_all[4] = summed(stage[4:6].reshape(256, 1024), parts[3]).astype(low)
    made = outputs(0)
    tok_all[5] = made[256:].astype(low)
    part_copy(1, 2).start()
    stage[0] = stage[0] + made[:128]
    stage[1] = stage[1] + made[128:256]
    for step in range(4):
        for half, flow in step_halves(step):
            w_copy(flow, step, half).wait_send()

    part_copy(0, 2).wait_recv()
    part_copy(0, 1).wait_recv()
    part_copy(1, 1).start()
    grad_second = summed(stage[2:4].reshape(256, 1024), parts[1], parts[2])
    hidden = tok_ref[...].astype(full) + jnp.dot(
        att[...], out_all[...].reshape(1024, 1024), preferred_element_type=full
    )
    normed_two, inv_two = normed_rows(hidden)
    gain_two = jnp.sum(grad_second * normed_two, axis=0, keepdims=True)
    for s in range(8):
        gp[s, 8:16, :] = jnp.broadcast_to(gain_two[:, s * 128 : s * 128 + 128], (8, 128))
    grad_hidden = cot_ref[...].astype(full) + norm_back(
        grad_second * gain_row(gains_ref, 1), normed_two, inv_two
    )
    stage[2] = grad_hidden[:128]
    stage[3] = grad_hidden[128:]
    grad_y = grad_hidden.astype(low)
    grad_attn = times_t(grad_y, out_all[...].reshape(1024, 1024)).astype(low)
    for copy in mix_sends:
        copy.wait_send()
    for s in range(8):
        slot_rows[s] = grad_attn[:, s * 128 : s * 128 + 128]
    do_sends = [
        remote(
            slot_rows.at[at.other(step)],
            do_slots.at[me],
            do_s.at[step],
            do_r.at[step],
            (rep, at.other(step)),
        )
        for step in range(1, 8)
    ]
    for copy in do_sends:
        copy.start()
    do_slots[me] = slot_rows[me]

    def w_grad(offset):
        block = around(at.place, offset)
        columns = pl.ds(pl.multiple_of(block * 128, 128), 128)
        seconds = xch[0:4, :, columns].reshape(1024, 128)
        gw[block, 0] = jnp.dot(
            seconds.T, acts[4:8].reshape(1024, 1024), preferred_element_type=full
        ).astype(low)
        heights = pl.ds(pl.multiple_of(block * 128, 128), 128)
        actives = acts[0:4, :, :, heights].reshape(1024, 128)
        gw[block, 1] = jnp.dot(
            actives.T, xch[4:8].reshape(1024, 1024), preferred_element_type=full
        ).astype(low)

    def rs_copy(flow, step, half):
        return remote(
            gw.at[flow_block(flow, 4 - step), half],
            rr.at[flow, step, half],
            rs_s.at[flow, step, half],
            rs_r.at[flow, step, half],
            ring_device[flow],
        )

    def rs_step(step):
        for flow in range(2):
            block = flow_block(flow, 4 - step)
            for half in range(2):
                if step == 0 and half != flow:
                    continue
                if step > 1 or (step == 1 and half == flow):
                    rs_copy(flow, step - 1, half).wait_recv()
                    gw[block, half] = summed(gw[block, half], rr[flow, step - 1, half]).astype(low)
                rs_copy(flow, step, half).start()

    w_grad(4)
    rs_step(0)
    w_grad(3)
    w_grad(-3)
    for step in range(4):
        for flow in out_flows(step):
            out_copy(flow, step).wait_send()
            out_over_y(flow, step).wait_send()
            out_over_core(flow, step, 0).wait_send()
            out_over_core(flow, step, 1).wait_send()
    for block in range(8):
        out_all[block] = (
            jnp.dot(
                att[:, block * 128 : block * 128 + 128].T, grad_y, preferred_element_type=full
            )
            .astype(low)
            .reshape(4, 32, 1024)
        )
    outs = out_all
    go_core = [
        remote(
            outs.at[:, 2 * i + 1 - core], cr_out.at[:, i], go_s.at[i], go_r.at[i], over_core
        )
        for i in range(2)
    ]
    for copy in go_core:
        copy.start()
    rs_step(1)
    for offset in BLOCK_ORDER[3:]:
        w_grad(offset)
    for copy in (cot_y, cot_core, cot_far, sec_y, sec_core, sec_far):
        copy.wait_send()
    fetch = pltpu.make_async_copy(ent_hbm, xch, load_s.at[0])
    fetch.start()
    for copy in go_core:
        copy.wait_recv()
    outs[:, at.rep_y] = summed(outs[:, at.rep_y], cr_out[:, 1 - y]).astype(low)
    go_y = remote(outs.at[:, at.rep_y], yr_out, go_s.at[2], go_r.at[2], over_y)
    go_y.start()

    def ro_copy(flow, step):
        return remote(
            outs.at[flow_block(flow, 4 - step), rep],
            rr_out.at[flow, step],
            ro_s.at[flow, step],
            ro_r.at[flow, step],
            ring_device[flow],
        )

    def ro_flows(step):
        return (0, 1) if step else (0,)

    def ro_step(step):
        for flow in ro_flows(step):
            block = flow_block(flow, 4 - step)
            if step > 0 and flow in ro_flows(step - 1):
                ro_copy(flow, step - 1).wait_recv()
                outs[block, rep] = summed(outs[block, rep], rr_out[flow, step - 1]).astype(low)
            ro_copy(flow, step).start()

    for copy in do_sends:
        copy.wait_recv()
    for seg in range(16):
        tree_rows[seg] = do_slots.reshape(16, 128, 128)[places[seg]]
    for block in range(8):
        side_t[:, block * 256 : block * 256 + 256] = qkv[block * 256 : block * 256 + 256, 128:256].T
    dk[...] = jnp.zeros_like(dk)
    dv[...] = jnp.zeros_like(dv)

    for block in range(8):
        masks = tile_masks(block, parents_ref)
        rows = pl.ds(block * 256, 256)

        def one_head_back(head, unused):
            head_rows = pl.ds(pl.multiple_of(head * HEAD, HEAD), HEAD)
            queries = head_lanes(qkv[rows, 0:128], head) * low(0.125)
            grads = tree_rows[2 * block : 2 * block + 2].reshape(256, 128)
            grad_rows = head_lanes(grads, head)
            lse = logs[pl.ds(pl.multiple_of(head * 8, 8), 8), block * 256 : block * 256 + 256][0:1]
            both = grads.T.astype(full) * mixed[:, block * 256 : block * 256 + 256]
            delta = jnp.where(
                head == 0,
                jnp.sum(both[:HEAD], axis=0, keepdims=True),
                jnp.sum(both[HEAD:], axis=0, keepdims=True),
            )
            grad_query = None
            for first, number, scores in score_parts(
                block, qkv.at[:, pl.ds(128, 128)], queries, masks
            ):
                keys = pl.ds(first, number)
                weights = jnp.exp(scores - lse)
                grad_weights = times_t(qkv[keys, 256:384], grad_rows)
                grad_scores = (weights * (grad_weights - delta)).astype(low)
                dk[keys, :] += jnp.dot(grad_scores, queries, preferred_element_type=full)
                dv[keys, :] += jnp.dot(weights.astype(low), grad_rows, preferred_element_type=full)
                term = jnp.dot(side_t[head_rows, keys], grad_scores, preferred_element_type=full)
                grad_query = term if grad_query is None else grad_query + term
            dq_t[head_rows, block * 256 : block * 256 + 256] = grad_query * 0.125
            return unused

        lax.fori_loop(0, 2, one_head_back, 0)
        if block == 3:
            rs_step(2)
        if block == 4:
            outs[:, rep] = summed(outs[:, rep], cr_out[:, y]).astype(low)
            go_y.wait_recv()
            outs[:, rep] = summed(outs[:, rep], yr_out[...]).astype(low)
            ro_step(0)
        if block == 6:
            ro_step(1)

    for seg in range(16):
        rows = pl.ds(seg * 128, 128)
        qkv_slots[seg, :, 0:128] = dq_t[:, seg * 128 : seg * 128 + 128].T.astype(low)
        qkv_slots[seg, :, 128:256] = dk[rows, :].astype(low)
        qkv_slots[seg, :, 256:384] = dv[rows, :].astype(low)
    for slot in range(16):
        gq_slots[slot // 2, (slot % 2) * 128 : (slot % 2) * 128 + 128, :] = qkv_slots[ids_ref[slot]]

    def ge_copy(flow, step):
        source, target = acts.at[flow * 4 + step], w_all.at[flow * 4 + step]
        if step == 0:
            source, target = source.at[flow], target.at[flow]
        return remote(
            source, target, ge_s.at[flow, step], ge_r.at[flow, step], ring_device[flow]
        )

    def ge_part(block):
        return times_t(gq_slots[block], slices[...].reshape(1024, 384))

    def ge_step(step):
        for flow in range(2):
            part = ge_part(flow_block(flow, 4 - step))
            if step > 0:
                ge_copy(flow, step - 1).wait_recv()
            for half in range(2):
                if step == 0 and half != flow:
                    continue
                rows = part[half * 128 : half * 128 + 128]
                if step > 1 or (step == 1 and half == flow):
                    rows = rows + w_all[flow * 4 + step - 1, half].astype(full)
                acts[flow * 4 + step, half] = rows.astype(low)
            ge_copy(flow, step).start()

    ge_step(0)
    rs_step(3)
    ro_step(2)
    for block in range(8):
        gq_t[:, block * 256 : block * 256 + 256] = gq_slots[block].T
    fetch.wait()
    for copy in small:
        copy.wait_send()
    for s in range(8):
        made = jnp.dot(
            gq_t[...],
            xch[:, :, s * 128 : s * 128 + 128].reshape(2048, 128),
            preferred_element_type=full,
        )
        wq_send[s] = made.T.astype(low).reshape(2, 2, 32, 384)
    qs_over_core = remote(wq_send.at[:, :, 1 - core], qs_core, qr_s.at[0], qr_r.at[0], over_core)
    qs_over_core.start()
    ge_step(1)
    qs_over_core.wait_recv()
    qs_half[...] = summed(wq_send[:, :, core], qs_core[...]).astype(low)
    qs_sends = [
        remote(
            qs_half.at[at.other(step)],
            qs_recv.at[me],
            qs_s.at[step],
            qs_r.at[step],
            (rep, at.other(step)),
        )
        for step in range(1, 8)
    ]
    for copy in qs_sends:
        copy.start()
    qs_recv[me] = qs_half[me]

    def final_copy(kind, leg):
        quarter = at.rep_y if leg == 2 else rep
        if kind == 0:
            spot = fin_up.at[quarter]
        elif kind == 1:
            spot = down_out.at[pl.ds(quarter * 128, 128), :]
        elif kind == 2:
            spot = out_out.at[pl.ds(quarter * 32, 32), :]
        else:
            spot = qkv_out.at[pl.ds(quarter * 32, 32), :]
        device = over_y if leg == 0 else over_core
        return remote(spot, spot, fin_s.at[kind, leg], fin_r.at[kind, leg], device)

    ro_step(3)
    ge_step(2)
    for half in range(2):
        for flow in range(2):
            rs_copy(flow, 3, half).wait_recv()
        total = summed(gw[me, half], rr[0, 3, half], rr[1, 3, half]).astype(low)
        if half == 0:
            fin_up[rep] = total
        else:
            down_out[pl.ds(rep * 128, 128), :] = total
        final_copy(half, 0).start()
        final_copy(half, 1).start()
    for copy in qs_sends:
        copy.wait_recv()
    qs_over_y = remote(qs_recv.at[:, 1 - y], qs_y, qr_s.at[1], qr_r.at[1], over_y)
    qs_over_y.start()
    for flow in range(2):
        ro_copy(flow, 3).wait_recv()
    out_out[pl.ds(rep * 32, 32), :] = summed(outs[me, rep], rr_out[0, 3], rr_out[1, 3]).astype(low)
    final_copy(2, 0).start()
    final_copy(2, 1).start()
    ge_step(3)
    part_copy(1, 1).wait_recv()
    part_copy(1, 2).wait_recv()
    tok_all[6] = summed(stage[0:2].reshape(256, 1024), parts[4], parts[5]).astype(low)
    layer_write = pltpu.make_async_copy(tok_all.at[6], layer_ref, load_s.at[1])
    layer_write.start()
    qs_over_y.wait_recv()
    quarter_rows = pl.ds(rep * 32, 32)
    for s in range(8):
        total = summed(qs_recv[s, y], qs_y[s]).astype(low)
        for j in range(3):
            first = j * 1024 + s * 128
            qkv_out[quarter_rows, first : first + 128] = total[:, j * 128 : j * 128 + 128]
    final_copy(3, 0).start()
    final_copy(3, 1).start()
    for kind in range(4):
        final_copy(kind, 0).wait_recv()
        final_copy(kind, 2).start()

    grad_entered = ge_part(me)
    for flow in range(2):
        ge_copy(flow, 3).wait_recv()
        grad_entered = grad_entered + w_all[flow * 4 + 3].reshape(256, 1024).astype(full)
    normed, inv_std = normed_rows(tok_ref[...].astype(full))
    gain_one = jnp.sum(grad_entered * normed, axis=0, keepdims=True)
    for s in range(8):
        gp[s, 0:8, :] = jnp.broadcast_to(gain_one[:, s * 128 : s * 128 + 128], (8, 128))
    gain_sends = [
        remote(
            gp.at[at.other(step)],
            gp_recv.at[me],
            gp_s.at[step],
            gp_r.at[step],
            (rep, at.other(step)),
        )
        for step in range(1, 8)
    ]
    for copy in gain_sends:
        copy.start()
    gp_recv[me] = gp[me]
    in_grad = stage[2:4].reshape(256, 1024) + norm_back(
        grad_entered * gain_row(gains_ref, 0), normed, inv_std
    )
    stage[4] = in_grad[:128]
    stage[5] = in_grad[128:]
    in_write = pltpu.make_async_copy(stage.at[4:6], in_ref, load_s.at[2])
    in_write.start()
    for copy in gain_sends:
        copy.wait_recv()
    total = gp_recv[0]
    for s in range(1, 8):
        total = total + gp_recv[s]
    gp_rep[rep] = total
    rep_sends = [
        remote(gp_rep.at[rep], gp_rep.at[rep], gr_s.at[i], gr_r.at[i], (to, me))
        for i, to in enumerate((at.rep_y, at.rep_core, at.rep_far))
    ]
    for copy in rep_sends:
        copy.start()
    for kind in range(4):
        final_copy(kind, 1).wait_recv()
        final_copy(kind, 2).wait_recv()
    for quarter in range(4):
        for s in range(8):
            first = s * 512 + quarter * 128
            up_out[:, first : first + 128] = fin_up[quarter, :, s * 128 : s * 128 + 128]
    for copy in rep_sends:
        copy.wait()
    gain_out[...] = gp_rep[0] + gp_rep[1] + gp_rep[2] + gp_rep[3]

    layer_write.wait()
    in_write.wait()
    for kind in range(4):
        for leg in range(3):
            final_copy(kind, leg).wait_send()
    qs_over_y.wait_send()
    qs_over_core.wait_send()
    go_y.wait_send()
    for copy in go_core + qs_sends + gain_sends + do_sends:
        copy.wait_send()
    slice_core.wait_send()
    for kind in range(2):
        for leg in range(3):
            part_copy(kind, leg).wait_send()
    for step in range(4):
        for flow in range(2):
            ge_copy(flow, step).wait_send()
            for half in range(2):
                if step > 0 or half == flow:
                    rs_copy(flow, step, half).wait_send()
        for flow in ro_flows(step):
            ro_copy(flow, step).wait_send()


W_START = 1
W_BLOCKS = [0, 3, 6]


def fast_shards(
    tokens, cotangent, qkv_weight, out_weight, up_weight, down_weight, gain_attn, gain_ffn, parents, slot_ids
):
    low, full = jnp.bfloat16, jnp.float32
    gains = jnp.concatenate(
        [jnp.broadcast_to(g.astype(low)[None], (8, 128)) for g in (gain_attn, gain_ffn)]
    )
    smem = pl.BlockSpec(memory_space=pltpu.SMEM)
    vmem = pl.BlockSpec(memory_space=pltpu.VMEM)
    anywhere = pl.BlockSpec(memory_space=pl.ANY)

    def dma(*shape):
        return pltpu.SemaphoreType.DMA(shape)

    v = pltpu.VMEM
    scratch = [
        v((6, 128, 1024), full),
        v((8, 2, 2, 32, 384), low),
        v((8, 2, 2, 32, 384), low),
        v((8, 16, 128), low),
        v((8, 256, 1024), low),
        v((16, 128, 384), low),
        v((2048, 384), low),
        v((128, 2048), low),
        v((16, 128, 128), low),
        v((8, 256, 128), low),
        v((128, 2048), full),
        v((16, 2048), full),
        v((256, 1024), low),
        v((8, 4, 32, 1024), low),
        v((8, 2, 128, 1024), low),
        v((8, 256, 1024), low),
        v((8, 2, 128, 1024), low),
        v((6, 256, 1024), low),
        v((8, 2, 128, 1024), low),
        v((2, 4, 2, 128, 1024), low),
        v((2, 4, 32, 1024), low),
        v((8, 2, 32, 1024), low),
        v((8, 32, 1024), low),
        v((8, 256, 128), low),
        v((2048, 128), full),
        v((2048, 128), full),
        v((384, 2048), low),
        v((8, 2, 32, 384), low),
        v((8, 2, 32, 384), low),
        v((8, 2, 32, 384), low),
        v((8, 32, 384), low),
        v((4, 128, 1024), low),
        v((8, 16, 128), full),
        v((8, 16, 128), full),
        v((4, 16, 128), full),
        dma(13), dma(2, 8), dma(2, 8), dma(1), dma(1), dma(2, 4, 2), dma(2, 4, 2),
        dma(2, 4), dma(2, 4), dma(2, 4), dma(2, 4), dma(2, 2, 4), dma(2, 2, 4),
        dma(2, 4, 2), dma(2, 4, 2), dma(2), dma(8), dma(8), dma(3), dma(3), dma(3), dma(3),
        dma(6), dma(6), dma(8), dma(8), dma(3), dma(3), dma(2, 4, 2), dma(2, 4, 2),
        dma(2, 4), dma(2, 4), dma(4, 3), dma(4, 3), dma(2, 4), dma(2, 4), dma(8), dma(8),
        dma(2), dma(2), dma(8), dma(8), dma(3), dma(3),
    ]
    made = pl.pallas_call(
        layer_kernel,
        out_shape=[
            jax.ShapeDtypeStruct((256, 1024), low),
            jax.ShapeDtypeStruct((2, 128, 1024), full),
            jax.ShapeDtypeStruct((128, 3072), low),
            jax.ShapeDtypeStruct((128, 1024), low),
            jax.ShapeDtypeStruct((128, 4096), low),
            jax.ShapeDtypeStruct((512, 1024), low),
            jax.ShapeDtypeStruct((16, 128), full),
            jax.ShapeDtypeStruct((8, 256, 1024), low),
        ],
        in_specs=[smem] * 2 + [vmem] * 3 + [anywhere] * 4,
        out_specs=[anywhere] * 2 + [vmem] * 5 + [anywhere],
        scratch_shapes=scratch,
        compiler_params=pltpu.CompilerParams(
            collective_id=1, has_side_effects=True, vmem_limit_bytes=VMEM_LIMIT
        ),
    )(
        slot_ids, parents.reshape(16), tokens, cotangent, gains, qkv_weight, out_weight, up_weight,
        down_weight,
    )
    layer_out, in_grad, qkv_grad, out_grad, up_grad, down_grad, gain_grads, _ = made
    return (
        layer_out,
        in_grad.reshape(256, 1024),
        qkv_grad.astype(full),
        out_grad.astype(full),
        up_grad.astype(full),
        down_grad.astype(full),
        gain_grads[0],
        gain_grads[8],
    )


VMEM_LIMIT = 61 * 2**20


def solution(mesh):
    in_specs = (
        P(("rep", "shard"), None),
        P(("rep", "shard"), None),
        P("shard", None),
        P("shard", None),
        P("shard", None),
        P("shard", None),
        P("shard"),
        P("shard"),
        P("rep", None),
        P("rep"),
    )
    out_specs = (
        P(("rep", "shard"), None),
        P(("rep", "shard"), None),
        P("shard", None),
        P("shard", None),
        P("shard", None),
        P("shard", None),
        P("shard"),
        P("shard"),
    )

    def fits(*args):
        shapes = [a.shape for a in args]
        return shapes[0] == (8192, 1024) and shapes[4] == (1024, 4096) and shapes[8] == (4, 16)

    small = mesh.shape["rep"] == 4 and mesh.shape["shard"] == 8

    def whole(*args):
        run = fast_shards if small and fits(*args) else shards
        return jax.shard_map(
            run, mesh=mesh, in_specs=in_specs, out_specs=out_specs, check_vma=False
        )(*args)

    return whole
```

```python
import jax
import jax.numpy as jnp
from jax import lax
from jax.experimental import pallas as pl
from jax.experimental.pallas import tpu as pltpu
from jax.sharding import PartitionSpec as P

HEADS = 16
HEAD = 64


masked_score = -1e30


def block_size():
    return 512


def normalize(values):
    average = jnp.mean(values, axis=-1, keepdims=True)
    centered = values - average
    variance = jnp.mean(centered * centered, axis=-1, keepdims=True)
    inv_std = lax.rsqrt(variance + 1e-05)
    return (centered * inv_std, inv_std)


def gelu_exact(values):
    return 0.5 * values * (1.0 + lax.erf(values * 0.7071067811865476))


def gelu_slope(values):
    return (
        0.5 * (1.0 + lax.erf(values * 0.7071067811865476))
        + values * jnp.exp(-0.5 * values * values) * 0.3989422804014327
    )


def norm_back(grad_normed, normed, inv_std):
    first_mean = jnp.mean(grad_normed, axis=-1, keepdims=True)
    second_mean = jnp.mean(grad_normed * normed, axis=-1, keepdims=True)
    return inv_std * (grad_normed - first_mean - normed * second_mean)


def times_t(left_side, right_side):
    return lax.dot_general(
        left_side, right_side, (((1,), (1,)), ((), ())), preferred_element_type=jnp.float32
    )


def t_times(left_side, right_side):
    return lax.dot_general(
        left_side, right_side, (((0,), (0,)), ((), ())), preferred_element_type=jnp.float32
    )


def exact_dot(left_side, right_side):
    return jnp.dot(
        left_side, right_side, precision=lax.Precision.HIGHEST, preferred_element_type=jnp.float32
    )


def slot_table(group_ids, parents):
    tree_segs = parents.shape[1]
    group_segs = group_ids.shape[0]
    seg_range = jnp.arange(tree_segs, dtype=jnp.int32)
    walker = seg_range[None, :]
    reached = walker[:, :, None] == seg_range[None, None, :]

    def climb(step_index, carried):
        walker_now, reached_now = carried
        walker_now = jnp.sum(
            jnp.where(walker_now[:, :, None] == seg_range[None, None, :], parents[:, None, :], 0),
            axis=2,
        )
        return (walker_now, reached_now | (walker_now[:, :, None] == seg_range[None, None, :]))

    walker, reached = lax.fori_loop(0, tree_segs, climb, (walker, reached))
    anc_flat = reached.reshape(group_segs, tree_segs).astype(jnp.float32)
    id_picks = (group_ids[:, None] == jnp.arange(group_segs, dtype=jnp.int32)[None, :]).astype(
        jnp.float32
    )
    seg_rows = exact_dot(id_picks, anc_flat)
    local_pick = ((group_ids % tree_segs)[:, None] == seg_range[None, :]).astype(jnp.float32)
    tree_of = group_ids // tree_segs
    same_tree = (tree_of[:, None] == tree_of[None, :]).astype(jnp.float32)
    return (
        lax.dot_general(
            seg_rows,
            local_pick,
            (((1,), (1,)), ((), ())),
            precision=lax.Precision.HIGHEST,
            preferred_element_type=jnp.float32,
        )
        * same_tree
    )


def visible_mask(allowed, seg_len, query_start, query_rows, key_start, key_rows):
    group_segs = allowed.shape[0]
    query_index = query_start + jnp.arange(query_rows, dtype=jnp.int32)
    key_index = key_start + jnp.arange(key_rows, dtype=jnp.int32)
    query_slot = query_index // seg_len
    key_slot = key_index // seg_len
    seg_range = jnp.arange(group_segs, dtype=jnp.int32)
    query_pick = (query_slot[:, None] == seg_range[None, :]).astype(jnp.float32)
    key_pick = (key_slot[:, None] == seg_range[None, :]).astype(jnp.float32)
    linked = (
        lax.dot_general(
            exact_dot(query_pick, allowed),
            key_pick,
            (((1,), (1,)), ((), ())),
            precision=lax.Precision.HIGHEST,
            preferred_element_type=jnp.float32,
        )
        > 0.5
    )
    return linked & (
        (query_slot[:, None] != key_slot[None, :]) | (key_index[None, :] <= query_index[:, None])
    )


def pair_terms(query_part, grad_part, stat_part, delta_part, key_part, value_part, visible):
    scores = (
        jnp.einsum("qhd,khd->qhk", query_part, key_part, preferred_element_type=jnp.float32) * 0.125
    )
    scores = jnp.where(visible[:, None, :], scores, masked_score)
    probs_full = jnp.exp(scores - stat_part[:, :, None])
    grad_probs = jnp.einsum(
        "qhd,khd->qhk", grad_part, value_part, preferred_element_type=jnp.float32
    )
    grad_scores = (probs_full * (grad_probs - delta_part[:, :, None])).astype(jnp.bfloat16)
    grad_query = None
    grad_key = None
    grad_value = None
    grad_query = (
        jnp.einsum("qhk,khd->qhd", grad_scores, key_part, preferred_element_type=jnp.float32)
        * 0.125
    )
    grad_key = (
        jnp.einsum("qhk,qhd->khd", grad_scores, query_part, preferred_element_type=jnp.float32)
        * 0.125
    )
    grad_value = jnp.einsum(
        "qhk,qhd->khd",
        probs_full.astype(jnp.bfloat16),
        grad_part,
        preferred_element_type=jnp.float32,
    )
    return (grad_query, grad_key, grad_value)


def shards(
    tokens,
    cotangent,
    qkv_weight,
    out_weight,
    up_weight,
    down_weight,
    gain_attn,
    gain_ffn,
    parents,
    slot_ids,
):
    local_rows = tokens.shape[0]
    model_width = tokens.shape[1]
    shard_count = lax.axis_size("shard")
    my_start = lax.axis_index("shard") * local_rows
    seg_len = local_rows * shard_count // slot_ids.shape[0]
    allowed = slot_table(slot_ids, parents)
    qkv_full, out_full, attn_gain = (
        lax.all_gather(qkv_weight.astype(jnp.bfloat16), "shard", axis=0, tiled=True),
        lax.all_gather(out_weight.astype(jnp.bfloat16), "shard", axis=0, tiled=True),
        lax.all_gather(gain_attn.astype(jnp.bfloat16), "shard", axis=0, tiled=True),
    )
    inputs = tokens.astype(jnp.float32)
    normed_one, inv_one = normalize(inputs)
    entered = (normed_one * attn_gain.astype(jnp.float32)).astype(jnp.bfloat16)
    qkv_all = jnp.dot(entered, qkv_full, preferred_element_type=jnp.float32).astype(jnp.bfloat16)
    queries = qkv_all[:, :model_width]
    keys_local = qkv_all[:, model_width : 2 * model_width]
    values_local = qkv_all[:, 2 * model_width :]
    query_heads = queries.reshape(local_rows, HEADS, HEAD)
    start_state = (
        jnp.full((local_rows, HEADS), masked_score, jnp.float32),
        jnp.zeros((local_rows, HEADS), jnp.float32),
        jnp.zeros((local_rows, HEADS, HEAD), jnp.float32),
    )
    carried = start_state
    key_piece = lax.all_gather(keys_local, "shard", axis=0, tiled=True)
    value_piece = lax.all_gather(values_local, "shard", axis=0, tiled=True)
    piece_rows = key_piece.shape[0]
    block_rows = block_size()
    count_blocks = piece_rows // block_rows
    key_blocks = key_piece.reshape(count_blocks, block_rows, HEADS, HEAD)
    value_blocks = value_piece.reshape(count_blocks, block_rows, HEADS, HEAD)

    def attend_block(running, blocks):
        key_block, value_block, block_index = blocks
        run_max, run_sum, run_acc = running
        visible = visible_mask(
            allowed, seg_len, my_start, local_rows, block_index * block_rows, block_rows
        )
        scores = (
            jnp.einsum("qhd,khd->qhk", query_heads, key_block, preferred_element_type=jnp.float32)
            * 0.125
        )
        scores = jnp.where(visible[:, None, :], scores, masked_score)
        new_max = jnp.maximum(run_max, jnp.max(scores, axis=2))
        rescale = jnp.exp(run_max - new_max)
        exp_scores = jnp.exp(scores - new_max[:, :, None])
        run_sum = run_sum * rescale + jnp.sum(exp_scores, axis=2)
        run_acc = run_acc * rescale[:, :, None] + jnp.einsum(
            "qhk,khd->qhd",
            exp_scores.astype(jnp.bfloat16),
            value_block,
            preferred_element_type=jnp.float32,
        )
        return ((new_max, run_sum, run_acc), None)

    carried, unused = lax.scan(
        attend_block, carried, (key_blocks, value_blocks, jnp.arange(count_blocks, dtype=jnp.int32))
    )
    run_max, run_sum, run_acc = carried
    attn_exact = run_acc / run_sum[:, :, None]
    log_sum = run_max + jnp.log(run_sum)
    attended = attn_exact.reshape(local_rows, model_width).astype(jnp.bfloat16)
    hidden = inputs + jnp.dot(attended, out_full, preferred_element_type=jnp.float32)
    up_full, down_full, ffn_gain = (
        lax.all_gather(up_weight.astype(jnp.bfloat16), "shard", axis=0, tiled=True),
        lax.all_gather(down_weight.astype(jnp.bfloat16), "shard", axis=0, tiled=True),
        lax.all_gather(gain_ffn.astype(jnp.bfloat16), "shard", axis=0, tiled=True),
    )
    normed_two, inv_two = normalize(hidden)
    second = (normed_two * ffn_gain.astype(jnp.float32)).astype(jnp.bfloat16)
    pre_act = jnp.dot(second, up_full, preferred_element_type=jnp.float32)
    active = gelu_exact(pre_act).astype(jnp.bfloat16)
    output = (hidden + jnp.dot(active, down_full, preferred_element_type=jnp.float32)).astype(
        jnp.bfloat16
    )
    up_full, down_full, ffn_gain = (
        lax.all_gather(up_weight.astype(jnp.bfloat16), "shard", axis=0, tiled=True),
        lax.all_gather(down_weight.astype(jnp.bfloat16), "shard", axis=0, tiled=True),
        lax.all_gather(gain_ffn.astype(jnp.bfloat16), "shard", axis=0, tiled=True),
    )
    qkv_full, out_full, attn_gain = (
        lax.all_gather(qkv_weight.astype(jnp.bfloat16), "shard", axis=0, tiled=True),
        lax.all_gather(out_weight.astype(jnp.bfloat16), "shard", axis=0, tiled=True),
        lax.all_gather(gain_attn.astype(jnp.bfloat16), "shard", axis=0, tiled=True),
    )
    grad_down = t_times(active, cotangent)
    grad_active = times_t(cotangent, down_full).astype(jnp.bfloat16)
    grad_pre = (grad_active.astype(jnp.float32) * gelu_slope(pre_act)).astype(jnp.bfloat16)
    grad_up = t_times(second, grad_pre)
    grad_second = times_t(grad_pre, up_full)
    grad_gain_ffn = jnp.sum(grad_second * normed_two, axis=0)
    grad_hidden = cotangent.astype(jnp.float32) + norm_back(
        grad_second * ffn_gain.astype(jnp.float32), normed_two, inv_two
    )
    grad_y = grad_hidden.astype(jnp.bfloat16)
    grad_out = t_times(attended, grad_y)
    grad_attn = times_t(grad_y, out_full).astype(jnp.bfloat16)
    grad_heads = grad_attn.reshape(local_rows, HEADS, HEAD)
    row_delta = jnp.sum(grad_heads.astype(jnp.float32) * attn_exact, axis=2)
    start_back = jnp.zeros((local_rows, HEADS, HEAD), jnp.float32)
    carried = start_back
    key_piece = lax.all_gather(keys_local, "shard", axis=0, tiled=True)
    value_piece = lax.all_gather(values_local, "shard", axis=0, tiled=True)
    piece_rows = key_piece.shape[0]
    back_block_rows = block_size()
    count_blocks = piece_rows // back_block_rows
    key_blocks = key_piece.reshape(count_blocks, back_block_rows, HEADS, HEAD)
    value_blocks = value_piece.reshape(count_blocks, back_block_rows, HEADS, HEAD)

    def back_block(running, blocks):
        grad_query = running
        key_block, value_block, block_index = blocks
        block_start = block_index * back_block_rows
        visible = visible_mask(allowed, seg_len, my_start, local_rows, block_start, back_block_rows)
        part_query, part_key, part_value = pair_terms(
            query_heads, grad_heads, log_sum, row_delta, key_block, value_block, visible
        )
        joined = jnp.concatenate(
            (
                part_key.reshape(back_block_rows, model_width),
                part_value.reshape(back_block_rows, model_width),
            ),
            axis=1,
        )
        return (grad_query + part_query, joined.astype(jnp.bfloat16))

    carried, key_terms = lax.scan(
        back_block, carried, (key_blocks, value_blocks, jnp.arange(count_blocks, dtype=jnp.int32))
    )
    grad_query = carried
    key_terms = key_terms.reshape(piece_rows, 2 * model_width)
    key_grads = lax.psum_scatter(key_terms, "shard", scatter_dimension=0, tiled=True)
    grad_qkv = jnp.concatenate(
        (grad_query.reshape(local_rows, model_width), key_grads), axis=1
    ).astype(jnp.bfloat16)
    grad_qkv_weight = t_times(entered, grad_qkv)
    grad_entered = times_t(grad_qkv, qkv_full)
    grad_gain_attn = jnp.sum(grad_entered * normed_one, axis=0)
    input_grad = grad_hidden + norm_back(
        grad_entered * attn_gain.astype(jnp.float32), normed_one, inv_one
    )
    group_sums = (
        lax.psum_scatter(grad_qkv_weight.astype(jnp.bfloat16), "shard", scatter_dimension=0, tiled=True),
        lax.psum_scatter(grad_out.astype(jnp.bfloat16), "shard", scatter_dimension=0, tiled=True),
        lax.psum_scatter(grad_up.astype(jnp.bfloat16), "shard", scatter_dimension=0, tiled=True),
        lax.psum_scatter(grad_down.astype(jnp.bfloat16), "shard", scatter_dimension=0, tiled=True),
        lax.psum_scatter(grad_gain_attn, "shard", scatter_dimension=0, tiled=True),
        lax.psum_scatter(grad_gain_ffn, "shard", scatter_dimension=0, tiled=True),
    )
    totals = (
        lax.psum(group_sums[0].astype(jnp.bfloat16), "rep").astype(jnp.float32),
        lax.psum(group_sums[1].astype(jnp.bfloat16), "rep").astype(jnp.float32),
        lax.psum(group_sums[2].astype(jnp.bfloat16), "rep").astype(jnp.float32),
        lax.psum(group_sums[3].astype(jnp.bfloat16), "rep").astype(jnp.float32),
        lax.psum(group_sums[4].astype(jnp.bfloat16), "rep").astype(jnp.float32),
        lax.psum(group_sums[5].astype(jnp.bfloat16), "rep").astype(jnp.float32),
    )
    return (output, input_grad, totals[0], totals[1], totals[2], totals[3], totals[4], totals[5])


MESH = pl.DeviceIdType.MESH


def ring_place(shard):
    return (1 - shard % 2) * (shard // 2) + (shard % 2) * (7 - shard // 2)


def ring_shard(place):
    upper = place // 4
    return (1 - upper) * 2 * place + upper * (15 - 2 * place)


def remote(source, target, sent, got, device):
    return pltpu.make_async_remote_copy(
        src_ref=source,
        dst_ref=target,
        send_sem=sent,
        recv_sem=got,
        device_id=device,
        device_id_type=MESH,
    )


def around(place, offset):
    return ring_shard(lax.rem(place + offset + 8, 8))


class Where:
    def __init__(self):
        self.rep = lax.axis_index("rep")
        self.me = lax.axis_index("shard")
        self.y = self.rep // 2
        self.core = self.rep % 2
        self.rep_y = (1 - self.y) * 2 + self.core
        self.rep_core = self.y * 2 + 1 - self.core
        self.rep_far = (1 - self.y) * 2 + 1 - self.core
        self.place = ring_place(self.me)
        self.right = around(self.place, 1)
        self.left = around(self.place, -1)

    def other(self, step):
        return lax.rem(self.me + step, 8)

    def back(self, step):
        return lax.rem(self.me + 8 - step, 8)

    def greet(self):
        barrier = pltpu.get_barrier_semaphore()
        for step in range(1, 8):
            pl.semaphore_signal(
                barrier, inc=1, device_id=(self.rep, self.other(step)), device_id_type=MESH
            )
        for rep in (self.rep_y, self.rep_core, self.rep_far):
            pl.semaphore_signal(barrier, inc=1, device_id=(rep, self.me), device_id_type=MESH)
        pl.semaphore_wait(barrier, 10)


def normed_rows(values):
    average = jnp.mean(values, axis=-1, keepdims=True)
    centered = values - average
    variance = jnp.mean(centered * centered, axis=-1, keepdims=True)
    inv_std = lax.rsqrt(variance + 1e-05)
    return (centered * inv_std, inv_std)


def gain_row(gains_ref, which):
    return jnp.concatenate(
        [gains_ref[s, which * 8 : which * 8 + 1, :] for s in range(8)], axis=1
    ).astype(jnp.float32)


def head_lanes(values, head):
    lane = lax.broadcasted_iota(jnp.int32, values.shape, 1)
    return jnp.where(lane // HEAD == head, values, jnp.zeros_like(values))


def tile_masks(block, parents_ref):
    key_row = lax.broadcasted_iota(jnp.int32, (256, 256), 0)
    query_row = lax.broadcasted_iota(jnp.int32, (256, 256), 1)
    own = key_row <= query_row
    if block < 5:
        return (own, None)
    own = own & (key_row // 128 == query_row // 128)
    if block == 5:
        return (own, None)
    parent = jnp.where(query_row < 128, parents_ref[2 * block], parents_ref[2 * block + 1])
    return (own, parent == 10 + key_row // 128)


def score_parts(block, keys_ref, queries, masks):
    own_mask, branch_mask = masks
    full = 256 * block if block < 5 else 1280
    spans = [(0, full, None)] if full else []
    if branch_mask is not None:
        spans.append((1280, 256, branch_mask))
    spans.append((256 * block, 256, own_mask))
    parts = []
    for first, rows, mask in spans:
        scores = times_t(keys_ref[pl.ds(first, rows), :], queries)
        if mask is not None:
            scores = jnp.where(mask, scores, masked_score)
        parts.append((first, rows, scores))
    return parts


def summed(*parts):
    total = parts[0].astype(jnp.float32)
    for part in parts[1:]:
        total = total + part.astype(jnp.float32)
    return total


BLOCK_ORDER = [4, 3, -3, 2, -2, 1, -1, 0]


def layer_kernel(
    ids_ref, parents_ref, tok_ref, cot_ref, gain_one_ref, gain_two_ref, qkv_w, out_w, up_w, down_w,
    layer_ref, in_ref, qkv_out, out_out, up_out, down_out, gain_out, ent_hbm,
    stage, gain_ref, wq_send, slices, gains_ref, tok_all, qkv_slots, qkv, side_t, tree_rows, slot_rows,
    mixed, logs, att, out_all, w_all, xch, acts, parts, gw, rr, rr_out, cr_out, yr_out,
    do_slots, dk, dv, gq_t, qs_core, qs_half, qs_recv, qs_y, fin_up, gp, gp_recv, gp_rep,
    load_s, small_s, small_r, slc_s, slc_r, tok_s, tok_r, o_s, o_r, oy_s, oy_r, oc_s, oc_r, w_s, w_r,
    keep_s, mix_s, mix_r, cot_s, cot_r, sec_s, sec_r, part_s, part_r, do_s, do_r,
    go_s, go_r, rs_s, rs_r, ro_s, ro_r, fin_s, fin_r, ge_s, ge_r, qs_s, qs_r, qr_s, qr_r,
    gp_s, gp_r, gr_s, gr_r,
):
    low, full = jnp.bfloat16, jnp.float32
    dq_t, gq_slots = mixed, qkv.reshape(8, 256, 384)
    at = Where()
    rep, me, y, core = at.rep, at.me, at.y, at.core
    ring_device = ((rep, at.right), (rep, at.left))
    over_y, over_core = (at.rep_y, me), (at.rep_core, me)
    places = []
    for seg in range(16):
        place = jnp.int32(0)
        for slot in range(1, 16):
            place = jnp.where(ids_ref[slot] == seg, slot, place)
        places.append(place)

    loads = [
        pltpu.make_async_copy(qkv_w.at[:, pl.ds(j * 1024, 1024)], stage.at[j], load_s.at[j])
        for j in range(3)
    ]
    loads.append(pltpu.make_async_copy(out_w, stage.at[3], load_s.at[3]))
    loads.append(
        pltpu.make_async_copy(down_w.at[pl.ds(rep * 128, 128), :], stage.at[5], load_s.at[4])
    )
    for s in range(8):
        columns = pl.ds(pl.multiple_of(s * 512 + rep * 128, 128), 128)
        loads.append(
            pltpu.make_async_copy(
                up_w.at[:, columns], stage.at[4, :, pl.ds(s * 128, 128)], load_s.at[5 + s]
            )
        )
    for copy in loads:
        copy.start()
    gain_ref[0:8, :] = jnp.broadcast_to(gain_one_ref[...], (8, 128)).astype(low)
    gain_ref[8:16, :] = jnp.broadcast_to(gain_two_ref[...], (8, 128)).astype(low)
    at.greet()

    def flow_block(flow, offset):
        return around(at.place, -offset if flow else offset)

    def token_copy(flow, step, half):
        origin = flow_block(flow, -step)
        source = tok_ref if step == 0 else tok_all.at[origin]
        rows = pl.ds(half * 128, 128)
        return remote(
            source.at[rows, :],
            tok_all.at[origin, rows, :],
            tok_s.at[flow, step, half],
            tok_r.at[flow, step, half],
            ring_device[flow],
        )

    def step_halves(step):
        if step == 3:
            return [(0, 0), (1, 1)]
        return [(half, flow) for half in range(2) for flow in range(2)]

    def out_copy(flow, step):
        spot = out_all.at[flow_block(flow, -step), rep]
        return remote(spot, spot, o_s.at[flow, step], o_r.at[flow, step], ring_device[flow])

    def out_flows(step):
        return (0, 1) if step < 3 else (0,)

    def out_over_y(flow, step):
        spot = out_all.at[flow_block(flow, -step - 1), rep]
        return remote(spot, spot, oy_s.at[flow, step], oy_r.at[flow, step], over_y)

    def out_over_core(flow, step, own):
        spot = out_all.at[flow_block(flow, -step - 1), rep if own else at.rep_y]
        return remote(spot, spot, oc_s.at[own, flow, step], oc_r.at[own, flow, step], over_core)

    def w_copy(flow, step, half):
        spot = w_all.at[flow_block(flow, -step), half]
        return remote(spot, spot, w_s.at[flow, step, half], w_r.at[flow, step, half], ring_device[flow])

    def w_step(step):
        for half, flow in step_halves(step):
            w_copy(flow, step, half).wait_recv()
            if step < 2 or (step == 2 and half == flow):
                w_copy(flow, step + 1, half).start()

    small = [
        remote(
            gain_ref,
            gains_ref.at[me],
            small_s.at[0, step],
            small_r.at[0, step],
            (rep, at.other(step)),
        )
        for step in range(1, 8)
    ]
    small += [
        remote(
            wq_send.at[at.other(step), :, core],
            slices.at[me, :, core],
            small_s.at[1, step],
            small_r.at[1, step],
            (rep, at.other(step)),
        )
        for step in range(1, 8)
    ]
    slice_core = remote(
        slices.at[:, :, core], slices.at[:, :, core], slc_s.at[0], slc_r.at[0], over_core
    )
    cot_y = remote(cot_ref, xch.at[6], cot_s.at[0], cot_r.at[0], over_y)
    cot_core = remote(cot_ref, xch.at[5], cot_s.at[1], cot_r.at[1], over_core)
    cot_far = remote(xch.at[6], xch.at[7], cot_s.at[2], cot_r.at[2], over_core)

    for copy in small[:7]:
        copy.start()
    for half in range(2):
        for flow in range(2):
            token_copy(flow, 0, half).start()
    cot_y.start()
    cot_core.start()
    for copy in loads[:3]:
        copy.wait()
    for s in range(8):
        for j in range(3):
            wq_send[s, :, :, :, j * 128 : j * 128 + 128] = (
                stage[j, :, s * 128 : s * 128 + 128].astype(low).reshape(2, 2, 32, 128)
            )
    for copy in small[7:]:
        copy.start()
    gains_ref[me] = gain_ref[...]
    slices[me, :, core] = wq_send[me, :, core]
    loads[3].wait()
    out_all[me] = stage[3].astype(low).reshape(4, 32, 1024)
    for flow in range(2):
        out_copy(flow, 0).start()
    for copy in loads[4:]:
        copy.wait()
    w_all[me, 0] = stage[4].astype(low)
    w_all[me, 1] = stage[5].astype(low)
    xch[4] = cot_ref[...]
    for copy in small:
        copy.wait_recv()
    slice_core.start()
    slice_core.wait_recv()
    gain = gain_row(gains_ref, 0)

    kept = {}

    def enter(rows, origin, count):
        slot = 4 + count % 2
        if count > 1:
            kept[count - 2].wait()
        normed, _ = normed_rows(rows.astype(full))
        entered = (normed * gain).astype(low)
        parts[slot] = entered
        kept[count] = pltpu.make_async_copy(parts.at[slot], ent_hbm.at[origin], keep_s.at[slot - 4])
        kept[count].start()
        weights = slices[...].reshape(1024, 384)
        made = jnp.dot(entered, weights, preferred_element_type=full).astype(low)
        qkv_slots[2 * origin] = made[:128]
        qkv_slots[2 * origin + 1] = made[128:]

    enter(tok_ref[...], me, 0)
    count = 1
    for step in range(4):
        for half, flow in step_halves(step):
            token_copy(flow, step, half).wait_recv()
            if step < 2 or (step == 2 and half == flow):
                token_copy(flow, step + 1, half).start()
        for flow in out_flows(step):
            out_copy(flow, step).wait_recv()
            if step < 2 or (step == 2 and flow == 0):
                out_copy(flow, step + 1).start()
            out_over_y(flow, step).start()
            out_over_core(flow, step, 1).start()
        if step == W_START:
            for half in range(2):
                for flow in range(2):
                    w_copy(flow, 0, half).start()
        for flow in out_flows(step):
            origin = flow_block(flow, -step - 1)
            enter(tok_all[origin], origin, count)
            count += 1
    cot_y.wait_recv()
    cot_far.start()
    kept[6].wait()
    kept[7].wait()

    for seg in range(16):
        qkv[seg * 128 : seg * 128 + 128, :] = qkv_slots[places[seg]]
    for block in range(8):
        side_t[:, block * 256 : block * 256 + 256] = qkv[block * 256 : block * 256 + 256, 256:384].T

    for block in range(8):
        masks = tile_masks(block, parents_ref)
        rows = pl.ds(block * 256, 256)

        def one_head(head, unused):
            queries = head_lanes(qkv[rows, 0:128], head) * low(0.125)
            tiles = score_parts(block, qkv.at[:, pl.ds(128, 128)], queries, masks)
            top = None
            for _, _, scores in tiles:
                part = jnp.max(scores, axis=0, keepdims=True)
                top = part if top is None else jnp.maximum(top, part)
            total = None
            mix = None
            head_rows = pl.ds(pl.multiple_of(head * HEAD, HEAD), HEAD)
            for first, number, scores in tiles:
                weights = jnp.exp(scores - top)
                part = jnp.sum(weights, axis=0, keepdims=True)
                total = part if total is None else total + part
                term = jnp.dot(
                    side_t[head_rows, pl.ds(first, number)],
                    weights.astype(low),
                    preferred_element_type=full,
                )
                mix = term if mix is None else mix + term
            mixed[head_rows, block * 256 : block * 256 + 256] = mix / total
            logs[pl.ds(pl.multiple_of(head * 8, 8), 8), block * 256 : block * 256 + 256] = (
                jnp.broadcast_to(top + jnp.log(total), (8, 256))
            )
            return unused

        lax.fori_loop(0, 2, one_head, 0)
        tree = mixed[:, block * 256 : block * 256 + 256].T.astype(low)
        tree_rows[2 * block] = tree[:128]
        tree_rows[2 * block + 1] = tree[128:]
        if block in W_BLOCKS:
            w_step(W_BLOCKS.index(block))

    for slot in range(16):
        slot_rows[slot // 2, (slot % 2) * 128 : (slot % 2) * 128 + 128, :] = tree_rows[
            ids_ref[slot]
        ]
    my_columns = pl.ds(pl.multiple_of(me * 128, 128), 128)
    mix_sends = [
        remote(
            slot_rows.at[at.other(step)],
            att.at[:, my_columns],
            mix_s.at[step],
            mix_r.at[step],
            (rep, at.other(step)),
        )
        for step in range(1, 8)
    ]
    for copy in mix_sends:
        copy.start()
    att[:, my_columns] = slot_rows[me]
    for step in range(4):
        for flow in out_flows(step):
            out_over_y(flow, step).wait_recv()
            out_over_core(flow, step, 0).start()
    for step in range(4):
        for flow in out_flows(step):
            out_over_core(flow, step, 1).wait_recv()
            out_over_core(flow, step, 0).wait_recv()
    for copy in mix_sends:
        copy.wait_recv()
    w_step(1)

    out_full = out_all[...].reshape(1024, 1024)
    hidden = tok_ref[...].astype(full) + jnp.dot(att[...], out_full, preferred_element_type=full)
    ffn_gain = gain_row(gains_ref, 1)
    normed_two, _ = normed_rows(hidden)
    xch[0] = (normed_two * ffn_gain).astype(low)
    sec_y = remote(xch.at[0], xch.at[2], sec_s.at[0], sec_r.at[0], over_y)
    sec_core = remote(xch.at[0], xch.at[1], sec_s.at[1], sec_r.at[1], over_core)
    sec_far = remote(xch.at[2], xch.at[3], sec_s.at[2], sec_r.at[2], over_core)
    sec_y.start()
    sec_core.start()
    stage[0] = hidden[:128]
    stage[1] = hidden[128:]
    for step in range(4):
        for half, flow in step_halves(step):
            token_copy(flow, step, half).wait_send()
    w_step(2)
    sec_y.wait_recv()
    sec_far.start()
    cot_core.wait_recv()
    cot_far.wait_recv()
    w_step(3)

    up = w_all[:, 0].reshape(1024, 1024)
    down = w_all[:, 1].reshape(1024, 1024)

    def ffn(first):
        second = xch[first : first + 2].reshape(512, 1024)
        cots = xch[4 + first : 6 + first].reshape(512, 1024)
        pre = jnp.dot(second, up, preferred_element_type=full)
        bell = 1.0 + lax.erf(pre * 0.7071067811865476)
        acts[first : first + 2] = (0.5 * pre * bell).astype(low).reshape(2, 2, 128, 1024)
        slope = 0.5 * bell + pre * jnp.exp(-0.5 * pre * pre) * 0.3989422804014327
        grad_act = times_t(cots, down).astype(low).astype(full)
        grad_pre = (grad_act * slope).astype(low)
        acts[4 + first : 6 + first] = grad_pre.reshape(2, 2, 128, 1024)
        return times_t(grad_pre, up)

    def part_copy(kind, leg):
        index = kind * 3 + leg
        return remote(
            tok_all.at[index],
            parts.at[index],
            part_s.at[index],
            part_r.at[index],
            over_y if leg == 1 else over_core,
        )

    sec_core.wait_recv()
    sec_far.wait_recv()
    grad_far = ffn(2)
    tok_all[0] = grad_far[256:].astype(low)
    part_copy(0, 0).start()
    stage[2] = grad_far[:128]
    stage[3] = grad_far[128:256]
    part_copy(0, 0).wait_recv()
    tok_all[1] = summed(stage[2:4].reshape(256, 1024), parts[0]).astype(low)
    part_copy(0, 1).start()
    grad_near = ffn(0)
    tok_all[2] = grad_near[256:].astype(low)
    part_copy(0, 2).start()
    stage[2] = grad_near[:128]
    stage[3] = grad_near[128:256]

    def w_grads(offsets):
        blocks = [around(at.place, offset) for offset in offsets]
        spans = [pl.ds(pl.multiple_of(block * 128, 128), 128) for block in blocks]
        lefts = [xch[0:4, :, span].reshape(1024, 128).T for span in spans]
        rights = [acts[0:4, :, :, span].reshape(1024, 128).T for span in spans]
        for half, (sides, other) in enumerate(((lefts, acts), (rights, xch))):
            made = jnp.dot(
                jnp.concatenate(sides, axis=0),
                other[4:8].reshape(1024, 1024),
                preferred_element_type=full,
            ).astype(low)
            for i, block in enumerate(blocks):
                gw[block, half] = made[i * 128 : i * 128 + 128]

    def rs_copy(flow, step, half):
        return remote(
            gw.at[flow_block(flow, 4 - step), half],
            rr.at[flow, step, half],
            rs_s.at[flow, step, half],
            rs_r.at[flow, step, half],
            ring_device[flow],
        )

    def rs_step(step):
        for flow in range(2):
            block = flow_block(flow, 4 - step)
            for half in range(2):
                if step == 0 and half != flow:
                    continue
                if step > 1 or (step == 1 and half == flow):
                    rs_copy(flow, step - 1, half).wait_recv()
                    gw[block, half] = summed(gw[block, half], rr[flow, step - 1, half]).astype(low)
                rs_copy(flow, step, half).start()

    w_grads([4, 3, -3])
    rs_step(0)

    def outputs(first):
        active = acts[first : first + 2].reshape(512, 1024)
        return jnp.dot(active, down, preferred_element_type=full)

    made = outputs(2)
    tok_all[3] = made[256:].astype(low)
    part_copy(1, 0).start()
    stage[4] = made[:128]
    stage[5] = made[128:256]
    part_copy(1, 0).wait_recv()
    tok_all[4] = summed(stage[4:6].reshape(256, 1024), parts[3]).astype(low)
    made = outputs(0)
    tok_all[5] = made[256:].astype(low)
    part_copy(1, 2).start()
    stage[0] = stage[0] + made[:128]
    stage[1] = stage[1] + made[128:256]
    part_copy(1, 1).start()

    for step in range(4):
        for half, flow in step_halves(step):
            w_copy(flow, step, half).wait_send()

    part_copy(0, 2).wait_recv()
    part_copy(0, 1).wait_recv()
    grad_second = summed(stage[2:4].reshape(256, 1024), parts[1], parts[2])
    hidden = tok_ref[...].astype(full) + jnp.dot(
        att[...], out_all[...].reshape(1024, 1024), preferred_element_type=full
    )
    normed_two, inv_two = normed_rows(hidden)
    gain_two = jnp.sum(grad_second * normed_two, axis=0, keepdims=True)
    for s in range(8):
        gp[s, 8:16, :] = jnp.broadcast_to(gain_two[:, s * 128 : s * 128 + 128], (8, 128))
    grad_hidden = cot_ref[...].astype(full) + norm_back(
        grad_second * gain_row(gains_ref, 1), normed_two, inv_two
    )
    stage[2] = grad_hidden[:128]
    stage[3] = grad_hidden[128:]
    grad_y = grad_hidden.astype(low)
    grad_attn = times_t(grad_y, out_all[...].reshape(1024, 1024)).astype(low)
    for copy in mix_sends:
        copy.wait_send()
    for s in range(8):
        slot_rows[s] = grad_attn[:, s * 128 : s * 128 + 128]
    do_sends = [
        remote(
            slot_rows.at[at.other(step)],
            do_slots.at[me],
            do_s.at[step],
            do_r.at[step],
            (rep, at.other(step)),
        )
        for step in range(1, 8)
    ]
    for copy in do_sends:
        copy.start()
    do_slots[me] = slot_rows[me]

    rs_step(1)
    w_grads([2, -2, 1, -1, 0])

    for step in range(4):
        for flow in out_flows(step):
            out_copy(flow, step).wait_send()
            out_over_y(flow, step).wait_send()
            out_over_core(flow, step, 0).wait_send()
            out_over_core(flow, step, 1).wait_send()
    for block in range(8):
        out_all[block] = (
            jnp.dot(
                att[:, block * 128 : block * 128 + 128].T, grad_y, preferred_element_type=full
            )
            .astype(low)
            .reshape(4, 32, 1024)
        )
    outs = out_all
    go_core = [
        remote(
            outs.at[:, 2 * i + 1 - core], cr_out.at[:, i], go_s.at[i], go_r.at[i], over_core
        )
        for i in range(2)
    ]
    for copy in go_core:
        copy.start()
    for copy in (cot_y, cot_core, cot_far, sec_y, sec_core, sec_far):
        copy.wait_send()
    fetch = pltpu.make_async_copy(ent_hbm, xch, load_s.at[0])
    fetch.start()
    for copy in go_core:
        copy.wait_recv()
    outs[:, at.rep_y] = summed(outs[:, at.rep_y], cr_out[:, 1 - y]).astype(low)
    go_y = remote(outs.at[:, at.rep_y], yr_out, go_s.at[2], go_r.at[2], over_y)
    go_y.start()

    def ro_copy(flow, step):
        return remote(
            outs.at[flow_block(flow, 4 - step), rep],
            rr_out.at[flow, step],
            ro_s.at[flow, step],
            ro_r.at[flow, step],
            ring_device[flow],
        )

    def ro_flows(step):
        return (0, 1) if step else (0,)

    def ro_step(step):
        for flow in ro_flows(step):
            block = flow_block(flow, 4 - step)
            if step > 0 and flow in ro_flows(step - 1):
                ro_copy(flow, step - 1).wait_recv()
                outs[block, rep] = summed(outs[block, rep], rr_out[flow, step - 1]).astype(low)
            ro_copy(flow, step).start()

    for copy in do_sends:
        copy.wait_recv()
    for seg in range(16):
        tree_rows[seg] = do_slots.reshape(16, 128, 128)[places[seg]]
    for block in range(8):
        side_t[:, block * 256 : block * 256 + 256] = qkv[block * 256 : block * 256 + 256, 128:256].T
    dk[...] = jnp.zeros_like(dk)
    dv[...] = jnp.zeros_like(dv)

    for block in range(8):
        masks = tile_masks(block, parents_ref)
        rows = pl.ds(block * 256, 256)

        def one_head_back(head, unused):
            head_rows = pl.ds(pl.multiple_of(head * HEAD, HEAD), HEAD)
            queries = head_lanes(qkv[rows, 0:128], head) * low(0.125)
            grads = tree_rows[2 * block : 2 * block + 2].reshape(256, 128)
            grad_rows = head_lanes(grads, head)
            lse = logs[pl.ds(pl.multiple_of(head * 8, 8), 8), block * 256 : block * 256 + 256][0:1]
            both = grads.T.astype(full) * mixed[:, block * 256 : block * 256 + 256]
            delta = jnp.where(
                head == 0,
                jnp.sum(both[:HEAD], axis=0, keepdims=True),
                jnp.sum(both[HEAD:], axis=0, keepdims=True),
            )
            grad_query = None
            for first, number, scores in score_parts(
                block, qkv.at[:, pl.ds(128, 128)], queries, masks
            ):
                keys = pl.ds(first, number)
                weights = jnp.exp(scores - lse)
                grad_weights = times_t(qkv[keys, 256:384], grad_rows)
                grad_scores = (weights * (grad_weights - delta)).astype(low)
                dk[keys, :] += jnp.dot(grad_scores, queries, preferred_element_type=full)
                dv[keys, :] += jnp.dot(weights.astype(low), grad_rows, preferred_element_type=full)
                term = jnp.dot(side_t[head_rows, keys], grad_scores, preferred_element_type=full)
                grad_query = term if grad_query is None else grad_query + term
            dq_t[head_rows, block * 256 : block * 256 + 256] = grad_query * 0.125
            return unused

        lax.fori_loop(0, 2, one_head_back, 0)
        if block == 1:
            rs_step(2)
        if block == 5:
            rs_step(3)
        if block == 4:
            outs[:, rep] = summed(outs[:, rep], cr_out[:, y]).astype(low)
            go_y.wait_recv()
            outs[:, rep] = summed(outs[:, rep], yr_out[...]).astype(low)
            ro_step(0)
        if block == 6:
            ro_step(1)

    for seg in range(16):
        rows = pl.ds(seg * 128, 128)
        qkv_slots[seg, :, 0:128] = dq_t[:, seg * 128 : seg * 128 + 128].T.astype(low)
        qkv_slots[seg, :, 128:256] = dk[rows, :].astype(low)
        qkv_slots[seg, :, 256:384] = dv[rows, :].astype(low)
    for slot in range(16):
        gq_slots[slot // 2, (slot % 2) * 128 : (slot % 2) * 128 + 128, :] = qkv_slots[ids_ref[slot]]

    def ge_copy(flow, step):
        source, target = acts.at[flow * 4 + step], w_all.at[flow * 4 + step]
        if step == 0:
            source, target = source.at[flow], target.at[flow]
        return remote(
            source, target, ge_s.at[flow, step], ge_r.at[flow, step], ring_device[flow]
        )

    def ge_part(block):
        return times_t(gq_slots[block], slices[...].reshape(1024, 384))

    def ge_step(step):
        for flow in range(2):
            part = ge_part(flow_block(flow, 4 - step))
            if step > 0:
                ge_copy(flow, step - 1).wait_recv()
            for half in range(2):
                if step == 0 and half != flow:
                    continue
                rows = part[half * 128 : half * 128 + 128]
                if step > 1 or (step == 1 and half == flow):
                    rows = rows + w_all[flow * 4 + step - 1, half].astype(full)
                acts[flow * 4 + step, half] = rows.astype(low)
            ge_copy(flow, step).start()

    ge_step(0)
    ro_step(2)
    for block in range(8):
        gq_t[:, block * 256 : block * 256 + 256] = gq_slots[block].T
    fetch.wait()
    for copy in small:
        copy.wait_send()
    for s in range(8):
        made = jnp.dot(
            gq_t[...],
            xch[:, :, s * 128 : s * 128 + 128].reshape(2048, 128),
            preferred_element_type=full,
        )
        wq_send[s] = made.T.astype(low).reshape(2, 2, 32, 384)
    qs_over_core = remote(wq_send.at[:, :, 1 - core], qs_core, qr_s.at[0], qr_r.at[0], over_core)
    qs_over_core.start()
    ge_step(1)
    qs_over_core.wait_recv()
    qs_half[...] = summed(wq_send[:, :, core], qs_core[...]).astype(low)
    qs_sends = [
        remote(
            qs_half.at[at.other(step)],
            qs_recv.at[me],
            qs_s.at[step],
            qs_r.at[step],
            (rep, at.other(step)),
        )
        for step in range(1, 8)
    ]
    for copy in qs_sends:
        copy.start()
    qs_recv[me] = qs_half[me]

    def final_copy(kind, leg):
        quarter = at.rep_y if leg == 2 else rep
        if kind == 0:
            spot = fin_up.at[quarter]
        elif kind == 1:
            spot = down_out.at[pl.ds(quarter * 128, 128), :]
        elif kind == 2:
            spot = out_out.at[pl.ds(quarter * 32, 32), :]
        else:
            spot = qkv_out.at[pl.ds(quarter * 32, 32), :]
        device = over_y if leg == 0 else over_core
        return remote(spot, spot, fin_s.at[kind, leg], fin_r.at[kind, leg], device)

    ro_step(3)
    ge_step(2)
    for half in range(2):
        for flow in range(2):
            rs_copy(flow, 3, half).wait_recv()
        total = summed(gw[me, half], rr[0, 3, half], rr[1, 3, half]).astype(low)
        if half == 0:
            fin_up[rep] = total
        else:
            down_out[pl.ds(rep * 128, 128), :] = total
        final_copy(half, 0).start()
        final_copy(half, 1).start()
    for copy in qs_sends:
        copy.wait_recv()
    qs_over_y = remote(qs_recv.at[:, 1 - y], qs_y, qr_s.at[1], qr_r.at[1], over_y)
    qs_over_y.start()
    for flow in range(2):
        ro_copy(flow, 3).wait_recv()
    out_out[pl.ds(rep * 32, 32), :] = summed(outs[me, rep], rr_out[0, 3], rr_out[1, 3]).astype(low)
    final_copy(2, 0).start()
    final_copy(2, 1).start()
    ge_step(3)
    part_copy(1, 1).wait_recv()
    part_copy(1, 2).wait_recv()
    tok_all[6] = summed(stage[0:2].reshape(256, 1024), parts[4], parts[5]).astype(low)
    layer_write = pltpu.make_async_copy(tok_all.at[6], layer_ref, load_s.at[1])
    layer_write.start()
    qs_over_y.wait_recv()
    quarter_rows = pl.ds(rep * 32, 32)
    for s in range(8):
        total = summed(qs_recv[s, y], qs_y[s]).astype(low)
        for j in range(3):
            first = j * 1024 + s * 128
            qkv_out[quarter_rows, first : first + 128] = total[:, j * 128 : j * 128 + 128]
    final_copy(3, 0).start()
    final_copy(3, 1).start()
    for kind in range(4):
        final_copy(kind, 0).wait_recv()
        final_copy(kind, 2).start()

    grad_entered = ge_part(me)
    for flow in range(2):
        ge_copy(flow, 3).wait_recv()
        grad_entered = grad_entered + w_all[flow * 4 + 3].reshape(256, 1024).astype(full)
    normed, inv_std = normed_rows(tok_ref[...].astype(full))
    gain_one = jnp.sum(grad_entered * normed, axis=0, keepdims=True)
    for s in range(8):
        gp[s, 0:8, :] = jnp.broadcast_to(gain_one[:, s * 128 : s * 128 + 128], (8, 128))
    gain_sends = [
        remote(
            gp.at[at.other(step)],
            gp_recv.at[me],
            gp_s.at[step],
            gp_r.at[step],
            (rep, at.other(step)),
        )
        for step in range(1, 8)
    ]
    for copy in gain_sends:
        copy.start()
    gp_recv[me] = gp[me]
    in_grad = stage[2:4].reshape(256, 1024) + norm_back(
        grad_entered * gain_row(gains_ref, 0), normed, inv_std
    )
    stage[4] = in_grad[:128]
    stage[5] = in_grad[128:]
    in_write = pltpu.make_async_copy(stage.at[4:6], in_ref, load_s.at[2])
    in_write.start()
    for copy in gain_sends:
        copy.wait_recv()
    total = gp_recv[0]
    for s in range(1, 8):
        total = total + gp_recv[s]
    gp_rep[rep] = total
    rep_sends = [
        remote(gp_rep.at[rep], gp_rep.at[rep], gr_s.at[i], gr_r.at[i], (to, me))
        for i, to in enumerate((at.rep_y, at.rep_core, at.rep_far))
    ]
    for copy in rep_sends:
        copy.start()
    for kind in range(4):
        final_copy(kind, 1).wait_recv()
        final_copy(kind, 2).wait_recv()
    for quarter in range(4):
        for s in range(8):
            first = s * 512 + quarter * 128
            up_out[:, first : first + 128] = fin_up[quarter, :, s * 128 : s * 128 + 128]
    for copy in rep_sends:
        copy.wait()
    gain_out[...] = gp_rep[0] + gp_rep[1] + gp_rep[2] + gp_rep[3]

    layer_write.wait()
    in_write.wait()
    for kind in range(4):
        for leg in range(3):
            final_copy(kind, leg).wait_send()
    qs_over_y.wait_send()
    qs_over_core.wait_send()
    go_y.wait_send()
    for copy in go_core + qs_sends + gain_sends + do_sends:
        copy.wait_send()
    slice_core.wait_send()
    for kind in range(2):
        for leg in range(3):
            part_copy(kind, leg).wait_send()
    for step in range(4):
        for flow in range(2):
            ge_copy(flow, step).wait_send()
            for half in range(2):
                if step > 0 or half == flow:
                    rs_copy(flow, step, half).wait_send()
        for flow in ro_flows(step):
            ro_copy(flow, step).wait_send()


def widen_kernel(*refs):
    for source, target in zip(refs[:6], refs[7:13]):
        target[...] = source[...].astype(target.dtype)
    refs[13][...] = refs[6][0:1, :]
    refs[14][...] = refs[6][8:9, :]


W_START = 2
W_BLOCKS = [2]


def fast_shards(
    tokens, cotangent, qkv_weight, out_weight, up_weight, down_weight, gain_attn, gain_ffn, parents, slot_ids
):
    low, full = jnp.bfloat16, jnp.float32
    smem = pl.BlockSpec(memory_space=pltpu.SMEM)
    vmem = pl.BlockSpec(memory_space=pltpu.VMEM)
    anywhere = pl.BlockSpec(memory_space=pl.ANY)

    def dma(*shape):
        return pltpu.SemaphoreType.DMA(shape)

    v = pltpu.VMEM
    scratch = [
        v((6, 128, 1024), full),
        v((16, 128), low),
        v((8, 2, 2, 32, 384), low),
        v((8, 2, 2, 32, 384), low),
        v((8, 16, 128), low),
        v((8, 256, 1024), low),
        v((16, 128, 384), low),
        v((2048, 384), low),
        v((128, 2048), low),
        v((16, 128, 128), low),
        v((8, 256, 128), low),
        v((128, 2048), full),
        v((16, 2048), full),
        v((256, 1024), low),
        v((8, 4, 32, 1024), low),
        v((8, 2, 128, 1024), low),
        v((8, 256, 1024), low),
        v((8, 2, 128, 1024), low),
        v((6, 256, 1024), low),
        v((8, 2, 128, 1024), low),
        v((2, 4, 2, 128, 1024), low),
        v((2, 4, 32, 1024), low),
        v((8, 2, 32, 1024), low),
        v((8, 32, 1024), low),
        v((8, 256, 128), low),
        v((2048, 128), full),
        v((2048, 128), full),
        v((384, 2048), low),
        v((8, 2, 32, 384), low),
        v((8, 2, 32, 384), low),
        v((8, 2, 32, 384), low),
        v((8, 32, 384), low),
        v((4, 128, 1024), low),
        v((8, 16, 128), full),
        v((8, 16, 128), full),
        v((4, 16, 128), full),
        dma(13), dma(2, 8), dma(2, 8), dma(1), dma(1), dma(2, 4, 2), dma(2, 4, 2),
        dma(2, 4), dma(2, 4), dma(2, 4), dma(2, 4), dma(2, 2, 4), dma(2, 2, 4),
        dma(2, 4, 2), dma(2, 4, 2), dma(2), dma(8), dma(8), dma(3), dma(3), dma(3), dma(3),
        dma(6), dma(6), dma(8), dma(8), dma(3), dma(3), dma(2, 4, 2), dma(2, 4, 2),
        dma(2, 4), dma(2, 4), dma(4, 3), dma(4, 3), dma(2, 4), dma(2, 4), dma(8), dma(8),
        dma(2), dma(2), dma(8), dma(8), dma(3), dma(3),
    ]
    made = pl.pallas_call(
        layer_kernel,
        out_shape=[
            jax.ShapeDtypeStruct((256, 1024), low),
            jax.ShapeDtypeStruct((2, 128, 1024), full),
            jax.ShapeDtypeStruct((128, 3072), low),
            jax.ShapeDtypeStruct((128, 1024), low),
            jax.ShapeDtypeStruct((128, 4096), low),
            jax.ShapeDtypeStruct((512, 1024), low),
            jax.ShapeDtypeStruct((16, 128), full),
            jax.ShapeDtypeStruct((8, 256, 1024), low),
        ],
        in_specs=[smem] * 2 + [vmem] * 4 + [anywhere] * 4,
        out_specs=[anywhere] * 2 + [vmem] * 5 + [anywhere],
        scratch_shapes=scratch,
        compiler_params=pltpu.CompilerParams(
            collective_id=1, has_side_effects=True, vmem_limit_bytes=VMEM_LIMIT
        ),
    )(
        slot_ids, parents.reshape(16), tokens, cotangent, gain_attn.reshape(1, 128), gain_ffn.reshape(1, 128), qkv_weight, out_weight, up_weight,
        down_weight,
    )
    shapes = [(256, 1024), (256, 1024), (128, 3072), (128, 1024), (128, 4096), (512, 1024)]
    results = [made[0], made[1].reshape(256, 1024)] + list(made[2:7])

    def spec(shape):
        return pl.BlockSpec((shape[0] // 4, shape[1]), lambda i: (i, 0))

    gain_spec = pl.BlockSpec((1, 128), lambda i: (0, 0))
    last = pl.pallas_call(
        widen_kernel,
        grid=(4,),
        out_shape=[jax.ShapeDtypeStruct(shapes[0], low)]
        + [jax.ShapeDtypeStruct(shape, full) for shape in shapes[1:]]
        + [jax.ShapeDtypeStruct((1, 128), full)] * 2,
        in_specs=[spec(shape) for shape in shapes] + [pl.BlockSpec((16, 128), lambda i: (0, 0))],
        out_specs=[spec(shape) for shape in shapes] + [gain_spec] * 2,
    )(*results)
    return tuple(last[:6]) + (last[6].reshape(128), last[7].reshape(128))


VMEM_LIMIT = 61 * 2**20


def solution(mesh):
    in_specs = (
        P(("rep", "shard"), None),
        P(("rep", "shard"), None),
        P("shard", None),
        P("shard", None),
        P("shard", None),
        P("shard", None),
        P("shard"),
        P("shard"),
        P("rep", None),
        P("rep"),
    )
    out_specs = (
        P(("rep", "shard"), None),
        P(("rep", "shard"), None),
        P("shard", None),
        P("shard", None),
        P("shard", None),
        P("shard", None),
        P("shard"),
        P("shard"),
    )

    def fits(*args):
        shapes = [a.shape for a in args]
        return shapes[0] == (8192, 1024) and shapes[4] == (1024, 4096) and shapes[8] == (4, 16)

    small = mesh.shape["rep"] == 4 and mesh.shape["shard"] == 8

    def whole(*args):
        run = fast_shards if small and fits(*args) else shards
        return jax.shard_map(
            run, mesh=mesh, in_specs=in_specs, out_specs=out_specs, check_vma=False
        )(*args)

    return whole
```

```python
import jax
import jax.numpy as jnp
from jax import lax
from jax.experimental import pallas as pl
from jax.experimental.pallas import tpu as pltpu
from jax.sharding import PartitionSpec as P

HEADS = 16
HEAD = 64


masked_score = -1e30


def block_size():
    return 512


def normalize(values):
    average = jnp.mean(values, axis=-1, keepdims=True)
    centered = values - average
    variance = jnp.mean(centered * centered, axis=-1, keepdims=True)
    inv_std = lax.rsqrt(variance + 1e-05)
    return (centered * inv_std, inv_std)


def gelu_exact(values):
    return 0.5 * values * (1.0 + lax.erf(values * 0.7071067811865476))


def gelu_slope(values):
    return (
        0.5 * (1.0 + lax.erf(values * 0.7071067811865476))
        + values * jnp.exp(-0.5 * values * values) * 0.3989422804014327
    )


def norm_back(grad_normed, normed, inv_std):
    first_mean = jnp.mean(grad_normed, axis=-1, keepdims=True)
    second_mean = jnp.mean(grad_normed * normed, axis=-1, keepdims=True)
    return inv_std * (grad_normed - first_mean - normed * second_mean)


def times_t(left_side, right_side):
    return lax.dot_general(
        left_side, right_side, (((1,), (1,)), ((), ())), preferred_element_type=jnp.float32
    )


def t_times(left_side, right_side):
    return lax.dot_general(
        left_side, right_side, (((0,), (0,)), ((), ())), preferred_element_type=jnp.float32
    )


def exact_dot(left_side, right_side):
    return jnp.dot(
        left_side, right_side, precision=lax.Precision.HIGHEST, preferred_element_type=jnp.float32
    )


def slot_table(group_ids, parents):
    tree_segs = parents.shape[1]
    group_segs = group_ids.shape[0]
    seg_range = jnp.arange(tree_segs, dtype=jnp.int32)
    walker = seg_range[None, :]
    reached = walker[:, :, None] == seg_range[None, None, :]

    def climb(step_index, carried):
        walker_now, reached_now = carried
        walker_now = jnp.sum(
            jnp.where(walker_now[:, :, None] == seg_range[None, None, :], parents[:, None, :], 0),
            axis=2,
        )
        return (walker_now, reached_now | (walker_now[:, :, None] == seg_range[None, None, :]))

    walker, reached = lax.fori_loop(0, tree_segs, climb, (walker, reached))
    anc_flat = reached.reshape(group_segs, tree_segs).astype(jnp.float32)
    id_picks = (group_ids[:, None] == jnp.arange(group_segs, dtype=jnp.int32)[None, :]).astype(
        jnp.float32
    )
    seg_rows = exact_dot(id_picks, anc_flat)
    local_pick = ((group_ids % tree_segs)[:, None] == seg_range[None, :]).astype(jnp.float32)
    tree_of = group_ids // tree_segs
    same_tree = (tree_of[:, None] == tree_of[None, :]).astype(jnp.float32)
    return (
        lax.dot_general(
            seg_rows,
            local_pick,
            (((1,), (1,)), ((), ())),
            precision=lax.Precision.HIGHEST,
            preferred_element_type=jnp.float32,
        )
        * same_tree
    )


def visible_mask(allowed, seg_len, query_start, query_rows, key_start, key_rows):
    group_segs = allowed.shape[0]
    query_index = query_start + jnp.arange(query_rows, dtype=jnp.int32)
    key_index = key_start + jnp.arange(key_rows, dtype=jnp.int32)
    query_slot = query_index // seg_len
    key_slot = key_index // seg_len
    seg_range = jnp.arange(group_segs, dtype=jnp.int32)
    query_pick = (query_slot[:, None] == seg_range[None, :]).astype(jnp.float32)
    key_pick = (key_slot[:, None] == seg_range[None, :]).astype(jnp.float32)
    linked = (
        lax.dot_general(
            exact_dot(query_pick, allowed),
            key_pick,
            (((1,), (1,)), ((), ())),
            precision=lax.Precision.HIGHEST,
            preferred_element_type=jnp.float32,
        )
        > 0.5
    )
    return linked & (
        (query_slot[:, None] != key_slot[None, :]) | (key_index[None, :] <= query_index[:, None])
    )


def pair_terms(query_part, grad_part, stat_part, delta_part, key_part, value_part, visible):
    scores = (
        jnp.einsum("qhd,khd->qhk", query_part, key_part, preferred_element_type=jnp.float32) * 0.125
    )
    scores = jnp.where(visible[:, None, :], scores, masked_score)
    probs_full = jnp.exp(scores - stat_part[:, :, None])
    grad_probs = jnp.einsum(
        "qhd,khd->qhk", grad_part, value_part, preferred_element_type=jnp.float32
    )
    grad_scores = (probs_full * (grad_probs - delta_part[:, :, None])).astype(jnp.bfloat16)
    grad_query = None
    grad_key = None
    grad_value = None
    grad_query = (
        jnp.einsum("qhk,khd->qhd", grad_scores, key_part, preferred_element_type=jnp.float32)
        * 0.125
    )
    grad_key = (
        jnp.einsum("qhk,qhd->khd", grad_scores, query_part, preferred_element_type=jnp.float32)
        * 0.125
    )
    grad_value = jnp.einsum(
        "qhk,qhd->khd",
        probs_full.astype(jnp.bfloat16),
        grad_part,
        preferred_element_type=jnp.float32,
    )
    return (grad_query, grad_key, grad_value)


def shards(
    tokens,
    cotangent,
    qkv_weight,
    out_weight,
    up_weight,
    down_weight,
    gain_attn,
    gain_ffn,
    parents,
    slot_ids,
):
    local_rows = tokens.shape[0]
    model_width = tokens.shape[1]
    shard_count = lax.axis_size("shard")
    my_start = lax.axis_index("shard") * local_rows
    seg_len = local_rows * shard_count // slot_ids.shape[0]
    allowed = slot_table(slot_ids, parents)
    qkv_full, out_full, attn_gain = (
        lax.all_gather(qkv_weight.astype(jnp.bfloat16), "shard", axis=0, tiled=True),
        lax.all_gather(out_weight.astype(jnp.bfloat16), "shard", axis=0, tiled=True),
        lax.all_gather(gain_attn.astype(jnp.bfloat16), "shard", axis=0, tiled=True),
    )
    inputs = tokens.astype(jnp.float32)
    normed_one, inv_one = normalize(inputs)
    entered = (normed_one * attn_gain.astype(jnp.float32)).astype(jnp.bfloat16)
    qkv_all = jnp.dot(entered, qkv_full, preferred_element_type=jnp.float32).astype(jnp.bfloat16)
    queries = qkv_all[:, :model_width]
    keys_local = qkv_all[:, model_width : 2 * model_width]
    values_local = qkv_all[:, 2 * model_width :]
    query_heads = queries.reshape(local_rows, HEADS, HEAD)
    start_state = (
        jnp.full((local_rows, HEADS), masked_score, jnp.float32),
        jnp.zeros((local_rows, HEADS), jnp.float32),
        jnp.zeros((local_rows, HEADS, HEAD), jnp.float32),
    )
    carried = start_state
    key_piece = lax.all_gather(keys_local, "shard", axis=0, tiled=True)
    value_piece = lax.all_gather(values_local, "shard", axis=0, tiled=True)
    piece_rows = key_piece.shape[0]
    block_rows = block_size()
    count_blocks = piece_rows // block_rows
    key_blocks = key_piece.reshape(count_blocks, block_rows, HEADS, HEAD)
    value_blocks = value_piece.reshape(count_blocks, block_rows, HEADS, HEAD)

    def attend_block(running, blocks):
        key_block, value_block, block_index = blocks
        run_max, run_sum, run_acc = running
        visible = visible_mask(
            allowed, seg_len, my_start, local_rows, block_index * block_rows, block_rows
        )
        scores = (
            jnp.einsum("qhd,khd->qhk", query_heads, key_block, preferred_element_type=jnp.float32)
            * 0.125
        )
        scores = jnp.where(visible[:, None, :], scores, masked_score)
        new_max = jnp.maximum(run_max, jnp.max(scores, axis=2))
        rescale = jnp.exp(run_max - new_max)
        exp_scores = jnp.exp(scores - new_max[:, :, None])
        run_sum = run_sum * rescale + jnp.sum(exp_scores, axis=2)
        run_acc = run_acc * rescale[:, :, None] + jnp.einsum(
            "qhk,khd->qhd",
            exp_scores.astype(jnp.bfloat16),
            value_block,
            preferred_element_type=jnp.float32,
        )
        return ((new_max, run_sum, run_acc), None)

    carried, unused = lax.scan(
        attend_block, carried, (key_blocks, value_blocks, jnp.arange(count_blocks, dtype=jnp.int32))
    )
    run_max, run_sum, run_acc = carried
    attn_exact = run_acc / run_sum[:, :, None]
    log_sum = run_max + jnp.log(run_sum)
    attended = attn_exact.reshape(local_rows, model_width).astype(jnp.bfloat16)
    hidden = inputs + jnp.dot(attended, out_full, preferred_element_type=jnp.float32)
    up_full, down_full, ffn_gain = (
        lax.all_gather(up_weight.astype(jnp.bfloat16), "shard", axis=0, tiled=True),
        lax.all_gather(down_weight.astype(jnp.bfloat16), "shard", axis=0, tiled=True),
        lax.all_gather(gain_ffn.astype(jnp.bfloat16), "shard", axis=0, tiled=True),
    )
    normed_two, inv_two = normalize(hidden)
    second = (normed_two * ffn_gain.astype(jnp.float32)).astype(jnp.bfloat16)
    pre_act = jnp.dot(second, up_full, preferred_element_type=jnp.float32)
    active = gelu_exact(pre_act).astype(jnp.bfloat16)
    output = (hidden + jnp.dot(active, down_full, preferred_element_type=jnp.float32)).astype(
        jnp.bfloat16
    )
    up_full, down_full, ffn_gain = (
        lax.all_gather(up_weight.astype(jnp.bfloat16), "shard", axis=0, tiled=True),
        lax.all_gather(down_weight.astype(jnp.bfloat16), "shard", axis=0, tiled=True),
        lax.all_gather(gain_ffn.astype(jnp.bfloat16), "shard", axis=0, tiled=True),
    )
    qkv_full, out_full, attn_gain = (
        lax.all_gather(qkv_weight.astype(jnp.bfloat16), "shard", axis=0, tiled=True),
        lax.all_gather(out_weight.astype(jnp.bfloat16), "shard", axis=0, tiled=True),
        lax.all_gather(gain_attn.astype(jnp.bfloat16), "shard", axis=0, tiled=True),
    )
    grad_down = t_times(active, cotangent)
    grad_active = times_t(cotangent, down_full).astype(jnp.bfloat16)
    grad_pre = (grad_active.astype(jnp.float32) * gelu_slope(pre_act)).astype(jnp.bfloat16)
    grad_up = t_times(second, grad_pre)
    grad_second = times_t(grad_pre, up_full)
    grad_gain_ffn = jnp.sum(grad_second * normed_two, axis=0)
    grad_hidden = cotangent.astype(jnp.float32) + norm_back(
        grad_second * ffn_gain.astype(jnp.float32), normed_two, inv_two
    )
    grad_y = grad_hidden.astype(jnp.bfloat16)
    grad_out = t_times(attended, grad_y)
    grad_attn = times_t(grad_y, out_full).astype(jnp.bfloat16)
    grad_heads = grad_attn.reshape(local_rows, HEADS, HEAD)
    row_delta = jnp.sum(grad_heads.astype(jnp.float32) * attn_exact, axis=2)
    start_back = jnp.zeros((local_rows, HEADS, HEAD), jnp.float32)
    carried = start_back
    key_piece = lax.all_gather(keys_local, "shard", axis=0, tiled=True)
    value_piece = lax.all_gather(values_local, "shard", axis=0, tiled=True)
    piece_rows = key_piece.shape[0]
    back_block_rows = block_size()
    count_blocks = piece_rows // back_block_rows
    key_blocks = key_piece.reshape(count_blocks, back_block_rows, HEADS, HEAD)
    value_blocks = value_piece.reshape(count_blocks, back_block_rows, HEADS, HEAD)

    def back_block(running, blocks):
        grad_query = running
        key_block, value_block, block_index = blocks
        block_start = block_index * back_block_rows
        visible = visible_mask(allowed, seg_len, my_start, local_rows, block_start, back_block_rows)
        part_query, part_key, part_value = pair_terms(
            query_heads, grad_heads, log_sum, row_delta, key_block, value_block, visible
        )
        joined = jnp.concatenate(
            (
                part_key.reshape(back_block_rows, model_width),
                part_value.reshape(back_block_rows, model_width),
            ),
            axis=1,
        )
        return (grad_query + part_query, joined.astype(jnp.bfloat16))

    carried, key_terms = lax.scan(
        back_block, carried, (key_blocks, value_blocks, jnp.arange(count_blocks, dtype=jnp.int32))
    )
    grad_query = carried
    key_terms = key_terms.reshape(piece_rows, 2 * model_width)
    key_grads = lax.psum_scatter(key_terms, "shard", scatter_dimension=0, tiled=True)
    grad_qkv = jnp.concatenate(
        (grad_query.reshape(local_rows, model_width), key_grads), axis=1
    ).astype(jnp.bfloat16)
    grad_qkv_weight = t_times(entered, grad_qkv)
    grad_entered = times_t(grad_qkv, qkv_full)
    grad_gain_attn = jnp.sum(grad_entered * normed_one, axis=0)
    input_grad = grad_hidden + norm_back(
        grad_entered * attn_gain.astype(jnp.float32), normed_one, inv_one
    )
    group_sums = (
        lax.psum_scatter(grad_qkv_weight.astype(jnp.bfloat16), "shard", scatter_dimension=0, tiled=True),
        lax.psum_scatter(grad_out.astype(jnp.bfloat16), "shard", scatter_dimension=0, tiled=True),
        lax.psum_scatter(grad_up.astype(jnp.bfloat16), "shard", scatter_dimension=0, tiled=True),
        lax.psum_scatter(grad_down.astype(jnp.bfloat16), "shard", scatter_dimension=0, tiled=True),
        lax.psum_scatter(grad_gain_attn, "shard", scatter_dimension=0, tiled=True),
        lax.psum_scatter(grad_gain_ffn, "shard", scatter_dimension=0, tiled=True),
    )
    totals = (
        lax.psum(group_sums[0].astype(jnp.bfloat16), "rep").astype(jnp.float32),
        lax.psum(group_sums[1].astype(jnp.bfloat16), "rep").astype(jnp.float32),
        lax.psum(group_sums[2].astype(jnp.bfloat16), "rep").astype(jnp.float32),
        lax.psum(group_sums[3].astype(jnp.bfloat16), "rep").astype(jnp.float32),
        lax.psum(group_sums[4].astype(jnp.bfloat16), "rep").astype(jnp.float32),
        lax.psum(group_sums[5].astype(jnp.bfloat16), "rep").astype(jnp.float32),
    )
    return (output, input_grad, totals[0], totals[1], totals[2], totals[3], totals[4], totals[5])


MESH = pl.DeviceIdType.MESH


def ring_place(shard):
    return (1 - shard % 2) * (shard // 2) + (shard % 2) * (7 - shard // 2)


def ring_shard(place):
    upper = place // 4
    return (1 - upper) * 2 * place + upper * (15 - 2 * place)


def remote(source, target, sent, got, device):
    return pltpu.make_async_remote_copy(
        src_ref=source,
        dst_ref=target,
        send_sem=sent,
        recv_sem=got,
        device_id=device,
        device_id_type=MESH,
    )


def around(place, offset):
    return ring_shard(lax.rem(place + offset + 8, 8))


class Where:
    def __init__(self):
        self.rep = lax.axis_index("rep")
        self.me = lax.axis_index("shard")
        self.y = self.rep // 2
        self.core = self.rep % 2
        self.rep_y = (1 - self.y) * 2 + self.core
        self.rep_core = self.y * 2 + 1 - self.core
        self.rep_far = (1 - self.y) * 2 + 1 - self.core
        self.place = ring_place(self.me)
        self.right = around(self.place, 1)
        self.left = around(self.place, -1)

    def other(self, step):
        return lax.rem(self.me + step, 8)

    def back(self, step):
        return lax.rem(self.me + 8 - step, 8)

    def greet(self):
        barrier = pltpu.get_barrier_semaphore()
        for step in range(1, 8):
            pl.semaphore_signal(
                barrier, inc=1, device_id=(self.rep, self.other(step)), device_id_type=MESH
            )
        for rep in (self.rep_y, self.rep_core, self.rep_far):
            pl.semaphore_signal(barrier, inc=1, device_id=(rep, self.me), device_id_type=MESH)
        pl.semaphore_wait(barrier, 10)


def normed_rows(values):
    average = jnp.mean(values, axis=-1, keepdims=True)
    centered = values - average
    variance = jnp.mean(centered * centered, axis=-1, keepdims=True)
    inv_std = lax.rsqrt(variance + 1e-05)
    return (centered * inv_std, inv_std)


def gain_row(gains_ref, which):
    return jnp.concatenate(
        [gains_ref[s, which * 8 : which * 8 + 1, :] for s in range(8)], axis=1
    ).astype(jnp.float32)


def head_lanes(values, head):
    lane = lax.broadcasted_iota(jnp.int32, values.shape, 1)
    return jnp.where(lane // HEAD == head, values, jnp.zeros_like(values))


def tile_masks(block, parents_ref):
    key_row = lax.broadcasted_iota(jnp.int32, (256, 256), 0)
    query_row = lax.broadcasted_iota(jnp.int32, (256, 256), 1)
    own = key_row <= query_row
    if block < 5:
        return (own, None)
    own = own & (key_row // 128 == query_row // 128)
    if block == 5:
        return (own, None)
    parent = jnp.where(query_row < 128, parents_ref[2 * block], parents_ref[2 * block + 1])
    return (own, parent == 10 + key_row // 128)


def score_parts(block, keys_ref, queries, masks):
    own_mask, branch_mask = masks
    full = 256 * block if block < 5 else 1280
    spans = [(0, full, None)] if full else []
    if branch_mask is not None:
        spans.append((1280, 256, branch_mask))
    spans.append((256 * block, 256, own_mask))
    parts = []
    for first, rows, mask in spans:
        scores = times_t(keys_ref[pl.ds(first, rows), :], queries)
        if mask is not None:
            scores = jnp.where(mask, scores, masked_score)
        parts.append((first, rows, scores))
    return parts


def summed(*parts):
    total = parts[0].astype(jnp.float32)
    for part in parts[1:]:
        total = total + part.astype(jnp.float32)
    return total


BLOCK_ORDER = [4, 3, -3, 2, -2, 1, -1, 0]


def layer_kernel(
    ids_ref, parents_ref, tok_ref, cot_ref, gain_one_ref, gain_two_ref, qkv_w, out_w, up_w, down_w,
    layer_ref, in_ref, qkv_out, out_out, up_out, down_out, gain_out, ent_hbm,
    stage, gain_ref, wq_send, slices, gains_ref, tok_all, qkv_slots, qkv, side_t, tree_rows, slot_rows,
    mixed, logs, att, out_all, w_all, xch, acts, parts, gw, rr, rr_out, cr_out, yr_out,
    do_slots, dk, dv, gq_t, qs_core, qs_half, qs_recv, qs_y, fin_up, gp, gp_recv, gp_rep,
    load_s, small_s, small_r, slc_s, slc_r, tok_s, tok_r, o_s, o_r, oy_s, oy_r, oc_s, oc_r, w_s, w_r,
    keep_s, mix_s, mix_r, cot_s, cot_r, sec_s, sec_r, part_s, part_r, do_s, do_r,
    go_s, go_r, rs_s, rs_r, ro_s, ro_r, fin_s, fin_r, ge_s, ge_r, qs_s, qs_r, qr_s, qr_r,
    gp_s, gp_r, gr_s, gr_r,
):
    low, full = jnp.bfloat16, jnp.float32
    dq_t, gq_slots = mixed, qkv.reshape(8, 256, 384)
    at = Where()
    rep, me, y, core = at.rep, at.me, at.y, at.core
    ring_device = ((rep, at.right), (rep, at.left))
    over_y, over_core = (at.rep_y, me), (at.rep_core, me)
    places = []
    for seg in range(16):
        place = jnp.int32(0)
        for slot in range(1, 16):
            place = jnp.where(ids_ref[slot] == seg, slot, place)
        places.append(place)

    loads = [
        pltpu.make_async_copy(qkv_w.at[:, pl.ds(j * 1024, 1024)], stage.at[j], load_s.at[j])
        for j in range(3)
    ]
    loads.append(pltpu.make_async_copy(out_w, stage.at[3], load_s.at[3]))
    loads.append(
        pltpu.make_async_copy(down_w.at[pl.ds(rep * 128, 128), :], stage.at[5], load_s.at[4])
    )
    for s in range(8):
        columns = pl.ds(pl.multiple_of(s * 512 + rep * 128, 128), 128)
        loads.append(
            pltpu.make_async_copy(
                up_w.at[:, columns], stage.at[4, :, pl.ds(s * 128, 128)], load_s.at[5 + s]
            )
        )
    for copy in loads:
        copy.start()
    gain_ref[0:8, :] = jnp.broadcast_to(gain_one_ref[...], (8, 128)).astype(low)
    gain_ref[8:16, :] = jnp.broadcast_to(gain_two_ref[...], (8, 128)).astype(low)
    at.greet()

    def flow_block(flow, offset):
        return around(at.place, -offset if flow else offset)

    def token_copy(flow, step, half):
        origin = flow_block(flow, -step)
        source = tok_ref if step == 0 else tok_all.at[origin]
        rows = pl.ds(half * 128, 128)
        return remote(
            source.at[rows, :],
            tok_all.at[origin, rows, :],
            tok_s.at[flow, step, half],
            tok_r.at[flow, step, half],
            ring_device[flow],
        )

    def step_halves(step):
        if step == 3:
            return [(0, 0), (1, 1)]
        return [(half, flow) for half in range(2) for flow in range(2)]

    def out_copy(flow, step):
        spot = out_all.at[flow_block(flow, -step), rep]
        return remote(spot, spot, o_s.at[flow, step], o_r.at[flow, step], ring_device[flow])

    def out_flows(step):
        return (0, 1) if step < 3 else (0,)

    def out_over_y(flow, step):
        spot = out_all.at[flow_block(flow, -step - 1), rep]
        return remote(spot, spot, oy_s.at[flow, step], oy_r.at[flow, step], over_y)

    def out_over_core(flow, step, own):
        spot = out_all.at[flow_block(flow, -step - 1), rep if own else at.rep_y]
        return remote(spot, spot, oc_s.at[own, flow, step], oc_r.at[own, flow, step], over_core)

    def w_copy(flow, step, half):
        spot = w_all.at[flow_block(flow, -step), half]
        return remote(spot, spot, w_s.at[flow, step, half], w_r.at[flow, step, half], ring_device[flow])

    def w_half(step, half):
        for flow in range(2):
            if step == 3 and flow != half:
                continue
            w_copy(flow, step, half).wait_recv()
            if step < 2 or (step == 2 and half == flow):
                w_copy(flow, step + 1, half).start()

    small = [
        remote(
            gain_ref,
            gains_ref.at[me],
            small_s.at[0, step],
            small_r.at[0, step],
            (rep, at.other(step)),
        )
        for step in range(1, 8)
    ]
    small += [
        remote(
            wq_send.at[at.other(step), :, core],
            slices.at[me, :, core],
            small_s.at[1, step],
            small_r.at[1, step],
            (rep, at.other(step)),
        )
        for step in range(1, 8)
    ]
    slice_core = remote(
        slices.at[:, :, core], slices.at[:, :, core], slc_s.at[0], slc_r.at[0], over_core
    )
    cot_y = remote(cot_ref, xch.at[6], cot_s.at[0], cot_r.at[0], over_y)
    cot_core = remote(cot_ref, xch.at[5], cot_s.at[1], cot_r.at[1], over_core)
    cot_far = remote(xch.at[6], xch.at[7], cot_s.at[2], cot_r.at[2], over_core)

    for copy in small[:7]:
        copy.start()
    for half in range(2):
        for flow in range(2):
            token_copy(flow, 0, half).start()
    cot_y.start()
    cot_core.start()
    for copy in loads[:3]:
        copy.wait()
    for s in range(8):
        for j in range(3):
            wq_send[s, :, :, :, j * 128 : j * 128 + 128] = (
                stage[j, :, s * 128 : s * 128 + 128].astype(low).reshape(2, 2, 32, 128)
            )
    for copy in small[7:]:
        copy.start()
    gains_ref[me] = gain_ref[...]
    slices[me, :, core] = wq_send[me, :, core]
    loads[3].wait()
    out_all[me] = stage[3].astype(low).reshape(4, 32, 1024)
    for flow in range(2):
        out_copy(flow, 0).start()
    for copy in loads[4:]:
        copy.wait()
    w_all[me, 0] = stage[4].astype(low)
    w_all[me, 1] = stage[5].astype(low)
    xch[4] = cot_ref[...]
    kept = {}

    def enter(rows, origin, count):
        slot = 4 + count % 2
        if count > 1:
            kept[count - 2].wait()
        normed, _ = normed_rows(rows.astype(full))
        entered = (normed * gain).astype(low)
        parts[slot] = entered
        kept[count] = pltpu.make_async_copy(parts.at[slot], ent_hbm.at[origin], keep_s.at[slot - 4])
        kept[count].start()
        weights = slices[...].reshape(1024, 384)
        made = jnp.dot(entered, weights, preferred_element_type=full).astype(low)
        qkv_slots[2 * origin] = made[:128]
        qkv_slots[2 * origin + 1] = made[128:]

    def token_step(step):
        for half, flow in step_halves(step):
            token_copy(flow, step, half).wait_recv()
            if step < 2 or (step == 2 and half == flow):
                token_copy(flow, step + 1, half).start()
        for flow in out_flows(step):
            out_copy(flow, step).wait_recv()
            if step < 2 or (step == 2 and flow == 0):
                out_copy(flow, step + 1).start()
            out_over_y(flow, step).start()
            out_over_core(flow, step, 1).start()

    token_step(0)
    for copy in small:
        copy.wait_recv()
    slice_core.start()
    slice_core.wait_recv()
    gain = gain_row(gains_ref, 0)
    enter(tok_ref[...], me, 0)
    count = 1
    for step in range(4):
        if step > 0:
            token_step(step)
        if step == W_START:
            for flow in range(2):
                w_copy(flow, 0, 0).start()
        for flow in out_flows(step):
            origin = flow_block(flow, -step - 1)
            enter(tok_all[origin], origin, count)
            count += 1
    cot_y.wait_recv()
    cot_far.start()
    kept[6].wait()
    kept[7].wait()

    for seg in range(16):
        qkv[seg * 128 : seg * 128 + 128, :] = qkv_slots[places[seg]]
    for block in range(8):
        side_t[:, block * 256 : block * 256 + 256] = qkv[block * 256 : block * 256 + 256, 256:384].T

    for block in range(8):
        masks = tile_masks(block, parents_ref)
        rows = pl.ds(block * 256, 256)

        def one_head(head, unused):
            queries = head_lanes(qkv[rows, 0:128], head) * low(0.125)
            tiles = score_parts(block, qkv.at[:, pl.ds(128, 128)], queries, masks)
            top = None
            for _, _, scores in tiles:
                part = jnp.max(scores, axis=0, keepdims=True)
                top = part if top is None else jnp.maximum(top, part)
            total = None
            mix = None
            head_rows = pl.ds(pl.multiple_of(head * HEAD, HEAD), HEAD)
            for first, number, scores in tiles:
                weights = jnp.exp(scores - top)
                part = jnp.sum(weights, axis=0, keepdims=True)
                total = part if total is None else total + part
                term = jnp.dot(
                    side_t[head_rows, pl.ds(first, number)],
                    weights.astype(low),
                    preferred_element_type=full,
                )
                mix = term if mix is None else mix + term
            mixed[head_rows, block * 256 : block * 256 + 256] = mix / total
            logs[pl.ds(pl.multiple_of(head * 8, 8), 8), block * 256 : block * 256 + 256] = (
                jnp.broadcast_to(top + jnp.log(total), (8, 256))
            )
            return unused

        lax.fori_loop(0, 2, one_head, 0)
        tree = mixed[:, block * 256 : block * 256 + 256].T.astype(low)
        tree_rows[2 * block] = tree[:128]
        tree_rows[2 * block + 1] = tree[128:]
        if block in W_BLOCKS:
            w_half(W_BLOCKS.index(block), 0)

    for slot in range(16):
        slot_rows[slot // 2, (slot % 2) * 128 : (slot % 2) * 128 + 128, :] = tree_rows[
            ids_ref[slot]
        ]
    my_columns = pl.ds(pl.multiple_of(me * 128, 128), 128)
    mix_sends = [
        remote(
            slot_rows.at[at.other(step)],
            att.at[:, my_columns],
            mix_s.at[step],
            mix_r.at[step],
            (rep, at.other(step)),
        )
        for step in range(1, 8)
    ]
    for copy in mix_sends:
        copy.start()
    for flow in range(2):
        w_copy(flow, 0, 1).start()
    att[:, my_columns] = slot_rows[me]
    for step in range(4):
        for flow in out_flows(step):
            out_over_y(flow, step).wait_recv()
            out_over_core(flow, step, 0).start()
    for step in range(4):
        for flow in out_flows(step):
            out_over_core(flow, step, 1).wait_recv()
            out_over_core(flow, step, 0).wait_recv()
    w_half(3, 0)
    for copy in mix_sends:
        copy.wait_recv()
    w_half(0, 1)

    out_full = out_all[...].reshape(1024, 1024)
    hidden = tok_ref[...].astype(full) + jnp.dot(att[...], out_full, preferred_element_type=full)
    ffn_gain = gain_row(gains_ref, 1)
    normed_two, _ = normed_rows(hidden)
    xch[0] = (normed_two * ffn_gain).astype(low)
    sec_y = remote(xch.at[0], xch.at[2], sec_s.at[0], sec_r.at[0], over_y)
    sec_core = remote(xch.at[0], xch.at[1], sec_s.at[1], sec_r.at[1], over_core)
    sec_far = remote(xch.at[2], xch.at[3], sec_s.at[2], sec_r.at[2], over_core)
    sec_y.start()
    sec_core.start()
    stage[0] = hidden[:128]
    stage[1] = hidden[128:]
    for step in range(4):
        for half, flow in step_halves(step):
            token_copy(flow, step, half).wait_send()
    w_half(1, 1)

    up = w_all[:, 0].reshape(1024, 1024)

    def ffn(first):
        second = xch[first : first + 2].reshape(512, 1024)
        pre = jnp.dot(second, up, preferred_element_type=full)
        bell = 1.0 + lax.erf(pre * 0.7071067811865476)
        acts[first : first + 2] = (0.5 * pre * bell).astype(low).reshape(2, 2, 128, 1024)
        slope = 0.5 * bell + pre * jnp.exp(-0.5 * pre * pre) * 0.3989422804014327
        acts[4 + first : 6 + first] = slope.astype(low).reshape(2, 2, 128, 1024)

    def ffn_back(first):
        cots = xch[4 + first : 6 + first].reshape(512, 1024)
        grad_act = times_t(cots, w_all[:, 1].reshape(1024, 1024)).astype(low).astype(full)
        slope = acts[4 + first : 6 + first].reshape(512, 1024).astype(full)
        grad_pre = (grad_act * slope).astype(low)
        acts[4 + first : 6 + first] = grad_pre.reshape(2, 2, 128, 1024)
        return times_t(grad_pre, w_all[:, 0].reshape(1024, 1024))

    sec_core.wait_recv()
    ffn(0)
    w_half(2, 1)
    sec_y.wait_recv()
    sec_far.start()
    cot_core.wait_recv()
    cot_far.wait_recv()
    w_half(3, 1)
    sec_far.wait_recv()
    ffn(2)

    def part_copy(kind, leg):
        index = kind * 3 + leg
        return remote(
            tok_all.at[index],
            parts.at[index],
            part_s.at[index],
            part_r.at[index],
            over_y if leg == 1 else over_core,
        )

    def weight_grads(half, offsets):
        blocks = [around(at.place, offset) for offset in offsets]
        spans = [pl.ds(pl.multiple_of(block * 128, 128), 128) for block in blocks]
        if half == 0:
            sides, other = [xch[0:4, :, span].reshape(1024, 128).T for span in spans], acts
        else:
            sides, other = [acts[0:4, :, :, span].reshape(1024, 128).T for span in spans], xch
        made = jnp.dot(
            jnp.concatenate(sides, axis=0),
            other[4:8].reshape(1024, 1024),
            preferred_element_type=full,
        ).astype(low)
        for i, block in enumerate(blocks):
            gw[block, half] = made[i * 128 : i * 128 + 128]

    def rs_copy(flow, step, half):
        return remote(
            gw.at[flow_block(flow, 4 - step), half],
            rr.at[flow, step, half],
            rs_s.at[flow, step, half],
            rs_r.at[flow, step, half],
            ring_device[flow],
        )

    def rs_half(step, half):
        for flow in range(2):
            block = flow_block(flow, 4 - step)
            if step == 0 and half != flow:
                continue
            if step > 1 or (step == 1 and half == flow):
                rs_copy(flow, step - 1, half).wait_recv()
                gw[block, half] = summed(gw[block, half], rr[flow, step - 1, half]).astype(low)
            rs_copy(flow, step, half).start()

    grad_far = ffn_back(2)
    tok_all[0] = grad_far[256:].astype(low)
    part_copy(0, 0).start()
    stage[2] = grad_far[:128]
    stage[3] = grad_far[128:256]
    part_copy(0, 0).wait_recv()
    tok_all[1] = summed(stage[2:4].reshape(256, 1024), parts[0]).astype(low)
    part_copy(0, 1).start()
    weight_grads(1, [4, 3, -3])
    rs_half(0, 1)
    grad_near = ffn_back(0)
    tok_all[2] = grad_near[256:].astype(low)
    part_copy(0, 2).start()
    stage[2] = grad_near[:128]
    stage[3] = grad_near[128:256]

    weight_grads(0, [4, 3, -3])
    rs_half(0, 0)
    rs_half(1, 1)

    def outputs(first):
        active = acts[first : first + 2].reshape(512, 1024)
        return jnp.dot(active, w_all[:, 1].reshape(1024, 1024), preferred_element_type=full)

    made = outputs(2)
    tok_all[3] = made[256:].astype(low)
    part_copy(1, 0).start()
    stage[4] = made[:128]
    stage[5] = made[128:256]
    part_copy(1, 0).wait_recv()
    tok_all[4] = summed(stage[4:6].reshape(256, 1024), parts[3]).astype(low)
    made = outputs(0)
    tok_all[5] = made[256:].astype(low)
    part_copy(1, 2).start()
    stage[0] = stage[0] + made[:128]
    stage[1] = stage[1] + made[128:256]
    part_copy(1, 1).start()

    for step in range(4):
        for half, flow in step_halves(step):
            w_copy(flow, step, half).wait_send()

    part_copy(0, 2).wait_recv()
    part_copy(0, 1).wait_recv()
    grad_second = summed(stage[2:4].reshape(256, 1024), parts[1], parts[2])
    hidden = tok_ref[...].astype(full) + jnp.dot(
        att[...], out_all[...].reshape(1024, 1024), preferred_element_type=full
    )
    normed_two, inv_two = normed_rows(hidden)
    gain_two = jnp.sum(grad_second * normed_two, axis=0, keepdims=True)
    for s in range(8):
        gp[s, 8:16, :] = jnp.broadcast_to(gain_two[:, s * 128 : s * 128 + 128], (8, 128))
    grad_hidden = cot_ref[...].astype(full) + norm_back(
        grad_second * gain_row(gains_ref, 1), normed_two, inv_two
    )
    stage[2] = grad_hidden[:128]
    stage[3] = grad_hidden[128:]
    grad_y = grad_hidden.astype(low)
    grad_attn = times_t(grad_y, out_all[...].reshape(1024, 1024)).astype(low)
    for copy in mix_sends:
        copy.wait_send()
    for s in range(8):
        slot_rows[s] = grad_attn[:, s * 128 : s * 128 + 128]
    do_sends = [
        remote(
            slot_rows.at[at.other(step)],
            do_slots.at[me],
            do_s.at[step],
            do_r.at[step],
            (rep, at.other(step)),
        )
        for step in range(1, 8)
    ]
    for copy in do_sends:
        copy.start()
    do_slots[me] = slot_rows[me]

    weight_grads(1, [2, -2, 1, -1, 0])
    rs_half(2, 1)
    rs_half(1, 0)
    weight_grads(0, [2, -2, 1, -1, 0])

    for step in range(4):
        for flow in out_flows(step):
            out_copy(flow, step).wait_send()
            out_over_y(flow, step).wait_send()
            out_over_core(flow, step, 0).wait_send()
            out_over_core(flow, step, 1).wait_send()
    for block in range(8):
        out_all[block] = (
            jnp.dot(
                att[:, block * 128 : block * 128 + 128].T, grad_y, preferred_element_type=full
            )
            .astype(low)
            .reshape(4, 32, 1024)
        )
    outs = out_all
    go_core = [
        remote(
            outs.at[:, 2 * i + 1 - core], cr_out.at[:, i], go_s.at[i], go_r.at[i], over_core
        )
        for i in range(2)
    ]
    for copy in go_core:
        copy.start()
    for copy in (cot_y, cot_core, cot_far, sec_y, sec_core, sec_far):
        copy.wait_send()
    fetch = pltpu.make_async_copy(ent_hbm, xch, load_s.at[0])
    fetch.start()
    for copy in go_core:
        copy.wait_recv()
    outs[:, at.rep_y] = summed(outs[:, at.rep_y], cr_out[:, 1 - y]).astype(low)
    go_y = remote(outs.at[:, at.rep_y], yr_out, go_s.at[2], go_r.at[2], over_y)
    go_y.start()

    def ro_copy(flow, step):
        return remote(
            outs.at[flow_block(flow, 4 - step), rep],
            rr_out.at[flow, step],
            ro_s.at[flow, step],
            ro_r.at[flow, step],
            ring_device[flow],
        )

    def ro_flows(step):
        return (0, 1) if step else (0,)

    def ro_step(step):
        for flow in ro_flows(step):
            block = flow_block(flow, 4 - step)
            if step > 0 and flow in ro_flows(step - 1):
                ro_copy(flow, step - 1).wait_recv()
                outs[block, rep] = summed(outs[block, rep], rr_out[flow, step - 1]).astype(low)
            ro_copy(flow, step).start()

    rs_half(3, 1)

    for copy in do_sends:
        copy.wait_recv()
    for seg in range(16):
        tree_rows[seg] = do_slots.reshape(16, 128, 128)[places[seg]]
    for block in range(8):
        side_t[:, block * 256 : block * 256 + 256] = qkv[block * 256 : block * 256 + 256, 128:256].T
    dk[...] = jnp.zeros_like(dk)
    dv[...] = jnp.zeros_like(dv)

    for block in range(8):
        masks = tile_masks(block, parents_ref)
        rows = pl.ds(block * 256, 256)

        def one_head_back(head, unused):
            head_rows = pl.ds(pl.multiple_of(head * HEAD, HEAD), HEAD)
            queries = head_lanes(qkv[rows, 0:128], head) * low(0.125)
            grads = tree_rows[2 * block : 2 * block + 2].reshape(256, 128)
            grad_rows = head_lanes(grads, head)
            lse = logs[pl.ds(pl.multiple_of(head * 8, 8), 8), block * 256 : block * 256 + 256][0:1]
            both = grads.T.astype(full) * mixed[:, block * 256 : block * 256 + 256]
            delta = jnp.where(
                head == 0,
                jnp.sum(both[:HEAD], axis=0, keepdims=True),
                jnp.sum(both[HEAD:], axis=0, keepdims=True),
            )
            grad_query = None
            for first, number, scores in score_parts(
                block, qkv.at[:, pl.ds(128, 128)], queries, masks
            ):
                keys = pl.ds(first, number)
                weights = jnp.exp(scores - lse)
                grad_weights = times_t(qkv[keys, 256:384], grad_rows)
                grad_scores = (weights * (grad_weights - delta)).astype(low)
                dk[keys, :] += jnp.dot(grad_scores, queries, preferred_element_type=full)
                dv[keys, :] += jnp.dot(weights.astype(low), grad_rows, preferred_element_type=full)
                term = jnp.dot(side_t[head_rows, keys], grad_scores, preferred_element_type=full)
                grad_query = term if grad_query is None else grad_query + term
            dq_t[head_rows, block * 256 : block * 256 + 256] = grad_query * 0.125
            return unused

        lax.fori_loop(0, 2, one_head_back, 0)
        if block == 1:
            rs_half(2, 0)
        if block == 5:
            rs_half(3, 0)
        if block == 4:
            outs[:, rep] = summed(outs[:, rep], cr_out[:, y]).astype(low)
            go_y.wait_recv()
            outs[:, rep] = summed(outs[:, rep], yr_out[...]).astype(low)
            ro_step(0)
        if block == 6:
            ro_step(1)

    for seg in range(16):
        rows = pl.ds(seg * 128, 128)
        qkv_slots[seg, :, 0:128] = dq_t[:, seg * 128 : seg * 128 + 128].T.astype(low)
        qkv_slots[seg, :, 128:256] = dk[rows, :].astype(low)
        qkv_slots[seg, :, 256:384] = dv[rows, :].astype(low)
    for slot in range(16):
        gq_slots[slot // 2, (slot % 2) * 128 : (slot % 2) * 128 + 128, :] = qkv_slots[ids_ref[slot]]

    def ge_copy(flow, step, half):
        return remote(
            acts.at[flow * 4 + step, half],
            w_all.at[flow * 4 + step, half],
            ge_s.at[flow, step, half],
            ge_r.at[flow, step, half],
            ring_device[flow],
        )

    def ge_part(block):
        return times_t(gq_slots[block], slices[...].reshape(1024, 384))

    def ge_step(step):
        made = [ge_part(flow_block(flow, 4 - step)) for flow in range(2)]
        for half in range(2):
            for flow in range(2):
                if step == 0 and half != flow:
                    continue
                rows = made[flow][half * 128 : half * 128 + 128]
                if step > 1 or (step == 1 and half == flow):
                    ge_copy(flow, step - 1, half).wait_recv()
                    rows = rows + w_all[flow * 4 + step - 1, half].astype(full)
                acts[flow * 4 + step, half] = rows.astype(low)
                ge_copy(flow, step, half).start()

    ge_step(0)
    ro_step(2)
    for block in range(8):
        gq_t[:, block * 256 : block * 256 + 256] = gq_slots[block].T
    fetch.wait()
    for copy in small:
        copy.wait_send()
    for s in range(8):
        made = jnp.dot(
            gq_t[...],
            xch[:, :, s * 128 : s * 128 + 128].reshape(2048, 128),
            preferred_element_type=full,
        )
        wq_send[s] = made.T.astype(low).reshape(2, 2, 32, 384)
    qs_over_core = remote(wq_send.at[:, :, 1 - core], qs_core, qr_s.at[0], qr_r.at[0], over_core)
    qs_over_core.start()
    ge_step(1)
    qs_over_core.wait_recv()
    qs_half[...] = summed(wq_send[:, :, core], qs_core[...]).astype(low)
    qs_over_y = remote(qs_half.at[:, 1 - y], qs_y, qr_s.at[1], qr_r.at[1], over_y)
    qs_over_y.start()
    ro_step(3)
    ge_step(2)
    qs_over_y.wait_recv()
    qs_half[:, y] = summed(qs_half[:, y], qs_y[...]).astype(low)
    qs_sends = [
        remote(
            qs_half.at[at.other(step), y],
            qs_recv.at[me],
            qs_s.at[step],
            qs_r.at[step],
            (rep, at.other(step)),
        )
        for step in range(1, 8)
    ]
    for copy in qs_sends:
        copy.start()
    qs_recv[me] = qs_half[me, y]

    def final_copy(kind, leg):
        quarter = at.rep_y if leg == 2 else rep
        if kind == 0:
            spot = fin_up.at[quarter]
        elif kind == 1:
            spot = down_out.at[pl.ds(quarter * 128, 128), :]
        elif kind == 2:
            spot = out_out.at[pl.ds(quarter * 32, 32), :]
        else:
            spot = qkv_out.at[pl.ds(quarter * 32, 32), :]
        device = over_y if leg == 0 else over_core
        return remote(spot, spot, fin_s.at[kind, leg], fin_r.at[kind, leg], device)

    for half in range(2):
        for flow in range(2):
            rs_copy(flow, 3, half).wait_recv()
        total = summed(gw[me, half], rr[0, 3, half], rr[1, 3, half]).astype(low)
        if half == 0:
            fin_up[rep] = total
        else:
            down_out[pl.ds(rep * 128, 128), :] = total
        final_copy(half, 0).start()
        final_copy(half, 1).start()
    for flow in range(2):
        ro_copy(flow, 3).wait_recv()
    out_out[pl.ds(rep * 32, 32), :] = summed(outs[me, rep], rr_out[0, 3], rr_out[1, 3]).astype(low)
    final_copy(2, 0).start()
    final_copy(2, 1).start()
    ge_step(3)
    part_copy(1, 1).wait_recv()
    part_copy(1, 2).wait_recv()
    tok_all[6] = summed(stage[0:2].reshape(256, 1024), parts[4], parts[5]).astype(low)
    layer_write = pltpu.make_async_copy(tok_all.at[6], layer_ref, load_s.at[1])
    layer_write.start()
    for copy in qs_sends:
        copy.wait_recv()
    quarter_rows = pl.ds(rep * 32, 32)
    for s in range(8):
        total = qs_recv[s]
        for j in range(3):
            first = j * 1024 + s * 128
            qkv_out[quarter_rows, first : first + 128] = total[:, j * 128 : j * 128 + 128]
    final_copy(3, 0).start()
    final_copy(3, 1).start()
    for kind in range(4):
        final_copy(kind, 0).wait_recv()
        final_copy(kind, 2).start()

    grad_entered = ge_part(me)
    for flow in range(2):
        ge_copy(flow, 3, 0).wait_recv()
        ge_copy(flow, 3, 1).wait_recv()
        grad_entered = grad_entered + w_all[flow * 4 + 3].reshape(256, 1024).astype(full)
    normed, inv_std = normed_rows(tok_ref[...].astype(full))
    gain_one = jnp.sum(grad_entered * normed, axis=0, keepdims=True)
    for s in range(8):
        gp[s, 0:8, :] = jnp.broadcast_to(gain_one[:, s * 128 : s * 128 + 128], (8, 128))
    gain_sends = [
        remote(
            gp.at[at.other(step)],
            gp_recv.at[me],
            gp_s.at[step],
            gp_r.at[step],
            (rep, at.other(step)),
        )
        for step in range(1, 8)
    ]
    for copy in gain_sends:
        copy.start()
    gp_recv[me] = gp[me]
    in_grad = stage[2:4].reshape(256, 1024) + norm_back(
        grad_entered * gain_row(gains_ref, 0), normed, inv_std
    )
    stage[4] = in_grad[:128]
    stage[5] = in_grad[128:]
    in_write = pltpu.make_async_copy(stage.at[4:6], in_ref, load_s.at[2])
    in_write.start()
    for copy in gain_sends:
        copy.wait_recv()
    total = gp_recv[0]
    for s in range(1, 8):
        total = total + gp_recv[s]
    gp_rep[rep] = total
    rep_sends = [
        remote(gp_rep.at[rep], gp_rep.at[rep], gr_s.at[i], gr_r.at[i], (to, me))
        for i, to in enumerate((at.rep_y, at.rep_core, at.rep_far))
    ]
    for copy in rep_sends:
        copy.start()
    for kind in range(4):
        final_copy(kind, 1).wait_recv()
        final_copy(kind, 2).wait_recv()
    for quarter in range(4):
        for s in range(8):
            first = s * 512 + quarter * 128
            up_out[:, first : first + 128] = fin_up[quarter, :, s * 128 : s * 128 + 128]
    for copy in rep_sends:
        copy.wait()
    gain_out[...] = gp_rep[0] + gp_rep[1] + gp_rep[2] + gp_rep[3]

    layer_write.wait()
    in_write.wait()
    for kind in range(4):
        for leg in range(3):
            final_copy(kind, leg).wait_send()
    qs_over_y.wait_send()
    qs_over_core.wait_send()
    go_y.wait_send()
    for copy in go_core + qs_sends + gain_sends + do_sends:
        copy.wait_send()
    slice_core.wait_send()
    for kind in range(2):
        for leg in range(3):
            part_copy(kind, leg).wait_send()
    for step in range(4):
        for flow in range(2):
            for half in range(2):
                if step > 0 or half == flow:
                    ge_copy(flow, step, half).wait_send()
                    rs_copy(flow, step, half).wait_send()
        for flow in ro_flows(step):
            ro_copy(flow, step).wait_send()


def widen_kernel(*refs):
    for source, target in zip(refs[:6], refs[7:13]):
        target[...] = source[...].astype(target.dtype)
    refs[13][...] = refs[6][0:1, :]
    refs[14][...] = refs[6][8:9, :]


W_START = 2
W_BLOCKS = [0, 4, 7]


def fast_shards(
    tokens, cotangent, qkv_weight, out_weight, up_weight, down_weight, gain_attn, gain_ffn, parents, slot_ids
):
    low, full = jnp.bfloat16, jnp.float32
    smem = pl.BlockSpec(memory_space=pltpu.SMEM)
    vmem = pl.BlockSpec(memory_space=pltpu.VMEM)
    anywhere = pl.BlockSpec(memory_space=pl.ANY)

    def dma(*shape):
        return pltpu.SemaphoreType.DMA(shape)

    v = pltpu.VMEM
    scratch = [
        v((6, 128, 1024), full),
        v((16, 128), low),
        v((8, 2, 2, 32, 384), low),
        v((8, 2, 2, 32, 384), low),
        v((8, 16, 128), low),
        v((8, 256, 1024), low),
        v((16, 128, 384), low),
        v((2048, 384), low),
        v((128, 2048), low),
        v((16, 128, 128), low),
        v((8, 256, 128), low),
        v((128, 2048), full),
        v((16, 2048), full),
        v((256, 1024), low),
        v((8, 4, 32, 1024), low),
        v((8, 2, 128, 1024), low),
        v((8, 256, 1024), low),
        v((8, 2, 128, 1024), low),
        v((6, 256, 1024), low),
        v((8, 2, 128, 1024), low),
        v((2, 4, 2, 128, 1024), low),
        v((2, 4, 32, 1024), low),
        v((8, 2, 32, 1024), low),
        v((8, 32, 1024), low),
        v((8, 256, 128), low),
        v((2048, 128), full),
        v((2048, 128), full),
        v((384, 2048), low),
        v((8, 2, 32, 384), low),
        v((8, 2, 32, 384), low),
        v((8, 32, 384), low),
        v((8, 32, 384), low),
        v((4, 128, 1024), low),
        v((8, 16, 128), full),
        v((8, 16, 128), full),
        v((4, 16, 128), full),
        dma(13), dma(2, 8), dma(2, 8), dma(1), dma(1), dma(2, 4, 2), dma(2, 4, 2),
        dma(2, 4), dma(2, 4), dma(2, 4), dma(2, 4), dma(2, 2, 4), dma(2, 2, 4),
        dma(2, 4, 2), dma(2, 4, 2), dma(2), dma(8), dma(8), dma(3), dma(3), dma(3), dma(3),
        dma(6), dma(6), dma(8), dma(8), dma(3), dma(3), dma(2, 4, 2), dma(2, 4, 2),
        dma(2, 4), dma(2, 4), dma(4, 3), dma(4, 3), dma(2, 4, 2), dma(2, 4, 2), dma(8), dma(8),
        dma(2), dma(2), dma(8), dma(8), dma(3), dma(3),
    ]
    made = pl.pallas_call(
        layer_kernel,
        out_shape=[
            jax.ShapeDtypeStruct((256, 1024), low),
            jax.ShapeDtypeStruct((2, 128, 1024), full),
            jax.ShapeDtypeStruct((128, 3072), low),
            jax.ShapeDtypeStruct((128, 1024), low),
            jax.ShapeDtypeStruct((128, 4096), low),
            jax.ShapeDtypeStruct((512, 1024), low),
            jax.ShapeDtypeStruct((16, 128), full),
            jax.ShapeDtypeStruct((8, 256, 1024), low),
        ],
        in_specs=[smem] * 2 + [vmem] * 4 + [anywhere] * 4,
        out_specs=[anywhere] * 2 + [vmem] * 5 + [anywhere],
        scratch_shapes=scratch,
        compiler_params=pltpu.CompilerParams(
            collective_id=1, has_side_effects=True, vmem_limit_bytes=VMEM_LIMIT
        ),
    )(
        slot_ids, parents.reshape(16), tokens, cotangent, gain_attn.reshape(1, 128), gain_ffn.reshape(1, 128), qkv_weight, out_weight, up_weight,
        down_weight,
    )
    shapes = [(256, 1024), (256, 1024), (128, 3072), (128, 1024), (128, 4096), (512, 1024)]
    results = [made[0], made[1].reshape(256, 1024)] + list(made[2:7])

    def spec(shape):
        return pl.BlockSpec((shape[0] // 4, shape[1]), lambda i: (i, 0))

    gain_spec = pl.BlockSpec((1, 128), lambda i: (0, 0))
    last = pl.pallas_call(
        widen_kernel,
        grid=(4,),
        out_shape=[jax.ShapeDtypeStruct(shapes[0], low)]
        + [jax.ShapeDtypeStruct(shape, full) for shape in shapes[1:]]
        + [jax.ShapeDtypeStruct((1, 128), full)] * 2,
        in_specs=[spec(shape) for shape in shapes] + [pl.BlockSpec((16, 128), lambda i: (0, 0))],
        out_specs=[spec(shape) for shape in shapes] + [gain_spec] * 2,
    )(*results)
    return tuple(last[:6]) + (last[6].reshape(128), last[7].reshape(128))


VMEM_LIMIT = 61 * 2**20


def solution(mesh):
    in_specs = (
        P(("rep", "shard"), None),
        P(("rep", "shard"), None),
        P("shard", None),
        P("shard", None),
        P("shard", None),
        P("shard", None),
        P("shard"),
        P("shard"),
        P("rep", None),
        P("rep"),
    )
    out_specs = (
        P(("rep", "shard"), None),
        P(("rep", "shard"), None),
        P("shard", None),
        P("shard", None),
        P("shard", None),
        P("shard", None),
        P("shard"),
        P("shard"),
    )

    def fits(*args):
        shapes = [a.shape for a in args]
        return shapes[0] == (8192, 1024) and shapes[4] == (1024, 4096) and shapes[8] == (4, 16)

    small = mesh.shape["rep"] == 4 and mesh.shape["shard"] == 8

    def whole(*args):
        run = fast_shards if small and fits(*args) else shards
        return jax.shard_map(
            run, mesh=mesh, in_specs=in_specs, out_specs=out_specs, check_vma=False
        )(*args)

    return whole
```

```python
import jax
import jax.numpy as jnp
from jax import lax
from jax.experimental import pallas as pl
from jax.experimental.pallas import tpu as pltpu
from jax.sharding import PartitionSpec as P

HEADS = 16
HEAD = 64


masked_score = -1e30


def block_size():
    return 512


def normalize(values):
    average = jnp.mean(values, axis=-1, keepdims=True)
    centered = values - average
    variance = jnp.mean(centered * centered, axis=-1, keepdims=True)
    inv_std = lax.rsqrt(variance + 1e-05)
    return (centered * inv_std, inv_std)


def gelu_exact(values):
    return 0.5 * values * (1.0 + lax.erf(values * 0.7071067811865476))


def gelu_slope(values):
    return (
        0.5 * (1.0 + lax.erf(values * 0.7071067811865476))
        + values * jnp.exp(-0.5 * values * values) * 0.3989422804014327
    )


def norm_back(grad_normed, normed, inv_std):
    first_mean = jnp.mean(grad_normed, axis=-1, keepdims=True)
    second_mean = jnp.mean(grad_normed * normed, axis=-1, keepdims=True)
    return inv_std * (grad_normed - first_mean - normed * second_mean)


def times_t(left_side, right_side):
    return lax.dot_general(
        left_side, right_side, (((1,), (1,)), ((), ())), preferred_element_type=jnp.float32
    )


def t_times(left_side, right_side):
    return lax.dot_general(
        left_side, right_side, (((0,), (0,)), ((), ())), preferred_element_type=jnp.float32
    )


def exact_dot(left_side, right_side):
    return jnp.dot(
        left_side, right_side, precision=lax.Precision.HIGHEST, preferred_element_type=jnp.float32
    )


def slot_table(group_ids, parents):
    tree_segs = parents.shape[1]
    group_segs = group_ids.shape[0]
    seg_range = jnp.arange(tree_segs, dtype=jnp.int32)
    walker = seg_range[None, :]
    reached = walker[:, :, None] == seg_range[None, None, :]

    def climb(step_index, carried):
        walker_now, reached_now = carried
        walker_now = jnp.sum(
            jnp.where(walker_now[:, :, None] == seg_range[None, None, :], parents[:, None, :], 0),
            axis=2,
        )
        return (walker_now, reached_now | (walker_now[:, :, None] == seg_range[None, None, :]))

    walker, reached = lax.fori_loop(0, tree_segs, climb, (walker, reached))
    anc_flat = reached.reshape(group_segs, tree_segs).astype(jnp.float32)
    id_picks = (group_ids[:, None] == jnp.arange(group_segs, dtype=jnp.int32)[None, :]).astype(
        jnp.float32
    )
    seg_rows = exact_dot(id_picks, anc_flat)
    local_pick = ((group_ids % tree_segs)[:, None] == seg_range[None, :]).astype(jnp.float32)
    tree_of = group_ids // tree_segs
    same_tree = (tree_of[:, None] == tree_of[None, :]).astype(jnp.float32)
    return (
        lax.dot_general(
            seg_rows,
            local_pick,
            (((1,), (1,)), ((), ())),
            precision=lax.Precision.HIGHEST,
            preferred_element_type=jnp.float32,
        )
        * same_tree
    )


def visible_mask(allowed, seg_len, query_start, query_rows, key_start, key_rows):
    group_segs = allowed.shape[0]
    query_index = query_start + jnp.arange(query_rows, dtype=jnp.int32)
    key_index = key_start + jnp.arange(key_rows, dtype=jnp.int32)
    query_slot = query_index // seg_len
    key_slot = key_index // seg_len
    seg_range = jnp.arange(group_segs, dtype=jnp.int32)
    query_pick = (query_slot[:, None] == seg_range[None, :]).astype(jnp.float32)
    key_pick = (key_slot[:, None] == seg_range[None, :]).astype(jnp.float32)
    linked = (
        lax.dot_general(
            exact_dot(query_pick, allowed),
            key_pick,
            (((1,), (1,)), ((), ())),
            precision=lax.Precision.HIGHEST,
            preferred_element_type=jnp.float32,
        )
        > 0.5
    )
    return linked & (
        (query_slot[:, None] != key_slot[None, :]) | (key_index[None, :] <= query_index[:, None])
    )


def pair_terms(query_part, grad_part, stat_part, delta_part, key_part, value_part, visible):
    scores = (
        jnp.einsum("qhd,khd->qhk", query_part, key_part, preferred_element_type=jnp.float32) * 0.125
    )
    scores = jnp.where(visible[:, None, :], scores, masked_score)
    probs_full = jnp.exp(scores - stat_part[:, :, None])
    grad_probs = jnp.einsum(
        "qhd,khd->qhk", grad_part, value_part, preferred_element_type=jnp.float32
    )
    grad_scores = (probs_full * (grad_probs - delta_part[:, :, None])).astype(jnp.bfloat16)
    grad_query = None
    grad_key = None
    grad_value = None
    grad_query = (
        jnp.einsum("qhk,khd->qhd", grad_scores, key_part, preferred_element_type=jnp.float32)
        * 0.125
    )
    grad_key = (
        jnp.einsum("qhk,qhd->khd", grad_scores, query_part, preferred_element_type=jnp.float32)
        * 0.125
    )
    grad_value = jnp.einsum(
        "qhk,qhd->khd",
        probs_full.astype(jnp.bfloat16),
        grad_part,
        preferred_element_type=jnp.float32,
    )
    return (grad_query, grad_key, grad_value)


def shards(
    tokens,
    cotangent,
    qkv_weight,
    out_weight,
    up_weight,
    down_weight,
    gain_attn,
    gain_ffn,
    parents,
    slot_ids,
):
    local_rows = tokens.shape[0]
    model_width = tokens.shape[1]
    shard_count = lax.axis_size("shard")
    my_start = lax.axis_index("shard") * local_rows
    seg_len = local_rows * shard_count // slot_ids.shape[0]
    allowed = slot_table(slot_ids, parents)
    qkv_full, out_full, attn_gain = (
        lax.all_gather(qkv_weight.astype(jnp.bfloat16), "shard", axis=0, tiled=True),
        lax.all_gather(out_weight.astype(jnp.bfloat16), "shard", axis=0, tiled=True),
        lax.all_gather(gain_attn.astype(jnp.bfloat16), "shard", axis=0, tiled=True),
    )
    inputs = tokens.astype(jnp.float32)
    normed_one, inv_one = normalize(inputs)
    entered = (normed_one * attn_gain.astype(jnp.float32)).astype(jnp.bfloat16)
    qkv_all = jnp.dot(entered, qkv_full, preferred_element_type=jnp.float32).astype(jnp.bfloat16)
    queries = qkv_all[:, :model_width]
    keys_local = qkv_all[:, model_width : 2 * model_width]
    values_local = qkv_all[:, 2 * model_width :]
    query_heads = queries.reshape(local_rows, HEADS, HEAD)
    start_state = (
        jnp.full((local_rows, HEADS), masked_score, jnp.float32),
        jnp.zeros((local_rows, HEADS), jnp.float32),
        jnp.zeros((local_rows, HEADS, HEAD), jnp.float32),
    )
    carried = start_state
    key_piece = lax.all_gather(keys_local, "shard", axis=0, tiled=True)
    value_piece = lax.all_gather(values_local, "shard", axis=0, tiled=True)
    piece_rows = key_piece.shape[0]
    block_rows = block_size()
    count_blocks = piece_rows // block_rows
    key_blocks = key_piece.reshape(count_blocks, block_rows, HEADS, HEAD)
    value_blocks = value_piece.reshape(count_blocks, block_rows, HEADS, HEAD)

    def attend_block(running, blocks):
        key_block, value_block, block_index = blocks
        run_max, run_sum, run_acc = running
        visible = visible_mask(
            allowed, seg_len, my_start, local_rows, block_index * block_rows, block_rows
        )
        scores = (
            jnp.einsum("qhd,khd->qhk", query_heads, key_block, preferred_element_type=jnp.float32)
            * 0.125
        )
        scores = jnp.where(visible[:, None, :], scores, masked_score)
        new_max = jnp.maximum(run_max, jnp.max(scores, axis=2))
        rescale = jnp.exp(run_max - new_max)
        exp_scores = jnp.exp(scores - new_max[:, :, None])
        run_sum = run_sum * rescale + jnp.sum(exp_scores, axis=2)
        run_acc = run_acc * rescale[:, :, None] + jnp.einsum(
            "qhk,khd->qhd",
            exp_scores.astype(jnp.bfloat16),
            value_block,
            preferred_element_type=jnp.float32,
        )
        return ((new_max, run_sum, run_acc), None)

    carried, unused = lax.scan(
        attend_block, carried, (key_blocks, value_blocks, jnp.arange(count_blocks, dtype=jnp.int32))
    )
    run_max, run_sum, run_acc = carried
    attn_exact = run_acc / run_sum[:, :, None]
    log_sum = run_max + jnp.log(run_sum)
    attended = attn_exact.reshape(local_rows, model_width).astype(jnp.bfloat16)
    hidden = inputs + jnp.dot(attended, out_full, preferred_element_type=jnp.float32)
    up_full, down_full, ffn_gain = (
        lax.all_gather(up_weight.astype(jnp.bfloat16), "shard", axis=0, tiled=True),
        lax.all_gather(down_weight.astype(jnp.bfloat16), "shard", axis=0, tiled=True),
        lax.all_gather(gain_ffn.astype(jnp.bfloat16), "shard", axis=0, tiled=True),
    )
    normed_two, inv_two = normalize(hidden)
    second = (normed_two * ffn_gain.astype(jnp.float32)).astype(jnp.bfloat16)
    pre_act = jnp.dot(second, up_full, preferred_element_type=jnp.float32)
    active = gelu_exact(pre_act).astype(jnp.bfloat16)
    output = (hidden + jnp.dot(active, down_full, preferred_element_type=jnp.float32)).astype(
        jnp.bfloat16
    )
    up_full, down_full, ffn_gain = (
        lax.all_gather(up_weight.astype(jnp.bfloat16), "shard", axis=0, tiled=True),
        lax.all_gather(down_weight.astype(jnp.bfloat16), "shard", axis=0, tiled=True),
        lax.all_gather(gain_ffn.astype(jnp.bfloat16), "shard", axis=0, tiled=True),
    )
    qkv_full, out_full, attn_gain = (
        lax.all_gather(qkv_weight.astype(jnp.bfloat16), "shard", axis=0, tiled=True),
        lax.all_gather(out_weight.astype(jnp.bfloat16), "shard", axis=0, tiled=True),
        lax.all_gather(gain_attn.astype(jnp.bfloat16), "shard", axis=0, tiled=True),
    )
    grad_down = t_times(active, cotangent)
    grad_active = times_t(cotangent, down_full).astype(jnp.bfloat16)
    grad_pre = (grad_active.astype(jnp.float32) * gelu_slope(pre_act)).astype(jnp.bfloat16)
    grad_up = t_times(second, grad_pre)
    grad_second = times_t(grad_pre, up_full)
    grad_gain_ffn = jnp.sum(grad_second * normed_two, axis=0)
    grad_hidden = cotangent.astype(jnp.float32) + norm_back(
        grad_second * ffn_gain.astype(jnp.float32), normed_two, inv_two
    )
    grad_y = grad_hidden.astype(jnp.bfloat16)
    grad_out = t_times(attended, grad_y)
    grad_attn = times_t(grad_y, out_full).astype(jnp.bfloat16)
    grad_heads = grad_attn.reshape(local_rows, HEADS, HEAD)
    row_delta = jnp.sum(grad_heads.astype(jnp.float32) * attn_exact, axis=2)
    start_back = jnp.zeros((local_rows, HEADS, HEAD), jnp.float32)
    carried = start_back
    key_piece = lax.all_gather(keys_local, "shard", axis=0, tiled=True)
    value_piece = lax.all_gather(values_local, "shard", axis=0, tiled=True)
    piece_rows = key_piece.shape[0]
    back_block_rows = block_size()
    count_blocks = piece_rows // back_block_rows
    key_blocks = key_piece.reshape(count_blocks, back_block_rows, HEADS, HEAD)
    value_blocks = value_piece.reshape(count_blocks, back_block_rows, HEADS, HEAD)

    def back_block(running, blocks):
        grad_query = running
        key_block, value_block, block_index = blocks
        block_start = block_index * back_block_rows
        visible = visible_mask(allowed, seg_len, my_start, local_rows, block_start, back_block_rows)
        part_query, part_key, part_value = pair_terms(
            query_heads, grad_heads, log_sum, row_delta, key_block, value_block, visible
        )
        joined = jnp.concatenate(
            (
                part_key.reshape(back_block_rows, model_width),
                part_value.reshape(back_block_rows, model_width),
            ),
            axis=1,
        )
        return (grad_query + part_query, joined.astype(jnp.bfloat16))

    carried, key_terms = lax.scan(
        back_block, carried, (key_blocks, value_blocks, jnp.arange(count_blocks, dtype=jnp.int32))
    )
    grad_query = carried
    key_terms = key_terms.reshape(piece_rows, 2 * model_width)
    key_grads = lax.psum_scatter(key_terms, "shard", scatter_dimension=0, tiled=True)
    grad_qkv = jnp.concatenate(
        (grad_query.reshape(local_rows, model_width), key_grads), axis=1
    ).astype(jnp.bfloat16)
    grad_qkv_weight = t_times(entered, grad_qkv)
    grad_entered = times_t(grad_qkv, qkv_full)
    grad_gain_attn = jnp.sum(grad_entered * normed_one, axis=0)
    input_grad = grad_hidden + norm_back(
        grad_entered * attn_gain.astype(jnp.float32), normed_one, inv_one
    )
    group_sums = (
        lax.psum_scatter(grad_qkv_weight.astype(jnp.bfloat16), "shard", scatter_dimension=0, tiled=True),
        lax.psum_scatter(grad_out.astype(jnp.bfloat16), "shard", scatter_dimension=0, tiled=True),
        lax.psum_scatter(grad_up.astype(jnp.bfloat16), "shard", scatter_dimension=0, tiled=True),
        lax.psum_scatter(grad_down.astype(jnp.bfloat16), "shard", scatter_dimension=0, tiled=True),
        lax.psum_scatter(grad_gain_attn, "shard", scatter_dimension=0, tiled=True),
        lax.psum_scatter(grad_gain_ffn, "shard", scatter_dimension=0, tiled=True),
    )
    totals = (
        lax.psum(group_sums[0].astype(jnp.bfloat16), "rep").astype(jnp.float32),
        lax.psum(group_sums[1].astype(jnp.bfloat16), "rep").astype(jnp.float32),
        lax.psum(group_sums[2].astype(jnp.bfloat16), "rep").astype(jnp.float32),
        lax.psum(group_sums[3].astype(jnp.bfloat16), "rep").astype(jnp.float32),
        lax.psum(group_sums[4].astype(jnp.bfloat16), "rep").astype(jnp.float32),
        lax.psum(group_sums[5].astype(jnp.bfloat16), "rep").astype(jnp.float32),
    )
    return (output, input_grad, totals[0], totals[1], totals[2], totals[3], totals[4], totals[5])


MESH = pl.DeviceIdType.MESH


def ring_place(shard):
    return (1 - shard % 2) * (shard // 2) + (shard % 2) * (7 - shard // 2)


def ring_shard(place):
    upper = place // 4
    return (1 - upper) * 2 * place + upper * (15 - 2 * place)


def remote(source, target, sent, got, device):
    return pltpu.make_async_remote_copy(
        src_ref=source,
        dst_ref=target,
        send_sem=sent,
        recv_sem=got,
        device_id=device,
        device_id_type=MESH,
    )


def around(place, offset):
    return ring_shard(lax.rem(place + offset + 8, 8))


class Where:
    def __init__(self):
        self.rep = lax.axis_index("rep")
        self.me = lax.axis_index("shard")
        self.y = self.rep // 2
        self.core = self.rep % 2
        self.rep_y = (1 - self.y) * 2 + self.core
        self.rep_core = self.y * 2 + 1 - self.core
        self.rep_far = (1 - self.y) * 2 + 1 - self.core
        self.place = ring_place(self.me)
        self.right = around(self.place, 1)
        self.left = around(self.place, -1)

    def other(self, step):
        return lax.rem(self.me + step, 8)

    def back(self, step):
        return lax.rem(self.me + 8 - step, 8)

    def greet(self):
        barrier = pltpu.get_barrier_semaphore()
        for step in range(1, 8):
            pl.semaphore_signal(
                barrier, inc=1, device_id=(self.rep, self.other(step)), device_id_type=MESH
            )
        for rep in (self.rep_y, self.rep_core, self.rep_far):
            pl.semaphore_signal(barrier, inc=1, device_id=(rep, self.me), device_id_type=MESH)
        pl.semaphore_wait(barrier, 10)


def normed_rows(values):
    average = jnp.mean(values, axis=-1, keepdims=True)
    centered = values - average
    variance = jnp.mean(centered * centered, axis=-1, keepdims=True)
    inv_std = lax.rsqrt(variance + 1e-05)
    return (centered * inv_std, inv_std)


def gain_row(gains_ref, which):
    return jnp.concatenate(
        [gains_ref[s, which * 8 : which * 8 + 1, :] for s in range(8)], axis=1
    ).astype(jnp.float32)


def head_lanes(values, head):
    lane = lax.broadcasted_iota(jnp.int32, values.shape, 1)
    return jnp.where(lane // HEAD == head, values, jnp.zeros_like(values))


def tile_masks(block, parents_ref):
    key_row = lax.broadcasted_iota(jnp.int32, (256, 256), 0)
    query_row = lax.broadcasted_iota(jnp.int32, (256, 256), 1)
    own = key_row <= query_row
    if block < 5:
        return (own, None)
    own = own & (key_row // 128 == query_row // 128)
    if block == 5:
        return (own, None)
    parent = jnp.where(query_row < 128, parents_ref[2 * block], parents_ref[2 * block + 1])
    return (own, parent == 10 + key_row // 128)


def score_parts(block, keys_ref, queries, masks):
    own_mask, branch_mask = masks
    full = 256 * block if block < 5 else 1280
    spans = [(0, full, None)] if full else []
    if branch_mask is not None:
        spans.append((1280, 256, branch_mask))
    spans.append((256 * block, 256, own_mask))
    parts = []
    for first, rows, mask in spans:
        scores = times_t(keys_ref[pl.ds(first, rows), :], queries)
        if mask is not None:
            scores = jnp.where(mask, scores, masked_score)
        parts.append((first, rows, scores))
    return parts


def summed(*parts):
    total = parts[0].astype(jnp.float32)
    for part in parts[1:]:
        total = total + part.astype(jnp.float32)
    return total


BLOCK_ORDER = [4, 3, -3, 2, -2, 1, -1, 0]


def layer_kernel(
    ids_ref, parents_ref, tok_ref, cot_ref, gain_one_ref, gain_two_ref, qkv_w, out_w, up_w, down_w,
    layer_ref, in_ref, qkv_out, out_out, up_out, down_out, gain_out, ent_hbm,
    stage, gain_ref, wq_send, slices, gains_ref, tok_all, qkv_slots, qkv, side_t, tree_rows, slot_rows,
    mixed, logs, att, out_all, w_all, xch, acts, parts, gw, rr, rr_out, cr_out, yr_out,
    do_slots, dk, dv, gq_t, qs_core, qs_half, qs_recv, qs_y, fin_up, gp, gp_recv, gp_rep,
    load_s, small_s, small_r, slc_s, slc_r, tok_s, tok_r, o_s, o_r, oy_s, oy_r, oc_s, oc_r, w_s, w_r,
    keep_s, mix_s, mix_r, cot_s, cot_r, sec_s, sec_r, part_s, part_r, do_s, do_r,
    go_s, go_r, rs_s, rs_r, ro_s, ro_r, fin_s, fin_r, ge_s, ge_r, qs_s, qs_r, qr_s, qr_r,
    gp_s, gp_r, gr_s, gr_r,
):
    low, full = jnp.bfloat16, jnp.float32
    dq_t, gq_slots = mixed, qkv.reshape(8, 256, 384)
    at = Where()
    rep, me, y, core = at.rep, at.me, at.y, at.core
    ring_device = ((rep, at.right), (rep, at.left))
    over_y, over_core = (at.rep_y, me), (at.rep_core, me)
    places = []
    for seg in range(16):
        place = jnp.int32(0)
        for slot in range(1, 16):
            place = jnp.where(ids_ref[slot] == seg, slot, place)
        places.append(place)

    loads = [
        pltpu.make_async_copy(qkv_w.at[:, pl.ds(j * 1024, 1024)], stage.at[j], load_s.at[j])
        for j in range(3)
    ]
    loads.append(pltpu.make_async_copy(out_w, stage.at[3], load_s.at[3]))
    loads.append(
        pltpu.make_async_copy(down_w.at[pl.ds(rep * 128, 128), :], stage.at[5], load_s.at[4])
    )
    for s in range(8):
        columns = pl.ds(pl.multiple_of(s * 512 + rep * 128, 128), 128)
        loads.append(
            pltpu.make_async_copy(
                up_w.at[:, columns], stage.at[4, :, pl.ds(s * 128, 128)], load_s.at[5 + s]
            )
        )
    for copy in loads:
        copy.start()
    gain_ref[0:8, :] = jnp.broadcast_to(gain_one_ref[...], (8, 128)).astype(low)
    gain_ref[8:16, :] = jnp.broadcast_to(gain_two_ref[...], (8, 128)).astype(low)
    at.greet()

    def flow_block(flow, offset):
        return around(at.place, -offset if flow else offset)

    def token_copy(flow, step, half):
        origin = flow_block(flow, -step)
        source = tok_ref if step == 0 else tok_all.at[origin]
        rows = pl.ds(half * 128, 128)
        return remote(
            source.at[rows, :],
            tok_all.at[origin, rows, :],
            tok_s.at[flow, step, half],
            tok_r.at[flow, step, half],
            ring_device[flow],
        )

    def step_halves(step):
        if step == 3:
            return [(0, 0), (1, 1)]
        return [(half, flow) for half in range(2) for flow in range(2)]

    def out_copy(flow, step):
        spot = out_all.at[flow_block(flow, -step), rep]
        return remote(spot, spot, o_s.at[flow, step], o_r.at[flow, step], ring_device[flow])

    def out_flows(step):
        return (0, 1) if step < 3 else (0,)

    def out_over_y(flow, step):
        spot = out_all.at[flow_block(flow, -step - 1), rep]
        return remote(spot, spot, oy_s.at[flow, step], oy_r.at[flow, step], over_y)

    def out_over_core(flow, step, own):
        spot = out_all.at[flow_block(flow, -step - 1), rep if own else at.rep_y]
        return remote(spot, spot, oc_s.at[own, flow, step], oc_r.at[own, flow, step], over_core)

    def w_copy(flow, step, half):
        spot = w_all.at[flow_block(flow, -step), half]
        return remote(spot, spot, w_s.at[flow, step, half], w_r.at[flow, step, half], ring_device[flow])

    def w_half(step, half):
        for flow in range(2):
            if step == 3 and flow != half:
                continue
            w_copy(flow, step, half).wait_recv()
            if step < 2 or (step == 2 and half == flow):
                w_copy(flow, step + 1, half).start()

    small = [
        remote(
            gain_ref,
            gains_ref.at[me],
            small_s.at[0, step],
            small_r.at[0, step],
            (rep, at.other(step)),
        )
        for step in range(1, 8)
    ]
    small += [
        remote(
            wq_send.at[at.other(step), :, core],
            slices.at[me, :, core],
            small_s.at[1, step],
            small_r.at[1, step],
            (rep, at.other(step)),
        )
        for step in range(1, 8)
    ]
    slice_core = remote(
        slices.at[:, :, core], slices.at[:, :, core], slc_s.at[0], slc_r.at[0], over_core
    )
    cot_y = remote(cot_ref, xch.at[6], cot_s.at[0], cot_r.at[0], over_y)
    cot_core = remote(cot_ref, xch.at[5], cot_s.at[1], cot_r.at[1], over_core)
    cot_far = remote(xch.at[6], xch.at[7], cot_s.at[2], cot_r.at[2], over_core)

    for copy in small[:7]:
        copy.start()
    for half in range(2):
        for flow in range(2):
            token_copy(flow, 0, half).start()
    cot_y.start()
    cot_core.start()
    for copy in loads[:3]:
        copy.wait()
    for s in range(8):
        for j in range(3):
            wq_send[s, :, :, :, j * 128 : j * 128 + 128] = (
                stage[j, :, s * 128 : s * 128 + 128].astype(low).reshape(2, 2, 32, 128)
            )
    for copy in small[7:]:
        copy.start()
    gains_ref[me] = gain_ref[...]
    slices[me, :, core] = wq_send[me, :, core]
    loads[3].wait()
    out_all[me] = stage[3].astype(low).reshape(4, 32, 1024)
    for flow in range(2):
        out_copy(flow, 0).start()
    for copy in loads[4:]:
        copy.wait()
    w_all[me, 0] = stage[4].astype(low)
    w_all[me, 1] = stage[5].astype(low)
    xch[4] = cot_ref[...]
    kept = {}

    def enter(rows, origin, count):
        slot = 4 + count % 2
        if count > 1:
            kept[count - 2].wait()
        normed, _ = normed_rows(rows.astype(full))
        entered = (normed * gain).astype(low)
        parts[slot] = entered
        kept[count] = pltpu.make_async_copy(parts.at[slot], ent_hbm.at[origin], keep_s.at[slot - 4])
        kept[count].start()
        weights = slices[...].reshape(1024, 384)
        made = jnp.dot(entered, weights, preferred_element_type=full).astype(low)
        qkv_slots[2 * origin] = made[:128]
        qkv_slots[2 * origin + 1] = made[128:]

    def token_step(step):
        for half, flow in step_halves(step):
            token_copy(flow, step, half).wait_recv()
            if step < 2 or (step == 2 and half == flow):
                token_copy(flow, step + 1, half).start()
        for flow in out_flows(step):
            out_copy(flow, step).wait_recv()
            if step < 2 or (step == 2 and flow == 0):
                out_copy(flow, step + 1).start()
            out_over_y(flow, step).start()
            out_over_core(flow, step, 1).start()

    token_step(0)
    for copy in small:
        copy.wait_recv()
    slice_core.start()
    slice_core.wait_recv()
    gain = gain_row(gains_ref, 0)
    enter(tok_ref[...], me, 0)
    count = 1
    for step in range(4):
        if step > 0:
            token_step(step)
        if step == W_START:
            for flow in range(2):
                w_copy(flow, 0, 0).start()
        for flow in out_flows(step):
            origin = flow_block(flow, -step - 1)
            enter(tok_all[origin], origin, count)
            count += 1
    cot_y.wait_recv()
    cot_far.start()
    kept[6].wait()
    kept[7].wait()

    for seg in range(16):
        qkv[seg * 128 : seg * 128 + 128, :] = qkv_slots[places[seg]]
    for block in range(8):
        side_t[:, block * 256 : block * 256 + 256] = qkv[block * 256 : block * 256 + 256, 256:384].T

    for block in range(8):
        masks = tile_masks(block, parents_ref)
        rows = pl.ds(block * 256, 256)

        def one_head(head, unused):
            queries = head_lanes(qkv[rows, 0:128], head) * low(0.125)
            tiles = score_parts(block, qkv.at[:, pl.ds(128, 128)], queries, masks)
            top = None
            for _, _, scores in tiles:
                part = jnp.max(scores, axis=0, keepdims=True)
                top = part if top is None else jnp.maximum(top, part)
            total = None
            mix = None
            head_rows = pl.ds(pl.multiple_of(head * HEAD, HEAD), HEAD)
            for first, number, scores in tiles:
                weights = jnp.exp(scores - top)
                part = jnp.sum(weights, axis=0, keepdims=True)
                total = part if total is None else total + part
                term = jnp.dot(
                    side_t[head_rows, pl.ds(first, number)],
                    weights.astype(low),
                    preferred_element_type=full,
                )
                mix = term if mix is None else mix + term
            mixed[head_rows, block * 256 : block * 256 + 256] = mix / total
            logs[pl.ds(pl.multiple_of(head * 8, 8), 8), block * 256 : block * 256 + 256] = (
                jnp.broadcast_to(top + jnp.log(total), (8, 256))
            )
            return unused

        lax.fori_loop(0, 2, one_head, 0)
        tree = mixed[:, block * 256 : block * 256 + 256].T.astype(low)
        tree_rows[2 * block] = tree[:128]
        tree_rows[2 * block + 1] = tree[128:]
        if block in W_BLOCKS:
            w_half(W_BLOCKS.index(block), 0)

    for slot in range(16):
        slot_rows[slot // 2, (slot % 2) * 128 : (slot % 2) * 128 + 128, :] = tree_rows[
            ids_ref[slot]
        ]
    my_columns = pl.ds(pl.multiple_of(me * 128, 128), 128)
    mix_sends = [
        remote(
            slot_rows.at[at.other(step)],
            att.at[:, my_columns],
            mix_s.at[step],
            mix_r.at[step],
            (rep, at.other(step)),
        )
        for step in range(1, 8)
    ]
    for copy in mix_sends:
        copy.start()
    for flow in range(2):
        w_copy(flow, 0, 1).start()
    att[:, my_columns] = slot_rows[me]
    for step in range(4):
        for flow in out_flows(step):
            out_over_y(flow, step).wait_recv()
            out_over_core(flow, step, 0).start()
    for step in range(4):
        for flow in out_flows(step):
            out_over_core(flow, step, 1).wait_recv()
            out_over_core(flow, step, 0).wait_recv()
    w_half(3, 0)
    for copy in mix_sends:
        copy.wait_recv()
    w_half(0, 1)

    out_full = out_all[...].reshape(1024, 1024)
    hidden = tok_ref[...].astype(full) + jnp.dot(att[...], out_full, preferred_element_type=full)
    ffn_gain = gain_row(gains_ref, 1)
    normed_two, _ = normed_rows(hidden)
    xch[0] = (normed_two * ffn_gain).astype(low)
    sec_y = remote(xch.at[0], xch.at[2], sec_s.at[0], sec_r.at[0], over_y)
    sec_core = remote(xch.at[0], xch.at[1], sec_s.at[1], sec_r.at[1], over_core)
    sec_far = remote(xch.at[2], xch.at[3], sec_s.at[2], sec_r.at[2], over_core)
    sec_y.start()
    sec_core.start()
    stage[0] = hidden[:128]
    stage[1] = hidden[128:]
    for step in range(4):
        for half, flow in step_halves(step):
            token_copy(flow, step, half).wait_send()
    w_half(1, 1)

    up = w_all[:, 0].reshape(1024, 1024)

    def ffn(first):
        second = xch[first : first + 2].reshape(512, 1024)
        pre = jnp.dot(second, up, preferred_element_type=full)
        bell = 1.0 + lax.erf(pre * 0.7071067811865476)
        acts[first : first + 2] = (0.5 * pre * bell).astype(low).reshape(2, 2, 128, 1024)
        slope = 0.5 * bell + pre * jnp.exp(-0.5 * pre * pre) * 0.3989422804014327
        acts[4 + first : 6 + first] = slope.astype(low).reshape(2, 2, 128, 1024)

    def ffn_back(first):
        cots = xch[4 + first : 6 + first].reshape(512, 1024)
        grad_act = times_t(cots, w_all[:, 1].reshape(1024, 1024)).astype(low).astype(full)
        slope = acts[4 + first : 6 + first].reshape(512, 1024).astype(full)
        grad_pre = (grad_act * slope).astype(low)
        acts[4 + first : 6 + first] = grad_pre.reshape(2, 2, 128, 1024)
        return times_t(grad_pre, w_all[:, 0].reshape(1024, 1024))

    sec_core.wait_recv()
    ffn(0)
    w_half(2, 1)
    sec_y.wait_recv()
    sec_far.start()
    cot_core.wait_recv()
    cot_far.wait_recv()
    w_half(3, 1)
    sec_far.wait_recv()
    ffn(2)

    def part_copy(kind, leg):
        index = kind * 3 + leg
        return remote(
            tok_all.at[index],
            parts.at[index],
            part_s.at[index],
            part_r.at[index],
            over_y if leg == 1 else over_core,
        )

    def weight_grads(half, offsets):
        blocks = [around(at.place, offset) for offset in offsets]
        spans = [pl.ds(pl.multiple_of(block * 128, 128), 128) for block in blocks]
        if half == 0:
            sides, other = [xch[0:4, :, span].reshape(1024, 128).T for span in spans], acts
        else:
            sides, other = [acts[0:4, :, :, span].reshape(1024, 128).T for span in spans], xch
        made = jnp.dot(
            jnp.concatenate(sides, axis=0),
            other[4:8].reshape(1024, 1024),
            preferred_element_type=full,
        ).astype(low)
        for i, block in enumerate(blocks):
            gw[block, half] = made[i * 128 : i * 128 + 128]

    def rs_copy(flow, step, half):
        return remote(
            gw.at[flow_block(flow, 4 - step), half],
            rr.at[flow, step, half],
            rs_s.at[flow, step, half],
            rs_r.at[flow, step, half],
            ring_device[flow],
        )

    def rs_half(step, half):
        for flow in range(2):
            block = flow_block(flow, 4 - step)
            if step == 0 and half != flow:
                continue
            if step > 1 or (step == 1 and half == flow):
                rs_copy(flow, step - 1, half).wait_recv()
                gw[block, half] = summed(gw[block, half], rr[flow, step - 1, half]).astype(low)
            rs_copy(flow, step, half).start()

    grad_far = ffn_back(2)
    tok_all[0] = grad_far[256:].astype(low)
    part_copy(0, 0).start()
    stage[2] = grad_far[:128]
    stage[3] = grad_far[128:256]
    part_copy(0, 0).wait_recv()
    tok_all[1] = summed(stage[2:4].reshape(256, 1024), parts[0]).astype(low)
    part_copy(0, 1).start()
    weight_grads(1, [4, 3, -3])
    rs_half(0, 1)
    grad_near = ffn_back(0)
    tok_all[2] = grad_near[256:].astype(low)
    part_copy(0, 2).start()
    stage[2] = grad_near[:128]
    stage[3] = grad_near[128:256]

    rs_half(1, 1)

    def outputs(first):
        active = acts[first : first + 2].reshape(512, 1024)
        return jnp.dot(active, w_all[:, 1].reshape(1024, 1024), preferred_element_type=full)

    made = outputs(2)
    tok_all[3] = made[256:].astype(low)
    part_copy(1, 0).start()
    stage[4] = made[:128]
    stage[5] = made[128:256]
    part_copy(1, 0).wait_recv()
    tok_all[4] = summed(stage[4:6].reshape(256, 1024), parts[3]).astype(low)
    made = outputs(0)
    tok_all[5] = made[256:].astype(low)
    part_copy(1, 2).start()
    stage[0] = stage[0] + made[:128]
    stage[1] = stage[1] + made[128:256]
    part_copy(1, 1).start()

    for step in range(4):
        for half, flow in step_halves(step):
            w_copy(flow, step, half).wait_send()

    hidden = tok_ref[...].astype(full) + jnp.dot(
        att[...], out_all[...].reshape(1024, 1024), preferred_element_type=full
    )
    normed_two, inv_two = normed_rows(hidden)
    part_copy(0, 2).wait_recv()
    part_copy(0, 1).wait_recv()
    grad_second = summed(stage[2:4].reshape(256, 1024), parts[1], parts[2])
    gain_two = jnp.sum(grad_second * normed_two, axis=0, keepdims=True)
    for s in range(8):
        gp[s, 8:16, :] = jnp.broadcast_to(gain_two[:, s * 128 : s * 128 + 128], (8, 128))
    grad_hidden = cot_ref[...].astype(full) + norm_back(
        grad_second * gain_row(gains_ref, 1), normed_two, inv_two
    )
    stage[2] = grad_hidden[:128]
    stage[3] = grad_hidden[128:]
    grad_y = grad_hidden.astype(low)
    grad_attn = times_t(grad_y, out_all[...].reshape(1024, 1024)).astype(low)
    for copy in mix_sends:
        copy.wait_send()
    for s in range(8):
        slot_rows[s] = grad_attn[:, s * 128 : s * 128 + 128]
    do_sends = [
        remote(
            slot_rows.at[at.other(step)],
            do_slots.at[me],
            do_s.at[step],
            do_r.at[step],
            (rep, at.other(step)),
        )
        for step in range(1, 8)
    ]
    for copy in do_sends:
        copy.start()
    do_slots[me] = slot_rows[me]

    weight_grads(0, [4, 3, -3])
    rs_half(0, 0)
    weight_grads(1, [2, -2, 1, -1, 0])
    rs_half(2, 1)
    rs_half(1, 0)
    weight_grads(0, [2, -2, 1, -1, 0])

    for step in range(4):
        for flow in out_flows(step):
            out_copy(flow, step).wait_send()
            out_over_y(flow, step).wait_send()
            out_over_core(flow, step, 0).wait_send()
            out_over_core(flow, step, 1).wait_send()
    for block in range(8):
        out_all[block] = (
            jnp.dot(
                att[:, block * 128 : block * 128 + 128].T, grad_y, preferred_element_type=full
            )
            .astype(low)
            .reshape(4, 32, 1024)
        )
    outs = out_all
    go_core = [
        remote(
            outs.at[:, 2 * i + 1 - core], cr_out.at[:, i], go_s.at[i], go_r.at[i], over_core
        )
        for i in range(2)
    ]
    for copy in go_core:
        copy.start()
    for copy in (cot_y, cot_core, cot_far, sec_y, sec_core, sec_far):
        copy.wait_send()
    fetch = pltpu.make_async_copy(ent_hbm, xch, load_s.at[0])
    fetch.start()
    for copy in go_core:
        copy.wait_recv()
    outs[:, at.rep_y] = summed(outs[:, at.rep_y], cr_out[:, 1 - y]).astype(low)
    go_y = remote(outs.at[:, at.rep_y], yr_out, go_s.at[2], go_r.at[2], over_y)
    go_y.start()

    def ro_copy(flow, step):
        return remote(
            outs.at[flow_block(flow, 4 - step), rep],
            rr_out.at[flow, step],
            ro_s.at[flow, step],
            ro_r.at[flow, step],
            ring_device[flow],
        )

    def ro_flows(step):
        return (0, 1) if step else (0,)

    def ro_step(step):
        for flow in ro_flows(step):
            block = flow_block(flow, 4 - step)
            if step > 0 and flow in ro_flows(step - 1):
                ro_copy(flow, step - 1).wait_recv()
                outs[block, rep] = summed(outs[block, rep], rr_out[flow, step - 1]).astype(low)
            ro_copy(flow, step).start()

    for copy in do_sends:
        copy.wait_recv()
    for seg in range(16):
        tree_rows[seg] = do_slots.reshape(16, 128, 128)[places[seg]]
    for block in range(8):
        side_t[:, block * 256 : block * 256 + 256] = qkv[block * 256 : block * 256 + 256, 128:256].T
    dk[...] = jnp.zeros_like(dk)
    dv[...] = jnp.zeros_like(dv)

    for block in range(8):
        masks = tile_masks(block, parents_ref)
        rows = pl.ds(block * 256, 256)

        def one_head_back(head, unused):
            head_rows = pl.ds(pl.multiple_of(head * HEAD, HEAD), HEAD)
            queries = head_lanes(qkv[rows, 0:128], head) * low(0.125)
            grads = tree_rows[2 * block : 2 * block + 2].reshape(256, 128)
            grad_rows = head_lanes(grads, head)
            lse = logs[pl.ds(pl.multiple_of(head * 8, 8), 8), block * 256 : block * 256 + 256][0:1]
            both = grads.T.astype(full) * mixed[:, block * 256 : block * 256 + 256]
            delta = jnp.where(
                head == 0,
                jnp.sum(both[:HEAD], axis=0, keepdims=True),
                jnp.sum(both[HEAD:], axis=0, keepdims=True),
            )
            grad_query = None
            for first, number, scores in score_parts(
                block, qkv.at[:, pl.ds(128, 128)], queries, masks
            ):
                keys = pl.ds(first, number)
                weights = jnp.exp(scores - lse)
                grad_weights = times_t(qkv[keys, 256:384], grad_rows)
                grad_scores = (weights * (grad_weights - delta)).astype(low)
                dk[keys, :] += jnp.dot(grad_scores, queries, preferred_element_type=full)
                dv[keys, :] += jnp.dot(weights.astype(low), grad_rows, preferred_element_type=full)
                term = jnp.dot(side_t[head_rows, keys], grad_scores, preferred_element_type=full)
                grad_query = term if grad_query is None else grad_query + term
            dq_t[head_rows, block * 256 : block * 256 + 256] = grad_query * 0.125
            return unused

        lax.fori_loop(0, 2, one_head_back, 0)
        if block == 1:
            rs_half(3, 1)
        if block == 3:
            rs_half(2, 0)
        if block == 6:
            rs_half(3, 0)
        if block == 4:
            outs[:, rep] = summed(outs[:, rep], cr_out[:, y]).astype(low)
            go_y.wait_recv()
            outs[:, rep] = summed(outs[:, rep], yr_out[...]).astype(low)
            ro_step(0)
        if block == 7:
            ro_step(1)

    for seg in range(16):
        rows = pl.ds(seg * 128, 128)
        qkv_slots[seg, :, 0:128] = dq_t[:, seg * 128 : seg * 128 + 128].T.astype(low)
        qkv_slots[seg, :, 128:256] = dk[rows, :].astype(low)
        qkv_slots[seg, :, 256:384] = dv[rows, :].astype(low)
    for slot in range(16):
        gq_slots[slot // 2, (slot % 2) * 128 : (slot % 2) * 128 + 128, :] = qkv_slots[ids_ref[slot]]

    def ge_copy(flow, step, half):
        return remote(
            acts.at[flow * 4 + step, half],
            w_all.at[flow * 4 + step, half],
            ge_s.at[flow, step, half],
            ge_r.at[flow, step, half],
            ring_device[flow],
        )

    def ge_part(block):
        return times_t(gq_slots[block], slices[...].reshape(1024, 384))

    def ge_step(step):
        made = [ge_part(flow_block(flow, 4 - step)) for flow in range(2)]
        for half in range(2):
            for flow in range(2):
                if step == 0 and half != flow:
                    continue
                rows = made[flow][half * 128 : half * 128 + 128]
                if step > 1 or (step == 1 and half == flow):
                    ge_copy(flow, step - 1, half).wait_recv()
                    rows = rows + w_all[flow * 4 + step - 1, half].astype(full)
                acts[flow * 4 + step, half] = rows.astype(low)
                ge_copy(flow, step, half).start()

    ge_step(0)
    ro_step(2)
    for block in range(8):
        gq_t[:, block * 256 : block * 256 + 256] = gq_slots[block].T
    fetch.wait()
    for copy in small:
        copy.wait_send()
    for s in range(8):
        made = jnp.dot(
            gq_t[...],
            xch[:, :, s * 128 : s * 128 + 128].reshape(2048, 128),
            preferred_element_type=full,
        )
        wq_send[s] = made.T.astype(low).reshape(2, 2, 32, 384)
    qs_over_core = remote(wq_send.at[:, :, 1 - core], qs_core, qr_s.at[0], qr_r.at[0], over_core)
    qs_over_core.start()
    ge_step(1)
    qs_over_core.wait_recv()
    qs_half[...] = summed(wq_send[:, :, core], qs_core[...]).astype(low)
    qs_over_y = remote(qs_half.at[:, 1 - y], qs_y, qr_s.at[1], qr_r.at[1], over_y)
    qs_over_y.start()
    ro_step(3)
    ge_step(2)
    qs_over_y.wait_recv()
    qs_half[:, y] = summed(qs_half[:, y], qs_y[...]).astype(low)
    qs_sends = [
        remote(
            qs_half.at[at.other(step), y],
            qs_recv.at[me],
            qs_s.at[step],
            qs_r.at[step],
            (rep, at.other(step)),
        )
        for step in range(1, 8)
    ]
    for copy in qs_sends:
        copy.start()
    qs_recv[me] = qs_half[me, y]

    def final_copy(kind, leg):
        quarter = at.rep_y if leg == 2 else rep
        if kind == 0:
            spot = fin_up.at[quarter]
        elif kind == 1:
            spot = down_out.at[pl.ds(quarter * 128, 128), :]
        elif kind == 2:
            spot = out_out.at[pl.ds(quarter * 32, 32), :]
        else:
            spot = qkv_out.at[pl.ds(quarter * 32, 32), :]
        device = over_y if leg == 0 else over_core
        return remote(spot, spot, fin_s.at[kind, leg], fin_r.at[kind, leg], device)

    for half in range(2):
        for flow in range(2):
            rs_copy(flow, 3, half).wait_recv()
        total = summed(gw[me, half], rr[0, 3, half], rr[1, 3, half]).astype(low)
        if half == 0:
            fin_up[rep] = total
        else:
            down_out[pl.ds(rep * 128, 128), :] = total
        final_copy(half, 0).start()
        final_copy(half, 1).start()
    for flow in range(2):
        ro_copy(flow, 3).wait_recv()
    out_out[pl.ds(rep * 32, 32), :] = summed(outs[me, rep], rr_out[0, 3], rr_out[1, 3]).astype(low)
    final_copy(2, 0).start()
    final_copy(2, 1).start()
    ge_step(3)
    part_copy(1, 1).wait_recv()
    part_copy(1, 2).wait_recv()
    tok_all[6] = summed(stage[0:2].reshape(256, 1024), parts[4], parts[5]).astype(low)
    layer_write = pltpu.make_async_copy(tok_all.at[6], layer_ref, load_s.at[1])
    layer_write.start()
    for copy in qs_sends:
        copy.wait_recv()
    quarter_rows = pl.ds(rep * 32, 32)
    for s in range(8):
        total = qs_recv[s]
        for j in range(3):
            first = j * 1024 + s * 128
            qkv_out[quarter_rows, first : first + 128] = total[:, j * 128 : j * 128 + 128]
    final_copy(3, 0).start()
    final_copy(3, 1).start()
    for kind in range(4):
        final_copy(kind, 0).wait_recv()
        final_copy(kind, 2).start()

    grad_entered = ge_part(me)
    for flow in range(2):
        ge_copy(flow, 3, 0).wait_recv()
        ge_copy(flow, 3, 1).wait_recv()
        grad_entered = grad_entered + w_all[flow * 4 + 3].reshape(256, 1024).astype(full)
    normed, inv_std = normed_rows(tok_ref[...].astype(full))
    gain_one = jnp.sum(grad_entered * normed, axis=0, keepdims=True)
    for s in range(8):
        gp[s, 0:8, :] = jnp.broadcast_to(gain_one[:, s * 128 : s * 128 + 128], (8, 128))
    gain_sends = [
        remote(
            gp.at[at.other(step)],
            gp_recv.at[me],
            gp_s.at[step],
            gp_r.at[step],
            (rep, at.other(step)),
        )
        for step in range(1, 8)
    ]
    for copy in gain_sends:
        copy.start()
    gp_recv[me] = gp[me]
    in_grad = stage[2:4].reshape(256, 1024) + norm_back(
        grad_entered * gain_row(gains_ref, 0), normed, inv_std
    )
    stage[4] = in_grad[:128]
    stage[5] = in_grad[128:]
    in_write = pltpu.make_async_copy(stage.at[4:6], in_ref, load_s.at[2])
    in_write.start()
    for copy in gain_sends:
        copy.wait_recv()
    total = gp_recv[0]
    for s in range(1, 8):
        total = total + gp_recv[s]
    gp_rep[rep] = total
    rep_sends = [
        remote(gp_rep.at[rep], gp_rep.at[rep], gr_s.at[i], gr_r.at[i], (to, me))
        for i, to in enumerate((at.rep_y, at.rep_core, at.rep_far))
    ]
    for copy in rep_sends:
        copy.start()
    for kind in range(4):
        final_copy(kind, 1).wait_recv()
        final_copy(kind, 2).wait_recv()
    for quarter in range(4):
        for s in range(8):
            first = s * 512 + quarter * 128
            up_out[:, first : first + 128] = fin_up[quarter, :, s * 128 : s * 128 + 128]
    for copy in rep_sends:
        copy.wait()
    gain_out[...] = gp_rep[0] + gp_rep[1] + gp_rep[2] + gp_rep[3]

    layer_write.wait()
    in_write.wait()
    for kind in range(4):
        for leg in range(3):
            final_copy(kind, leg).wait_send()
    qs_over_y.wait_send()
    qs_over_core.wait_send()
    go_y.wait_send()
    for copy in go_core + qs_sends + gain_sends + do_sends:
        copy.wait_send()
    slice_core.wait_send()
    for kind in range(2):
        for leg in range(3):
            part_copy(kind, leg).wait_send()
    for step in range(4):
        for flow in range(2):
            for half in range(2):
                if step > 0 or half == flow:
                    ge_copy(flow, step, half).wait_send()
                    rs_copy(flow, step, half).wait_send()
        for flow in ro_flows(step):
            ro_copy(flow, step).wait_send()


def widen_kernel(*refs):
    for source, target in zip(refs[:6], refs[7:13]):
        target[...] = source[...].astype(target.dtype)
    refs[13][...] = refs[6][0:1, :]
    refs[14][...] = refs[6][8:9, :]


W_START = 2
W_BLOCKS = [0, 4, 7]


def fast_shards(
    tokens, cotangent, qkv_weight, out_weight, up_weight, down_weight, gain_attn, gain_ffn, parents, slot_ids
):
    low, full = jnp.bfloat16, jnp.float32
    smem = pl.BlockSpec(memory_space=pltpu.SMEM)
    vmem = pl.BlockSpec(memory_space=pltpu.VMEM)
    anywhere = pl.BlockSpec(memory_space=pl.ANY)

    def dma(*shape):
        return pltpu.SemaphoreType.DMA(shape)

    v = pltpu.VMEM
    scratch = [
        v((6, 128, 1024), full),
        v((16, 128), low),
        v((8, 2, 2, 32, 384), low),
        v((8, 2, 2, 32, 384), low),
        v((8, 16, 128), low),
        v((8, 256, 1024), low),
        v((16, 128, 384), low),
        v((2048, 384), low),
        v((128, 2048), low),
        v((16, 128, 128), low),
        v((8, 256, 128), low),
        v((128, 2048), full),
        v((16, 2048), full),
        v((256, 1024), low),
        v((8, 4, 32, 1024), low),
        v((8, 2, 128, 1024), low),
        v((8, 256, 1024), low),
        v((8, 2, 128, 1024), low),
        v((6, 256, 1024), low),
        v((8, 2, 128, 1024), low),
        v((2, 4, 2, 128, 1024), low),
        v((2, 4, 32, 1024), low),
        v((8, 2, 32, 1024), low),
        v((8, 32, 1024), low),
        v((8, 256, 128), low),
        v((2048, 128), full),
        v((2048, 128), full),
        v((384, 2048), low),
        v((8, 2, 32, 384), low),
        v((8, 2, 32, 384), low),
        v((8, 32, 384), low),
        v((8, 32, 384), low),
        v((4, 128, 1024), low),
        v((8, 16, 128), full),
        v((8, 16, 128), full),
        v((4, 16, 128), full),
        dma(13), dma(2, 8), dma(2, 8), dma(1), dma(1), dma(2, 4, 2), dma(2, 4, 2),
        dma(2, 4), dma(2, 4), dma(2, 4), dma(2, 4), dma(2, 2, 4), dma(2, 2, 4),
        dma(2, 4, 2), dma(2, 4, 2), dma(2), dma(8), dma(8), dma(3), dma(3), dma(3), dma(3),
        dma(6), dma(6), dma(8), dma(8), dma(3), dma(3), dma(2, 4, 2), dma(2, 4, 2),
        dma(2, 4), dma(2, 4), dma(4, 3), dma(4, 3), dma(2, 4, 2), dma(2, 4, 2), dma(8), dma(8),
        dma(2), dma(2), dma(8), dma(8), dma(3), dma(3),
    ]
    made = pl.pallas_call(
        layer_kernel,
        out_shape=[
            jax.ShapeDtypeStruct((256, 1024), low),
            jax.ShapeDtypeStruct((2, 128, 1024), full),
            jax.ShapeDtypeStruct((128, 3072), low),
            jax.ShapeDtypeStruct((128, 1024), low),
            jax.ShapeDtypeStruct((128, 4096), low),
            jax.ShapeDtypeStruct((512, 1024), low),
            jax.ShapeDtypeStruct((16, 128), full),
            jax.ShapeDtypeStruct((8, 256, 1024), low),
        ],
        in_specs=[smem] * 2 + [vmem] * 4 + [anywhere] * 4,
        out_specs=[anywhere] * 2 + [vmem] * 5 + [anywhere],
        scratch_shapes=scratch,
        compiler_params=pltpu.CompilerParams(
            collective_id=1, has_side_effects=True, vmem_limit_bytes=VMEM_LIMIT
        ),
    )(
        slot_ids, parents.reshape(16), tokens, cotangent, gain_attn.reshape(1, 128), gain_ffn.reshape(1, 128), qkv_weight, out_weight, up_weight,
        down_weight,
    )
    shapes = [(256, 1024), (256, 1024), (128, 3072), (128, 1024), (128, 4096), (512, 1024)]
    results = [made[0], made[1].reshape(256, 1024)] + list(made[2:7])

    def spec(shape):
        return pl.BlockSpec((shape[0] // 4, shape[1]), lambda i: (i, 0))

    gain_spec = pl.BlockSpec((1, 128), lambda i: (0, 0))
    last = pl.pallas_call(
        widen_kernel,
        grid=(4,),
        out_shape=[jax.ShapeDtypeStruct(shapes[0], low)]
        + [jax.ShapeDtypeStruct(shape, full) for shape in shapes[1:]]
        + [jax.ShapeDtypeStruct((1, 128), full)] * 2,
        in_specs=[spec(shape) for shape in shapes] + [pl.BlockSpec((16, 128), lambda i: (0, 0))],
        out_specs=[spec(shape) for shape in shapes] + [gain_spec] * 2,
    )(*results)
    return tuple(last[:6]) + (last[6].reshape(128), last[7].reshape(128))


VMEM_LIMIT = 61 * 2**20


def solution(mesh):
    in_specs = (
        P(("rep", "shard"), None),
        P(("rep", "shard"), None),
        P("shard", None),
        P("shard", None),
        P("shard", None),
        P("shard", None),
        P("shard"),
        P("shard"),
        P("rep", None),
        P("rep"),
    )
    out_specs = (
        P(("rep", "shard"), None),
        P(("rep", "shard"), None),
        P("shard", None),
        P("shard", None),
        P("shard", None),
        P("shard", None),
        P("shard"),
        P("shard"),
    )

    def fits(*args):
        shapes = [a.shape for a in args]
        return shapes[0] == (8192, 1024) and shapes[4] == (1024, 4096) and shapes[8] == (4, 16)

    small = mesh.shape["rep"] == 4 and mesh.shape["shard"] == 8

    def whole(*args):
        run = fast_shards if small and fits(*args) else shards
        return jax.shard_map(
            run, mesh=mesh, in_specs=in_specs, out_specs=out_specs, check_vma=False
        )(*args)

    return whole
```

```python
import jax
import jax.numpy as jnp
from jax import lax
from jax.experimental import pallas as pl
from jax.experimental.pallas import tpu as pltpu
from jax.sharding import PartitionSpec as P

HEADS = 16
HEAD = 64


masked_score = -1e30


def block_size():
    return 512


def normalize(values):
    average = jnp.mean(values, axis=-1, keepdims=True)
    centered = values - average
    variance = jnp.mean(centered * centered, axis=-1, keepdims=True)
    inv_std = lax.rsqrt(variance + 1e-05)
    return (centered * inv_std, inv_std)


def gelu_exact(values):
    return 0.5 * values * (1.0 + lax.erf(values * 0.7071067811865476))


def gelu_slope(values):
    return (
        0.5 * (1.0 + lax.erf(values * 0.7071067811865476))
        + values * jnp.exp(-0.5 * values * values) * 0.3989422804014327
    )


def norm_back(grad_normed, normed, inv_std):
    first_mean = jnp.mean(grad_normed, axis=-1, keepdims=True)
    second_mean = jnp.mean(grad_normed * normed, axis=-1, keepdims=True)
    return inv_std * (grad_normed - first_mean - normed * second_mean)


def times_t(left_side, right_side):
    return lax.dot_general(
        left_side, right_side, (((1,), (1,)), ((), ())), preferred_element_type=jnp.float32
    )


def t_times(left_side, right_side):
    return lax.dot_general(
        left_side, right_side, (((0,), (0,)), ((), ())), preferred_element_type=jnp.float32
    )


def exact_dot(left_side, right_side):
    return jnp.dot(
        left_side, right_side, precision=lax.Precision.HIGHEST, preferred_element_type=jnp.float32
    )


def slot_table(group_ids, parents):
    tree_segs = parents.shape[1]
    group_segs = group_ids.shape[0]
    seg_range = jnp.arange(tree_segs, dtype=jnp.int32)
    walker = seg_range[None, :]
    reached = walker[:, :, None] == seg_range[None, None, :]

    def climb(step_index, carried):
        walker_now, reached_now = carried
        walker_now = jnp.sum(
            jnp.where(walker_now[:, :, None] == seg_range[None, None, :], parents[:, None, :], 0),
            axis=2,
        )
        return (walker_now, reached_now | (walker_now[:, :, None] == seg_range[None, None, :]))

    walker, reached = lax.fori_loop(0, tree_segs, climb, (walker, reached))
    anc_flat = reached.reshape(group_segs, tree_segs).astype(jnp.float32)
    id_picks = (group_ids[:, None] == jnp.arange(group_segs, dtype=jnp.int32)[None, :]).astype(
        jnp.float32
    )
    seg_rows = exact_dot(id_picks, anc_flat)
    local_pick = ((group_ids % tree_segs)[:, None] == seg_range[None, :]).astype(jnp.float32)
    tree_of = group_ids // tree_segs
    same_tree = (tree_of[:, None] == tree_of[None, :]).astype(jnp.float32)
    return (
        lax.dot_general(
            seg_rows,
            local_pick,
            (((1,), (1,)), ((), ())),
            precision=lax.Precision.HIGHEST,
            preferred_element_type=jnp.float32,
        )
        * same_tree
    )


def visible_mask(allowed, seg_len, query_start, query_rows, key_start, key_rows):
    group_segs = allowed.shape[0]
    query_index = query_start + jnp.arange(query_rows, dtype=jnp.int32)
    key_index = key_start + jnp.arange(key_rows, dtype=jnp.int32)
    query_slot = query_index // seg_len
    key_slot = key_index // seg_len
    seg_range = jnp.arange(group_segs, dtype=jnp.int32)
    query_pick = (query_slot[:, None] == seg_range[None, :]).astype(jnp.float32)
    key_pick = (key_slot[:, None] == seg_range[None, :]).astype(jnp.float32)
    linked = (
        lax.dot_general(
            exact_dot(query_pick, allowed),
            key_pick,
            (((1,), (1,)), ((), ())),
            precision=lax.Precision.HIGHEST,
            preferred_element_type=jnp.float32,
        )
        > 0.5
    )
    return linked & (
        (query_slot[:, None] != key_slot[None, :]) | (key_index[None, :] <= query_index[:, None])
    )


def pair_terms(query_part, grad_part, stat_part, delta_part, key_part, value_part, visible):
    scores = (
        jnp.einsum("qhd,khd->qhk", query_part, key_part, preferred_element_type=jnp.float32) * 0.125
    )
    scores = jnp.where(visible[:, None, :], scores, masked_score)
    probs_full = jnp.exp(scores - stat_part[:, :, None])
    grad_probs = jnp.einsum(
        "qhd,khd->qhk", grad_part, value_part, preferred_element_type=jnp.float32
    )
    grad_scores = (probs_full * (grad_probs - delta_part[:, :, None])).astype(jnp.bfloat16)
    grad_query = None
    grad_key = None
    grad_value = None
    grad_query = (
        jnp.einsum("qhk,khd->qhd", grad_scores, key_part, preferred_element_type=jnp.float32)
        * 0.125
    )
    grad_key = (
        jnp.einsum("qhk,qhd->khd", grad_scores, query_part, preferred_element_type=jnp.float32)
        * 0.125
    )
    grad_value = jnp.einsum(
        "qhk,qhd->khd",
        probs_full.astype(jnp.bfloat16),
        grad_part,
        preferred_element_type=jnp.float32,
    )
    return (grad_query, grad_key, grad_value)


def shards(
    tokens,
    cotangent,
    qkv_weight,
    out_weight,
    up_weight,
    down_weight,
    gain_attn,
    gain_ffn,
    parents,
    slot_ids,
):
    local_rows = tokens.shape[0]
    model_width = tokens.shape[1]
    shard_count = lax.axis_size("shard")
    my_start = lax.axis_index("shard") * local_rows
    seg_len = local_rows * shard_count // slot_ids.shape[0]
    allowed = slot_table(slot_ids, parents)
    qkv_full, out_full, attn_gain = (
        lax.all_gather(qkv_weight.astype(jnp.bfloat16), "shard", axis=0, tiled=True),
        lax.all_gather(out_weight.astype(jnp.bfloat16), "shard", axis=0, tiled=True),
        lax.all_gather(gain_attn.astype(jnp.bfloat16), "shard", axis=0, tiled=True),
    )
    inputs = tokens.astype(jnp.float32)
    normed_one, inv_one = normalize(inputs)
    entered = (normed_one * attn_gain.astype(jnp.float32)).astype(jnp.bfloat16)
    qkv_all = jnp.dot(entered, qkv_full, preferred_element_type=jnp.float32).astype(jnp.bfloat16)
    queries = qkv_all[:, :model_width]
    keys_local = qkv_all[:, model_width : 2 * model_width]
    values_local = qkv_all[:, 2 * model_width :]
    query_heads = queries.reshape(local_rows, HEADS, HEAD)
    start_state = (
        jnp.full((local_rows, HEADS), masked_score, jnp.float32),
        jnp.zeros((local_rows, HEADS), jnp.float32),
        jnp.zeros((local_rows, HEADS, HEAD), jnp.float32),
    )
    carried = start_state
    key_piece = lax.all_gather(keys_local, "shard", axis=0, tiled=True)
    value_piece = lax.all_gather(values_local, "shard", axis=0, tiled=True)
    piece_rows = key_piece.shape[0]
    block_rows = block_size()
    count_blocks = piece_rows // block_rows
    key_blocks = key_piece.reshape(count_blocks, block_rows, HEADS, HEAD)
    value_blocks = value_piece.reshape(count_blocks, block_rows, HEADS, HEAD)

    def attend_block(running, blocks):
        key_block, value_block, block_index = blocks
        run_max, run_sum, run_acc = running
        visible = visible_mask(
            allowed, seg_len, my_start, local_rows, block_index * block_rows, block_rows
        )
        scores = (
            jnp.einsum("qhd,khd->qhk", query_heads, key_block, preferred_element_type=jnp.float32)
            * 0.125
        )
        scores = jnp.where(visible[:, None, :], scores, masked_score)
        new_max = jnp.maximum(run_max, jnp.max(scores, axis=2))
        rescale = jnp.exp(run_max - new_max)
        exp_scores = jnp.exp(scores - new_max[:, :, None])
        run_sum = run_sum * rescale + jnp.sum(exp_scores, axis=2)
        run_acc = run_acc * rescale[:, :, None] + jnp.einsum(
            "qhk,khd->qhd",
            exp_scores.astype(jnp.bfloat16),
            value_block,
            preferred_element_type=jnp.float32,
        )
        return ((new_max, run_sum, run_acc), None)

    carried, unused = lax.scan(
        attend_block, carried, (key_blocks, value_blocks, jnp.arange(count_blocks, dtype=jnp.int32))
    )
    run_max, run_sum, run_acc = carried
    attn_exact = run_acc / run_sum[:, :, None]
    log_sum = run_max + jnp.log(run_sum)
    attended = attn_exact.reshape(local_rows, model_width).astype(jnp.bfloat16)
    hidden = inputs + jnp.dot(attended, out_full, preferred_element_type=jnp.float32)
    up_full, down_full, ffn_gain = (
        lax.all_gather(up_weight.astype(jnp.bfloat16), "shard", axis=0, tiled=True),
        lax.all_gather(down_weight.astype(jnp.bfloat16), "shard", axis=0, tiled=True),
        lax.all_gather(gain_ffn.astype(jnp.bfloat16), "shard", axis=0, tiled=True),
    )
    normed_two, inv_two = normalize(hidden)
    second = (normed_two * ffn_gain.astype(jnp.float32)).astype(jnp.bfloat16)
    pre_act = jnp.dot(second, up_full, preferred_element_type=jnp.float32)
    active = gelu_exact(pre_act).astype(jnp.bfloat16)
    output = (hidden + jnp.dot(active, down_full, preferred_element_type=jnp.float32)).astype(
        jnp.bfloat16
    )
    up_full, down_full, ffn_gain = (
        lax.all_gather(up_weight.astype(jnp.bfloat16), "shard", axis=0, tiled=True),
        lax.all_gather(down_weight.astype(jnp.bfloat16), "shard", axis=0, tiled=True),
        lax.all_gather(gain_ffn.astype(jnp.bfloat16), "shard", axis=0, tiled=True),
    )
    qkv_full, out_full, attn_gain = (
        lax.all_gather(qkv_weight.astype(jnp.bfloat16), "shard", axis=0, tiled=True),
        lax.all_gather(out_weight.astype(jnp.bfloat16), "shard", axis=0, tiled=True),
        lax.all_gather(gain_attn.astype(jnp.bfloat16), "shard", axis=0, tiled=True),
    )
    grad_down = t_times(active, cotangent)
    grad_active = times_t(cotangent, down_full).astype(jnp.bfloat16)
    grad_pre = (grad_active.astype(jnp.float32) * gelu_slope(pre_act)).astype(jnp.bfloat16)
    grad_up = t_times(second, grad_pre)
    grad_second = times_t(grad_pre, up_full)
    grad_gain_ffn = jnp.sum(grad_second * normed_two, axis=0)
    grad_hidden = cotangent.astype(jnp.float32) + norm_back(
        grad_second * ffn_gain.astype(jnp.float32), normed_two, inv_two
    )
    grad_y = grad_hidden.astype(jnp.bfloat16)
    grad_out = t_times(attended, grad_y)
    grad_attn = times_t(grad_y, out_full).astype(jnp.bfloat16)
    grad_heads = grad_attn.reshape(local_rows, HEADS, HEAD)
    row_delta = jnp.sum(grad_heads.astype(jnp.float32) * attn_exact, axis=2)
    start_back = jnp.zeros((local_rows, HEADS, HEAD), jnp.float32)
    carried = start_back
    key_piece = lax.all_gather(keys_local, "shard", axis=0, tiled=True)
    value_piece = lax.all_gather(values_local, "shard", axis=0, tiled=True)
    piece_rows = key_piece.shape[0]
    back_block_rows = block_size()
    count_blocks = piece_rows // back_block_rows
    key_blocks = key_piece.reshape(count_blocks, back_block_rows, HEADS, HEAD)
    value_blocks = value_piece.reshape(count_blocks, back_block_rows, HEADS, HEAD)

    def back_block(running, blocks):
        grad_query = running
        key_block, value_block, block_index = blocks
        block_start = block_index * back_block_rows
        visible = visible_mask(allowed, seg_len, my_start, local_rows, block_start, back_block_rows)
        part_query, part_key, part_value = pair_terms(
            query_heads, grad_heads, log_sum, row_delta, key_block, value_block, visible
        )
        joined = jnp.concatenate(
            (
                part_key.reshape(back_block_rows, model_width),
                part_value.reshape(back_block_rows, model_width),
            ),
            axis=1,
        )
        return (grad_query + part_query, joined.astype(jnp.bfloat16))

    carried, key_terms = lax.scan(
        back_block, carried, (key_blocks, value_blocks, jnp.arange(count_blocks, dtype=jnp.int32))
    )
    grad_query = carried
    key_terms = key_terms.reshape(piece_rows, 2 * model_width)
    key_grads = lax.psum_scatter(key_terms, "shard", scatter_dimension=0, tiled=True)
    grad_qkv = jnp.concatenate(
        (grad_query.reshape(local_rows, model_width), key_grads), axis=1
    ).astype(jnp.bfloat16)
    grad_qkv_weight = t_times(entered, grad_qkv)
    grad_entered = times_t(grad_qkv, qkv_full)
    grad_gain_attn = jnp.sum(grad_entered * normed_one, axis=0)
    input_grad = grad_hidden + norm_back(
        grad_entered * attn_gain.astype(jnp.float32), normed_one, inv_one
    )
    group_sums = (
        lax.psum_scatter(grad_qkv_weight.astype(jnp.bfloat16), "shard", scatter_dimension=0, tiled=True),
        lax.psum_scatter(grad_out.astype(jnp.bfloat16), "shard", scatter_dimension=0, tiled=True),
        lax.psum_scatter(grad_up.astype(jnp.bfloat16), "shard", scatter_dimension=0, tiled=True),
        lax.psum_scatter(grad_down.astype(jnp.bfloat16), "shard", scatter_dimension=0, tiled=True),
        lax.psum_scatter(grad_gain_attn, "shard", scatter_dimension=0, tiled=True),
        lax.psum_scatter(grad_gain_ffn, "shard", scatter_dimension=0, tiled=True),
    )
    totals = (
        lax.psum(group_sums[0].astype(jnp.bfloat16), "rep").astype(jnp.float32),
        lax.psum(group_sums[1].astype(jnp.bfloat16), "rep").astype(jnp.float32),
        lax.psum(group_sums[2].astype(jnp.bfloat16), "rep").astype(jnp.float32),
        lax.psum(group_sums[3].astype(jnp.bfloat16), "rep").astype(jnp.float32),
        lax.psum(group_sums[4].astype(jnp.bfloat16), "rep").astype(jnp.float32),
        lax.psum(group_sums[5].astype(jnp.bfloat16), "rep").astype(jnp.float32),
    )
    return (output, input_grad, totals[0], totals[1], totals[2], totals[3], totals[4], totals[5])


MESH = pl.DeviceIdType.MESH


def ring_place(shard):
    return (1 - shard % 2) * (shard // 2) + (shard % 2) * (7 - shard // 2)


def ring_shard(place):
    upper = place // 4
    return (1 - upper) * 2 * place + upper * (15 - 2 * place)


def remote(source, target, sent, got, device):
    return pltpu.make_async_remote_copy(
        src_ref=source,
        dst_ref=target,
        send_sem=sent,
        recv_sem=got,
        device_id=device,
        device_id_type=MESH,
    )


def around(place, offset):
    return ring_shard(lax.rem(place + offset + 8, 8))


class Where:
    def __init__(self):
        self.rep = lax.axis_index("rep")
        self.me = lax.axis_index("shard")
        self.y = self.rep // 2
        self.core = self.rep % 2
        self.rep_y = (1 - self.y) * 2 + self.core
        self.rep_core = self.y * 2 + 1 - self.core
        self.rep_far = (1 - self.y) * 2 + 1 - self.core
        self.place = ring_place(self.me)
        self.right = around(self.place, 1)
        self.left = around(self.place, -1)

    def other(self, step):
        return lax.rem(self.me + step, 8)

    def back(self, step):
        return lax.rem(self.me + 8 - step, 8)

    def greet(self):
        barrier = pltpu.get_barrier_semaphore()
        for step in range(1, 8):
            pl.semaphore_signal(
                barrier, inc=1, device_id=(self.rep, self.other(step)), device_id_type=MESH
            )
        for rep in (self.rep_y, self.rep_core, self.rep_far):
            pl.semaphore_signal(barrier, inc=1, device_id=(rep, self.me), device_id_type=MESH)
        pl.semaphore_wait(barrier, 10)


def normed_rows(values):
    average = jnp.mean(values, axis=-1, keepdims=True)
    centered = values - average
    variance = jnp.mean(centered * centered, axis=-1, keepdims=True)
    inv_std = lax.rsqrt(variance + 1e-05)
    return (centered * inv_std, inv_std)


def gain_row(gains_ref, which):
    return jnp.concatenate(
        [gains_ref[s, which * 8 : which * 8 + 1, :] for s in range(8)], axis=1
    ).astype(jnp.float32)


def head_lanes(values, head):
    lane = lax.broadcasted_iota(jnp.int32, values.shape, 1)
    return jnp.where(lane // HEAD == head, values, jnp.zeros_like(values))


def tile_masks(block, parents_ref):
    key_row = lax.broadcasted_iota(jnp.int32, (256, 256), 0)
    query_row = lax.broadcasted_iota(jnp.int32, (256, 256), 1)
    own = key_row <= query_row
    if block < 5:
        return (own, None)
    own = own & (key_row // 128 == query_row // 128)
    if block == 5:
        return (own, None)
    parent = jnp.where(query_row < 128, parents_ref[2 * block], parents_ref[2 * block + 1])
    return (own, parent == 10 + key_row // 128)


def score_parts(block, keys_ref, queries, masks):
    own_mask, branch_mask = masks
    full = 256 * block if block < 5 else 1280
    spans = [(0, full, None)] if full else []
    if branch_mask is not None:
        spans.append((1280, 256, branch_mask))
    spans.append((256 * block, 256, own_mask))
    parts = []
    for first, rows, mask in spans:
        scores = times_t(keys_ref[pl.ds(first, rows), :], queries)
        if mask is not None:
            scores = jnp.where(mask, scores, masked_score)
        parts.append((first, rows, scores))
    return parts


def summed(*parts):
    total = parts[0].astype(jnp.float32)
    for part in parts[1:]:
        total = total + part.astype(jnp.float32)
    return total


BLOCK_ORDER = [4, 3, -3, 2, -2, 1, -1, 0]


def layer_kernel(
    ids_ref, parents_ref, tok_ref, cot_ref, gain_one_ref, gain_two_ref, qkv_w, out_w, up_w, down_w,
    layer_ref, in_ref, qkv_out, out_out, up_out, down_out, gain_out, ent_hbm,
    stage, gain_ref, wq_send, slices, gains_ref, tok_all, qkv_slots, qkv, side_t, tree_rows, slot_rows,
    mixed, logs, att, out_all, w_all, xch, acts, parts, gw, rr, rr_out, cr_out, yr_out,
    do_slots, dk, dv, gq_t, qs_core, qs_half, qs_recv, qs_y, fin_up, gp, gp_recv, gp_rep,
    load_s, small_s, small_r, slc_s, slc_r, tok_s, tok_r, o_s, o_r, oy_s, oy_r, oc_s, oc_r, w_s, w_r,
    keep_s, mix_s, mix_r, cot_s, cot_r, sec_s, sec_r, part_s, part_r, do_s, do_r,
    go_s, go_r, rs_s, rs_r, ro_s, ro_r, fin_s, fin_r, ge_s, ge_r, qs_s, qs_r, qr_s, qr_r,
    gp_s, gp_r, gr_s, gr_r,
):
    low, full = jnp.bfloat16, jnp.float32
    dq_t, gq_slots = mixed, qkv.reshape(8, 256, 384)
    at = Where()
    rep, me, y, core = at.rep, at.me, at.y, at.core
    ring_device = ((rep, at.right), (rep, at.left))
    over_y, over_core = (at.rep_y, me), (at.rep_core, me)
    places = []
    for seg in range(16):
        place = jnp.int32(0)
        for slot in range(1, 16):
            place = jnp.where(ids_ref[slot] == seg, slot, place)
        places.append(place)

    loads = [
        pltpu.make_async_copy(qkv_w.at[:, pl.ds(j * 1024, 1024)], stage.at[j], load_s.at[j])
        for j in range(3)
    ]
    loads.append(pltpu.make_async_copy(out_w, stage.at[3], load_s.at[3]))
    loads.append(
        pltpu.make_async_copy(down_w.at[pl.ds(rep * 128, 128), :], stage.at[5], load_s.at[4])
    )
    for s in range(8):
        columns = pl.ds(pl.multiple_of(s * 512 + rep * 128, 128), 128)
        loads.append(
            pltpu.make_async_copy(
                up_w.at[:, columns], stage.at[4, :, pl.ds(s * 128, 128)], load_s.at[5 + s]
            )
        )
    for copy in loads:
        copy.start()
    gain_ref[0:8, :] = jnp.broadcast_to(gain_one_ref[...], (8, 128)).astype(low)
    gain_ref[8:16, :] = jnp.broadcast_to(gain_two_ref[...], (8, 128)).astype(low)
    at.greet()

    def flow_block(flow, offset):
        return around(at.place, -offset if flow else offset)

    def token_copy(flow, step, half):
        origin = flow_block(flow, -step)
        source = tok_ref if step == 0 else tok_all.at[origin]
        rows = pl.ds(half * 128, 128)
        return remote(
            source.at[rows, :],
            tok_all.at[origin, rows, :],
            tok_s.at[flow, step, half],
            tok_r.at[flow, step, half],
            ring_device[flow],
        )

    def step_halves(step):
        if step == 3:
            return [(0, 0), (1, 1)]
        return [(half, flow) for half in range(2) for flow in range(2)]

    def out_copy(flow, step):
        spot = out_all.at[flow_block(flow, -step), rep]
        return remote(spot, spot, o_s.at[flow, step], o_r.at[flow, step], ring_device[flow])

    def out_flows(step):
        return (0, 1) if step < 3 else (0,)

    def out_over_y(flow, step):
        spot = out_all.at[flow_block(flow, -step - 1), rep]
        return remote(spot, spot, oy_s.at[flow, step], oy_r.at[flow, step], over_y)

    def out_over_core(flow, step, own):
        spot = out_all.at[flow_block(flow, -step - 1), rep if own else at.rep_y]
        return remote(spot, spot, oc_s.at[own, flow, step], oc_r.at[own, flow, step], over_core)

    def w_copy(flow, step, half):
        spot = w_all.at[flow_block(flow, -step), half]
        return remote(spot, spot, w_s.at[flow, step, half], w_r.at[flow, step, half], ring_device[flow])

    def w_half(step, half):
        for flow in range(2):
            if step == 3 and flow != half:
                continue
            w_copy(flow, step, half).wait_recv()
            if step < 2 or (step == 2 and half == flow):
                w_copy(flow, step + 1, half).start()

    small = [
        remote(
            gain_ref,
            gains_ref.at[me],
            small_s.at[0, step],
            small_r.at[0, step],
            (rep, at.other(step)),
        )
        for step in range(1, 8)
    ]
    small += [
        remote(
            wq_send.at[at.other(step), :, core],
            slices.at[me, :, core],
            small_s.at[1, step],
            small_r.at[1, step],
            (rep, at.other(step)),
        )
        for step in range(1, 8)
    ]
    slice_core = remote(
        slices.at[:, :, core], slices.at[:, :, core], slc_s.at[0], slc_r.at[0], over_core
    )
    cot_y = remote(cot_ref, xch.at[6], cot_s.at[0], cot_r.at[0], over_y)
    cot_core = remote(cot_ref, xch.at[5], cot_s.at[1], cot_r.at[1], over_core)
    cot_far = remote(xch.at[6], xch.at[7], cot_s.at[2], cot_r.at[2], over_core)

    for copy in small[:7]:
        copy.start()
    for half in range(2):
        for flow in range(2):
            token_copy(flow, 0, half).start()
    cot_y.start()
    cot_core.start()
    for copy in loads[:3]:
        copy.wait()
    for s in range(8):
        for j in range(3):
            wq_send[s, :, :, :, j * 128 : j * 128 + 128] = (
                stage[j, :, s * 128 : s * 128 + 128].astype(low).reshape(2, 2, 32, 128)
            )
    for copy in small[7:]:
        copy.start()
    gains_ref[me] = gain_ref[...]
    slices[me, :, core] = wq_send[me, :, core]
    loads[3].wait()
    out_all[me] = stage[3].astype(low).reshape(4, 32, 1024)
    for flow in range(2):
        out_copy(flow, 0).start()
    for copy in loads[4:]:
        copy.wait()
    w_all[me, 0] = stage[4].astype(low)
    w_all[me, 1] = stage[5].astype(low)
    xch[4] = cot_ref[...]
    kept = {}

    def enter(rows, origin, count):
        slot = 4 + count % 2
        if count > 1:
            kept[count - 2].wait()
        normed, _ = normed_rows(rows.astype(full))
        entered = (normed * gain).astype(low)
        parts[slot] = entered
        kept[count] = pltpu.make_async_copy(parts.at[slot], ent_hbm.at[origin], keep_s.at[slot - 4])
        kept[count].start()
        weights = slices[...].reshape(1024, 384)
        made = jnp.dot(entered, weights, preferred_element_type=full).astype(low)
        qkv_slots[2 * origin] = made[:128]
        qkv_slots[2 * origin + 1] = made[128:]

    def token_step(step):
        for half, flow in step_halves(step):
            token_copy(flow, step, half).wait_recv()
            if step < 2 or (step == 2 and half == flow):
                token_copy(flow, step + 1, half).start()
        for flow in out_flows(step):
            out_copy(flow, step).wait_recv()
            if step < 2 or (step == 2 and flow == 0):
                out_copy(flow, step + 1).start()
            out_over_y(flow, step).start()
            out_over_core(flow, step, 1).start()

    token_step(0)
    for copy in small:
        copy.wait_recv()
    slice_core.start()
    slice_core.wait_recv()
    gain = gain_row(gains_ref, 0)
    enter(tok_ref[...], me, 0)
    count = 1
    for step in range(4):
        if step > 0:
            token_step(step)
        if step == W_START:
            for flow in range(2):
                w_copy(flow, 0, 0).start()
        for flow in out_flows(step):
            origin = flow_block(flow, -step - 1)
            enter(tok_all[origin], origin, count)
            count += 1
    cot_y.wait_recv()
    cot_far.start()
    kept[6].wait()
    kept[7].wait()

    for seg in range(16):
        qkv[seg * 128 : seg * 128 + 128, :] = qkv_slots[places[seg]]
    for block in range(8):
        side_t[:, block * 256 : block * 256 + 256] = qkv[block * 256 : block * 256 + 256, 256:384].T

    for block in range(8):
        masks = tile_masks(block, parents_ref)
        rows = pl.ds(block * 256, 256)

        def one_head(head, unused):
            queries = head_lanes(qkv[rows, 0:128], head) * low(0.125)
            tiles = score_parts(block, qkv.at[:, pl.ds(128, 128)], queries, masks)
            top = None
            for _, _, scores in tiles:
                part = jnp.max(scores, axis=0, keepdims=True)
                top = part if top is None else jnp.maximum(top, part)
            total = None
            mix = None
            head_rows = pl.ds(pl.multiple_of(head * HEAD, HEAD), HEAD)
            for first, number, scores in tiles:
                weights = jnp.exp(scores - top)
                part = jnp.sum(weights, axis=0, keepdims=True)
                total = part if total is None else total + part
                term = jnp.dot(
                    side_t[head_rows, pl.ds(first, number)],
                    weights.astype(low),
                    preferred_element_type=full,
                )
                mix = term if mix is None else mix + term
            mixed[head_rows, block * 256 : block * 256 + 256] = mix / total
            logs[pl.ds(pl.multiple_of(head * 8, 8), 8), block * 256 : block * 256 + 256] = (
                jnp.broadcast_to(top + jnp.log(total), (8, 256))
            )
            return unused

        lax.fori_loop(0, 2, one_head, 0)
        tree = mixed[:, block * 256 : block * 256 + 256].T.astype(low)
        tree_rows[2 * block] = tree[:128]
        tree_rows[2 * block + 1] = tree[128:]
        if block in W_BLOCKS:
            w_half(W_BLOCKS.index(block), 0)

    for slot in range(16):
        slot_rows[slot // 2, (slot % 2) * 128 : (slot % 2) * 128 + 128, :] = tree_rows[
            ids_ref[slot]
        ]
    my_columns = pl.ds(pl.multiple_of(me * 128, 128), 128)
    mix_sends = [
        remote(
            slot_rows.at[at.other(step)],
            att.at[:, my_columns],
            mix_s.at[step],
            mix_r.at[step],
            (rep, at.other(step)),
        )
        for step in range(1, 8)
    ]
    for copy in mix_sends:
        copy.start()
    for flow in range(2):
        w_copy(flow, 0, 1).start()
    att[:, my_columns] = slot_rows[me]
    for step in range(4):
        for flow in out_flows(step):
            out_over_y(flow, step).wait_recv()
            out_over_core(flow, step, 0).start()
    for step in range(4):
        for flow in out_flows(step):
            out_over_core(flow, step, 1).wait_recv()
            out_over_core(flow, step, 0).wait_recv()
    w_half(3, 0)
    for copy in mix_sends:
        copy.wait_recv()
    w_half(0, 1)

    out_full = out_all[...].reshape(1024, 1024)
    hidden = tok_ref[...].astype(full) + jnp.dot(att[...], out_full, preferred_element_type=full)
    ffn_gain = gain_row(gains_ref, 1)
    normed_two, _ = normed_rows(hidden)
    xch[0] = (normed_two * ffn_gain).astype(low)
    sec_y = remote(xch.at[0], xch.at[2], sec_s.at[0], sec_r.at[0], over_y)
    sec_core = remote(xch.at[0], xch.at[1], sec_s.at[1], sec_r.at[1], over_core)
    sec_far = remote(xch.at[2], xch.at[3], sec_s.at[2], sec_r.at[2], over_core)
    sec_y.start()
    sec_core.start()
    stage[0] = hidden[:128]
    stage[1] = hidden[128:]
    for step in range(4):
        for half, flow in step_halves(step):
            token_copy(flow, step, half).wait_send()
    w_half(1, 1)

    up = w_all[:, 0].reshape(1024, 1024)

    def ffn(first):
        second = xch[first : first + 2].reshape(512, 1024)
        pre = jnp.dot(second, up, preferred_element_type=full)
        bell = 1.0 + lax.erf(pre * 0.7071067811865476)
        acts[first : first + 2] = (0.5 * pre * bell).astype(low).reshape(2, 2, 128, 1024)
        slope = 0.5 * bell + pre * jnp.exp(-0.5 * pre * pre) * 0.3989422804014327
        acts[4 + first : 6 + first] = slope.astype(low).reshape(2, 2, 128, 1024)

    def ffn_back(first):
        cots = xch[4 + first : 6 + first].reshape(512, 1024)
        grad_act = times_t(cots, w_all[:, 1].reshape(1024, 1024)).astype(low).astype(full)
        slope = acts[4 + first : 6 + first].reshape(512, 1024).astype(full)
        grad_pre = (grad_act * slope).astype(low)
        acts[4 + first : 6 + first] = grad_pre.reshape(2, 2, 128, 1024)
        return times_t(grad_pre, w_all[:, 0].reshape(1024, 1024))

    sec_core.wait_recv()
    ffn(0)
    w_half(2, 1)
    sec_y.wait_recv()
    sec_far.start()
    cot_core.wait_recv()
    cot_far.wait_recv()
    w_half(3, 1)
    sec_far.wait_recv()
    ffn(2)

    def part_copy(kind, leg):
        index = kind * 3 + leg
        return remote(
            tok_all.at[index],
            parts.at[index],
            part_s.at[index],
            part_r.at[index],
            over_y if leg == 1 else over_core,
        )

    def weight_grads(half, offsets):
        blocks = [around(at.place, offset) for offset in offsets]
        spans = [pl.ds(pl.multiple_of(block * 128, 128), 128) for block in blocks]
        if half == 0:
            sides, other = [xch[0:4, :, span].reshape(1024, 128).T for span in spans], acts
        else:
            sides, other = [acts[0:4, :, :, span].reshape(1024, 128).T for span in spans], xch
        made = jnp.dot(
            jnp.concatenate(sides, axis=0),
            other[4:8].reshape(1024, 1024),
            preferred_element_type=full,
        ).astype(low)
        for i, block in enumerate(blocks):
            gw[block, half] = made[i * 128 : i * 128 + 128]

    def rs_copy(flow, step, half):
        return remote(
            gw.at[flow_block(flow, 4 - step), half],
            rr.at[flow, step, half],
            rs_s.at[flow, step, half],
            rs_r.at[flow, step, half],
            ring_device[flow],
        )

    def rs_half(step, half):
        for flow in range(2):
            block = flow_block(flow, 4 - step)
            if step == 0 and half != flow:
                continue
            if step > 1 or (step == 1 and half == flow):
                rs_copy(flow, step - 1, half).wait_recv()
                gw[block, half] = summed(gw[block, half], rr[flow, step - 1, half]).astype(low)
            rs_copy(flow, step, half).start()

    grad_far = ffn_back(2)
    tok_all[0] = grad_far[256:].astype(low)
    part_copy(0, 0).start()
    stage[2] = grad_far[:128]
    stage[3] = grad_far[128:256]
    part_copy(0, 0).wait_recv()
    tok_all[1] = summed(stage[2:4].reshape(256, 1024), parts[0]).astype(low)
    part_copy(0, 1).start()
    weight_grads(1, [4, 3, -3])
    rs_half(0, 1)
    grad_near = ffn_back(0)
    tok_all[2] = grad_near[256:].astype(low)
    part_copy(0, 2).start()
    stage[2] = grad_near[:128]
    stage[3] = grad_near[128:256]

    weight_grads(0, [4, 3, -3])
    rs_half(0, 0)
    rs_half(1, 1)

    def outputs(first):
        active = acts[first : first + 2].reshape(512, 1024)
        return jnp.dot(active, w_all[:, 1].reshape(1024, 1024), preferred_element_type=full)

    made = outputs(2)
    tok_all[3] = made[256:].astype(low)
    part_copy(1, 0).start()
    stage[4] = made[:128]
    stage[5] = made[128:256]
    part_copy(1, 0).wait_recv()
    tok_all[4] = summed(stage[4:6].reshape(256, 1024), parts[3]).astype(low)
    made = outputs(0)
    tok_all[5] = made[256:].astype(low)
    part_copy(1, 2).start()
    stage[0] = stage[0] + made[:128]
    stage[1] = stage[1] + made[128:256]
    part_copy(1, 1).start()

    for step in range(4):
        for half, flow in step_halves(step):
            w_copy(flow, step, half).wait_send()

    hidden = tok_ref[...].astype(full) + jnp.dot(
        att[...], out_all[...].reshape(1024, 1024), preferred_element_type=full
    )
    normed_two, inv_two = normed_rows(hidden)
    part_copy(0, 2).wait_recv()
    part_copy(0, 1).wait_recv()
    grad_second = summed(stage[2:4].reshape(256, 1024), parts[1], parts[2])
    gain_two = jnp.sum(grad_second * normed_two, axis=0, keepdims=True)
    for s in range(8):
        gp[s, 8:16, :] = jnp.broadcast_to(gain_two[:, s * 128 : s * 128 + 128], (8, 128))
    grad_hidden = cot_ref[...].astype(full) + norm_back(
        grad_second * gain_row(gains_ref, 1), normed_two, inv_two
    )
    stage[2] = grad_hidden[:128]
    stage[3] = grad_hidden[128:]
    grad_y = grad_hidden.astype(low)
    grad_attn = times_t(grad_y, out_all[...].reshape(1024, 1024)).astype(low)
    for copy in mix_sends:
        copy.wait_send()
    for s in range(8):
        slot_rows[s] = grad_attn[:, s * 128 : s * 128 + 128]
    do_sends = [
        remote(
            slot_rows.at[at.other(step)],
            do_slots.at[me],
            do_s.at[step],
            do_r.at[step],
            (rep, at.other(step)),
        )
        for step in range(1, 8)
    ]
    for copy in do_sends:
        copy.start()
    do_slots[me] = slot_rows[me]

    weight_grads(1, [2, -2, 1, -1, 0])
    rs_half(2, 1)
    rs_half(1, 0)
    weight_grads(0, [2, -2, 1, -1, 0])

    for step in range(4):
        for flow in out_flows(step):
            out_copy(flow, step).wait_send()
            out_over_y(flow, step).wait_send()
            out_over_core(flow, step, 0).wait_send()
            out_over_core(flow, step, 1).wait_send()
    for block in range(8):
        out_all[block] = (
            jnp.dot(
                att[:, block * 128 : block * 128 + 128].T, grad_y, preferred_element_type=full
            )
            .astype(low)
            .reshape(4, 32, 1024)
        )
    outs = out_all
    go_core = [
        remote(
            outs.at[:, 2 * i + 1 - core], cr_out.at[:, i], go_s.at[i], go_r.at[i], over_core
        )
        for i in range(2)
    ]
    for copy in go_core:
        copy.start()
    for copy in (cot_y, cot_core, cot_far, sec_y, sec_core, sec_far):
        copy.wait_send()
    fetch = pltpu.make_async_copy(ent_hbm, xch, load_s.at[0])
    fetch.start()
    for copy in go_core:
        copy.wait_recv()
    outs[:, at.rep_y] = summed(outs[:, at.rep_y], cr_out[:, 1 - y]).astype(low)
    go_y = remote(outs.at[:, at.rep_y], yr_out, go_s.at[2], go_r.at[2], over_y)
    go_y.start()

    def ro_copy(flow, step):
        return remote(
            outs.at[flow_block(flow, 4 - step), rep],
            rr_out.at[flow, step],
            ro_s.at[flow, step],
            ro_r.at[flow, step],
            ring_device[flow],
        )

    def ro_flows(step):
        return (0, 1) if step else (0,)

    def ro_step(step):
        for flow in ro_flows(step):
            block = flow_block(flow, 4 - step)
            if step > 0 and flow in ro_flows(step - 1):
                ro_copy(flow, step - 1).wait_recv()
                outs[block, rep] = summed(outs[block, rep], rr_out[flow, step - 1]).astype(low)
            ro_copy(flow, step).start()

    rs_half(3, 1)

    for copy in do_sends:
        copy.wait_recv()
    for seg in range(16):
        tree_rows[seg] = do_slots.reshape(16, 128, 128)[places[seg]]
    for block in range(8):
        side_t[:, block * 256 : block * 256 + 256] = qkv[block * 256 : block * 256 + 256, 128:256].T
    dk[...] = jnp.zeros_like(dk)
    dv[...] = jnp.zeros_like(dv)

    for block in range(8):
        masks = tile_masks(block, parents_ref)
        rows = pl.ds(block * 256, 256)

        def one_head_back(head, unused):
            head_rows = pl.ds(pl.multiple_of(head * HEAD, HEAD), HEAD)
            queries = head_lanes(qkv[rows, 0:128], head) * low(0.125)
            grads = tree_rows[2 * block : 2 * block + 2].reshape(256, 128)
            grad_rows = head_lanes(grads, head)
            lse = logs[pl.ds(pl.multiple_of(head * 8, 8), 8), block * 256 : block * 256 + 256][0:1]
            both = grads.T.astype(full) * mixed[:, block * 256 : block * 256 + 256]
            delta = jnp.where(
                head == 0,
                jnp.sum(both[:HEAD], axis=0, keepdims=True),
                jnp.sum(both[HEAD:], axis=0, keepdims=True),
            )
            grad_query = None
            for first, number, scores in score_parts(
                block, qkv.at[:, pl.ds(128, 128)], queries, masks
            ):
                keys = pl.ds(first, number)
                weights = jnp.exp(scores - lse)
                grad_weights = times_t(qkv[keys, 256:384], grad_rows)
                grad_scores = (weights * (grad_weights - delta)).astype(low)
                dk[keys, :] += jnp.dot(grad_scores, queries, preferred_element_type=full)
                dv[keys, :] += jnp.dot(weights.astype(low), grad_rows, preferred_element_type=full)
                term = jnp.dot(side_t[head_rows, keys], grad_scores, preferred_element_type=full)
                grad_query = term if grad_query is None else grad_query + term
            dq_t[head_rows, block * 256 : block * 256 + 256] = grad_query * 0.125
            return unused

        lax.fori_loop(0, 2, one_head_back, 0)
        if block == 1:
            rs_half(2, 0)
        if block == 5:
            rs_half(3, 0)
        if block == 4:
            outs[:, rep] = summed(outs[:, rep], cr_out[:, y]).astype(low)
            go_y.wait_recv()
            outs[:, rep] = summed(outs[:, rep], yr_out[...]).astype(low)
            ro_step(0)
        if block == 6:
            ro_step(1)

    for seg in range(16):
        rows = pl.ds(seg * 128, 128)
        qkv_slots[seg, :, 0:128] = dq_t[:, seg * 128 : seg * 128 + 128].T.astype(low)
        qkv_slots[seg, :, 128:256] = dk[rows, :].astype(low)
        qkv_slots[seg, :, 256:384] = dv[rows, :].astype(low)
    for slot in range(16):
        gq_slots[slot // 2, (slot % 2) * 128 : (slot % 2) * 128 + 128, :] = qkv_slots[ids_ref[slot]]

    def ge_copy(flow, step, half):
        return remote(
            acts.at[flow * 4 + step, half],
            w_all.at[flow * 4 + step, half],
            ge_s.at[flow, step, half],
            ge_r.at[flow, step, half],
            ring_device[flow],
        )

    def ge_part(block):
        return times_t(gq_slots[block], slices[...].reshape(1024, 384))

    def ge_step(step):
        made = [ge_part(flow_block(flow, 4 - step)) for flow in range(2)]
        for half in range(2):
            for flow in range(2):
                if step == 0 and half != flow:
                    continue
                rows = made[flow][half * 128 : half * 128 + 128]
                if step > 1 or (step == 1 and half == flow):
                    ge_copy(flow, step - 1, half).wait_recv()
                    rows = rows + w_all[flow * 4 + step - 1, half].astype(full)
                acts[flow * 4 + step, half] = rows.astype(low)
                ge_copy(flow, step, half).start()

    ge_step(0)
    ro_step(2)
    for block in range(8):
        gq_t[:, block * 256 : block * 256 + 256] = gq_slots[block].T
    fetch.wait()
    for copy in small:
        copy.wait_send()
    for s in range(8):
        made = jnp.dot(
            gq_t[...],
            xch[:, :, s * 128 : s * 128 + 128].reshape(2048, 128),
            preferred_element_type=full,
        )
        wq_send[s] = made.T.astype(low).reshape(2, 2, 32, 384)
    qs_over_core = remote(wq_send.at[:, :, 1 - core], qs_core, qr_s.at[0], qr_r.at[0], over_core)
    qs_over_core.start()
    ge_step(1)
    qs_over_core.wait_recv()
    qs_half[...] = summed(wq_send[:, :, core], qs_core[...]).astype(low)
    qs_over_y = remote(qs_half.at[:, 1 - y], qs_y, qr_s.at[1], qr_r.at[1], over_y)
    qs_over_y.start()
    ro_step(3)
    ge_step(2)
    qs_over_y.wait_recv()
    qs_half[:, y] = summed(qs_half[:, y], qs_y[...]).astype(low)
    qs_sends = [
        remote(
            qs_half.at[at.other(step), y],
            qs_recv.at[me],
            qs_s.at[step],
            qs_r.at[step],
            (rep, at.other(step)),
        )
        for step in range(1, 8)
    ]
    for copy in qs_sends:
        copy.start()
    qs_recv[me] = qs_half[me, y]

    def final_copy(kind, leg):
        quarter = at.rep_y if leg == 2 else rep
        if kind == 0:
            spot = fin_up.at[quarter]
        elif kind == 1:
            spot = down_out.at[pl.ds(quarter * 128, 128), :]
        elif kind == 2:
            spot = out_out.at[pl.ds(quarter * 32, 32), :]
        else:
            spot = qkv_out.at[pl.ds(quarter * 32, 32), :]
        device = over_y if leg == 0 else over_core
        return remote(spot, spot, fin_s.at[kind, leg], fin_r.at[kind, leg], device)

    for half in range(2):
        for flow in range(2):
            rs_copy(flow, 3, half).wait_recv()
        total = summed(gw[me, half], rr[0, 3, half], rr[1, 3, half]).astype(low)
        if half == 0:
            fin_up[rep] = total
        else:
            down_out[pl.ds(rep * 128, 128), :] = total
        final_copy(half, 0).start()
        final_copy(half, 1).start()
    for flow in range(2):
        ro_copy(flow, 3).wait_recv()
    out_out[pl.ds(rep * 32, 32), :] = summed(outs[me, rep], rr_out[0, 3], rr_out[1, 3]).astype(low)
    final_copy(2, 0).start()
    final_copy(2, 1).start()
    ge_step(3)
    part_copy(1, 1).wait_recv()
    part_copy(1, 2).wait_recv()
    tok_all[6] = summed(stage[0:2].reshape(256, 1024), parts[4], parts[5]).astype(low)
    layer_write = pltpu.make_async_copy(tok_all.at[6], layer_ref, load_s.at[1])
    layer_write.start()
    for copy in qs_sends:
        copy.wait_recv()
    quarter_rows = pl.ds(rep * 32, 32)
    for s in range(8):
        total = qs_recv[s]
        for j in range(3):
            first = j * 1024 + s * 128
            qkv_out[quarter_rows, first : first + 128] = total[:, j * 128 : j * 128 + 128]
    final_copy(3, 0).start()
    final_copy(3, 1).start()
    for kind in range(4):
        final_copy(kind, 0).wait_recv()
        final_copy(kind, 2).start()

    grad_entered = ge_part(me)
    for flow in range(2):
        ge_copy(flow, 3, 0).wait_recv()
        ge_copy(flow, 3, 1).wait_recv()
        grad_entered = grad_entered + w_all[flow * 4 + 3].reshape(256, 1024).astype(full)
    normed, inv_std = normed_rows(tok_ref[...].astype(full))
    gain_one = jnp.sum(grad_entered * normed, axis=0, keepdims=True)
    for s in range(8):
        gp[s, 0:8, :] = jnp.broadcast_to(gain_one[:, s * 128 : s * 128 + 128], (8, 128))
    gain_sends = [
        remote(
            gp.at[at.other(step)],
            gp_recv.at[me],
            gp_s.at[step],
            gp_r.at[step],
            (rep, at.other(step)),
        )
        for step in range(1, 8)
    ]
    for copy in gain_sends:
        copy.start()
    gp_recv[me] = gp[me]
    in_grad = stage[2:4].reshape(256, 1024) + norm_back(
        grad_entered * gain_row(gains_ref, 0), normed, inv_std
    )
    stage[4] = in_grad[:128]
    stage[5] = in_grad[128:]
    in_write = pltpu.make_async_copy(stage.at[4:6], in_ref, load_s.at[2])
    in_write.start()
    for copy in gain_sends:
        copy.wait_recv()
    total = gp_recv[0]
    for s in range(1, 8):
        total = total + gp_recv[s]
    gp_rep[rep] = total
    rep_sends = [
        remote(gp_rep.at[rep], gp_rep.at[rep], gr_s.at[i], gr_r.at[i], (to, me))
        for i, to in enumerate((at.rep_y, at.rep_core, at.rep_far))
    ]
    for copy in rep_sends:
        copy.start()
    for kind in range(4):
        final_copy(kind, 1).wait_recv()
        final_copy(kind, 2).wait_recv()
    for quarter in range(4):
        for s in range(8):
            first = s * 512 + quarter * 128
            up_out[:, first : first + 128] = fin_up[quarter, :, s * 128 : s * 128 + 128]
    for copy in rep_sends:
        copy.wait()
    gain_out[...] = gp_rep[0] + gp_rep[1] + gp_rep[2] + gp_rep[3]

    layer_write.wait()
    in_write.wait()
    for kind in range(4):
        for leg in range(3):
            final_copy(kind, leg).wait_send()
    qs_over_y.wait_send()
    qs_over_core.wait_send()
    go_y.wait_send()
    for copy in go_core + qs_sends + gain_sends + do_sends:
        copy.wait_send()
    slice_core.wait_send()
    for kind in range(2):
        for leg in range(3):
            part_copy(kind, leg).wait_send()
    for step in range(4):
        for flow in range(2):
            for half in range(2):
                if step > 0 or half == flow:
                    ge_copy(flow, step, half).wait_send()
                    rs_copy(flow, step, half).wait_send()
        for flow in ro_flows(step):
            ro_copy(flow, step).wait_send()


def widen_kernel(*refs):
    for source, target in zip(refs[:6], refs[7:13]):
        target[...] = source[...].astype(target.dtype)
    refs[13][...] = refs[6][0:1, :]
    refs[14][...] = refs[6][8:9, :]


W_START = 2
W_BLOCKS = [0, 4, 7]


def fast_shards(
    tokens, cotangent, qkv_weight, out_weight, up_weight, down_weight, gain_attn, gain_ffn, parents, slot_ids
):
    low, full = jnp.bfloat16, jnp.float32
    smem = pl.BlockSpec(memory_space=pltpu.SMEM)
    vmem = pl.BlockSpec(memory_space=pltpu.VMEM)
    anywhere = pl.BlockSpec(memory_space=pl.ANY)

    def dma(*shape):
        return pltpu.SemaphoreType.DMA(shape)

    v = pltpu.VMEM
    scratch = [
        v((6, 128, 1024), full),
        v((16, 128), low),
        v((8, 2, 2, 32, 384), low),
        v((8, 2, 2, 32, 384), low),
        v((8, 16, 128), low),
        v((8, 256, 1024), low),
        v((16, 128, 384), low),
        v((2048, 384), low),
        v((128, 2048), low),
        v((16, 128, 128), low),
        v((8, 256, 128), low),
        v((128, 2048), full),
        v((16, 2048), full),
        v((256, 1024), low),
        v((8, 4, 32, 1024), low),
        v((8, 2, 128, 1024), low),
        v((8, 256, 1024), low),
        v((8, 2, 128, 1024), low),
        v((6, 256, 1024), low),
        v((8, 2, 128, 1024), low),
        v((2, 4, 2, 128, 1024), low),
        v((2, 4, 32, 1024), low),
        v((8, 2, 32, 1024), low),
        v((8, 32, 1024), low),
        v((8, 256, 128), low),
        v((2048, 128), full),
        v((2048, 128), full),
        v((384, 2048), low),
        v((8, 2, 32, 384), low),
        v((8, 2, 32, 384), low),
        v((8, 32, 384), low),
        v((8, 32, 384), low),
        v((4, 128, 1024), low),
        v((8, 16, 128), full),
        v((8, 16, 128), full),
        v((4, 16, 128), full),
        dma(13), dma(2, 8), dma(2, 8), dma(1), dma(1), dma(2, 4, 2), dma(2, 4, 2),
        dma(2, 4), dma(2, 4), dma(2, 4), dma(2, 4), dma(2, 2, 4), dma(2, 2, 4),
        dma(2, 4, 2), dma(2, 4, 2), dma(2), dma(8), dma(8), dma(3), dma(3), dma(3), dma(3),
        dma(6), dma(6), dma(8), dma(8), dma(3), dma(3), dma(2, 4, 2), dma(2, 4, 2),
        dma(2, 4), dma(2, 4), dma(4, 3), dma(4, 3), dma(2, 4, 2), dma(2, 4, 2), dma(8), dma(8),
        dma(2), dma(2), dma(8), dma(8), dma(3), dma(3),
    ]
    made = pl.pallas_call(
        layer_kernel,
        out_shape=[
            jax.ShapeDtypeStruct((256, 1024), low),
            jax.ShapeDtypeStruct((2, 128, 1024), full),
            jax.ShapeDtypeStruct((128, 3072), low),
            jax.ShapeDtypeStruct((128, 1024), low),
            jax.ShapeDtypeStruct((128, 4096), low),
            jax.ShapeDtypeStruct((512, 1024), low),
            jax.ShapeDtypeStruct((16, 128), full),
            jax.ShapeDtypeStruct((8, 256, 1024), low),
        ],
        in_specs=[smem] * 2 + [vmem] * 4 + [anywhere] * 4,
        out_specs=[anywhere] * 2 + [vmem] * 5 + [anywhere],
        scratch_shapes=scratch,
        compiler_params=pltpu.CompilerParams(
            collective_id=1, has_side_effects=True, vmem_limit_bytes=VMEM_LIMIT
        ),
    )(
        slot_ids, parents.reshape(16), tokens, cotangent, gain_attn.reshape(1, 128), gain_ffn.reshape(1, 128), qkv_weight, out_weight, up_weight,
        down_weight,
    )
    shapes = [(256, 1024), (256, 1024), (128, 3072), (128, 1024), (128, 4096), (512, 1024)]
    results = [made[0], made[1].reshape(256, 1024)] + list(made[2:7])

    def spec(shape):
        return pl.BlockSpec((shape[0] // 4, shape[1]), lambda i: (i, 0))

    gain_spec = pl.BlockSpec((1, 128), lambda i: (0, 0))
    last = pl.pallas_call(
        widen_kernel,
        grid=(4,),
        out_shape=[jax.ShapeDtypeStruct(shapes[0], low)]
        + [jax.ShapeDtypeStruct(shape, full) for shape in shapes[1:]]
        + [jax.ShapeDtypeStruct((1, 128), full)] * 2,
        in_specs=[spec(shape) for shape in shapes] + [pl.BlockSpec((16, 128), lambda i: (0, 0))],
        out_specs=[spec(shape) for shape in shapes] + [gain_spec] * 2,
    )(*results)
    return tuple(last[:6]) + (last[6].reshape(128), last[7].reshape(128))


VMEM_LIMIT = 61 * 2**20


def solution(mesh):
    in_specs = (
        P(("rep", "shard"), None),
        P(("rep", "shard"), None),
        P("shard", None),
        P("shard", None),
        P("shard", None),
        P("shard", None),
        P("shard"),
        P("shard"),
        P("rep", None),
        P("rep"),
    )
    out_specs = (
        P(("rep", "shard"), None),
        P(("rep", "shard"), None),
        P("shard", None),
        P("shard", None),
        P("shard", None),
        P("shard", None),
        P("shard"),
        P("shard"),
    )

    def fits(*args):
        shapes = [a.shape for a in args]
        return shapes[0] == (8192, 1024) and shapes[4] == (1024, 4096) and shapes[8] == (4, 16)

    small = mesh.shape["rep"] == 4 and mesh.shape["shard"] == 8

    def whole(*args):
        run = fast_shards if small and fits(*args) else shards
        return jax.shard_map(
            run, mesh=mesh, in_specs=in_specs, out_specs=out_specs, check_vma=False
        )(*args)

    return whole
```

```python
import jax
import jax.numpy as jnp
from jax import lax
from jax.experimental import pallas as pl
from jax.experimental.pallas import tpu as pltpu
from jax.sharding import PartitionSpec as P

HEADS = 16
HEAD = 64


masked_score = -1e30


def block_size():
    return 512


def normalize(values):
    average = jnp.mean(values, axis=-1, keepdims=True)
    centered = values - average
    variance = jnp.mean(centered * centered, axis=-1, keepdims=True)
    inv_std = lax.rsqrt(variance + 1e-05)
    return (centered * inv_std, inv_std)


def gelu_exact(values):
    return 0.5 * values * (1.0 + lax.erf(values * 0.7071067811865476))


def gelu_slope(values):
    return (
        0.5 * (1.0 + lax.erf(values * 0.7071067811865476))
        + values * jnp.exp(-0.5 * values * values) * 0.3989422804014327
    )


def norm_back(grad_normed, normed, inv_std):
    first_mean = jnp.mean(grad_normed, axis=-1, keepdims=True)
    second_mean = jnp.mean(grad_normed * normed, axis=-1, keepdims=True)
    return inv_std * (grad_normed - first_mean - normed * second_mean)


def times_t(left_side, right_side):
    return lax.dot_general(
        left_side, right_side, (((1,), (1,)), ((), ())), preferred_element_type=jnp.float32
    )


def t_times(left_side, right_side):
    return lax.dot_general(
        left_side, right_side, (((0,), (0,)), ((), ())), preferred_element_type=jnp.float32
    )


def exact_dot(left_side, right_side):
    return jnp.dot(
        left_side, right_side, precision=lax.Precision.HIGHEST, preferred_element_type=jnp.float32
    )


def slot_table(group_ids, parents):
    tree_segs = parents.shape[1]
    group_segs = group_ids.shape[0]
    seg_range = jnp.arange(tree_segs, dtype=jnp.int32)
    walker = seg_range[None, :]
    reached = walker[:, :, None] == seg_range[None, None, :]

    def climb(step_index, carried):
        walker_now, reached_now = carried
        walker_now = jnp.sum(
            jnp.where(walker_now[:, :, None] == seg_range[None, None, :], parents[:, None, :], 0),
            axis=2,
        )
        return (walker_now, reached_now | (walker_now[:, :, None] == seg_range[None, None, :]))

    walker, reached = lax.fori_loop(0, tree_segs, climb, (walker, reached))
    anc_flat = reached.reshape(group_segs, tree_segs).astype(jnp.float32)
    id_picks = (group_ids[:, None] == jnp.arange(group_segs, dtype=jnp.int32)[None, :]).astype(
        jnp.float32
    )
    seg_rows = exact_dot(id_picks, anc_flat)
    local_pick = ((group_ids % tree_segs)[:, None] == seg_range[None, :]).astype(jnp.float32)
    tree_of = group_ids // tree_segs
    same_tree = (tree_of[:, None] == tree_of[None, :]).astype(jnp.float32)
    return (
        lax.dot_general(
            seg_rows,
            local_pick,
            (((1,), (1,)), ((), ())),
            precision=lax.Precision.HIGHEST,
            preferred_element_type=jnp.float32,
        )
        * same_tree
    )


def visible_mask(allowed, seg_len, query_start, query_rows, key_start, key_rows):
    group_segs = allowed.shape[0]
    query_index = query_start + jnp.arange(query_rows, dtype=jnp.int32)
    key_index = key_start + jnp.arange(key_rows, dtype=jnp.int32)
    query_slot = query_index // seg_len
    key_slot = key_index // seg_len
    seg_range = jnp.arange(group_segs, dtype=jnp.int32)
    query_pick = (query_slot[:, None] == seg_range[None, :]).astype(jnp.float32)
    key_pick = (key_slot[:, None] == seg_range[None, :]).astype(jnp.float32)
    linked = (
        lax.dot_general(
            exact_dot(query_pick, allowed),
            key_pick,
            (((1,), (1,)), ((), ())),
            precision=lax.Precision.HIGHEST,
            preferred_element_type=jnp.float32,
        )
        > 0.5
    )
    return linked & (
        (query_slot[:, None] != key_slot[None, :]) | (key_index[None, :] <= query_index[:, None])
    )


def pair_terms(query_part, grad_part, stat_part, delta_part, key_part, value_part, visible):
    scores = (
        jnp.einsum("qhd,khd->qhk", query_part, key_part, preferred_element_type=jnp.float32) * 0.125
    )
    scores = jnp.where(visible[:, None, :], scores, masked_score)
    probs_full = jnp.exp(scores - stat_part[:, :, None])
    grad_probs = jnp.einsum(
        "qhd,khd->qhk", grad_part, value_part, preferred_element_type=jnp.float32
    )
    grad_scores = (probs_full * (grad_probs - delta_part[:, :, None])).astype(jnp.bfloat16)
    grad_query = None
    grad_key = None
    grad_value = None
    grad_query = (
        jnp.einsum("qhk,khd->qhd", grad_scores, key_part, preferred_element_type=jnp.float32)
        * 0.125
    )
    grad_key = (
        jnp.einsum("qhk,qhd->khd", grad_scores, query_part, preferred_element_type=jnp.float32)
        * 0.125
    )
    grad_value = jnp.einsum(
        "qhk,qhd->khd",
        probs_full.astype(jnp.bfloat16),
        grad_part,
        preferred_element_type=jnp.float32,
    )
    return (grad_query, grad_key, grad_value)


def shards(
    tokens,
    cotangent,
    qkv_weight,
    out_weight,
    up_weight,
    down_weight,
    gain_attn,
    gain_ffn,
    parents,
    slot_ids,
):
    local_rows = tokens.shape[0]
    model_width = tokens.shape[1]
    shard_count = lax.axis_size("shard")
    my_start = lax.axis_index("shard") * local_rows
    seg_len = local_rows * shard_count // slot_ids.shape[0]
    allowed = slot_table(slot_ids, parents)
    qkv_full, out_full, attn_gain = (
        lax.all_gather(qkv_weight.astype(jnp.bfloat16), "shard", axis=0, tiled=True),
        lax.all_gather(out_weight.astype(jnp.bfloat16), "shard", axis=0, tiled=True),
        lax.all_gather(gain_attn.astype(jnp.bfloat16), "shard", axis=0, tiled=True),
    )
    inputs = tokens.astype(jnp.float32)
    normed_one, inv_one = normalize(inputs)
    entered = (normed_one * attn_gain.astype(jnp.float32)).astype(jnp.bfloat16)
    qkv_all = jnp.dot(entered, qkv_full, preferred_element_type=jnp.float32).astype(jnp.bfloat16)
    queries = qkv_all[:, :model_width]
    keys_local = qkv_all[:, model_width : 2 * model_width]
    values_local = qkv_all[:, 2 * model_width :]
    query_heads = queries.reshape(local_rows, HEADS, HEAD)
    start_state = (
        jnp.full((local_rows, HEADS), masked_score, jnp.float32),
        jnp.zeros((local_rows, HEADS), jnp.float32),
        jnp.zeros((local_rows, HEADS, HEAD), jnp.float32),
    )
    carried = start_state
    key_piece = lax.all_gather(keys_local, "shard", axis=0, tiled=True)
    value_piece = lax.all_gather(values_local, "shard", axis=0, tiled=True)
    piece_rows = key_piece.shape[0]
    block_rows = block_size()
    count_blocks = piece_rows // block_rows
    key_blocks = key_piece.reshape(count_blocks, block_rows, HEADS, HEAD)
    value_blocks = value_piece.reshape(count_blocks, block_rows, HEADS, HEAD)

    def attend_block(running, blocks):
        key_block, value_block, block_index = blocks
        run_max, run_sum, run_acc = running
        visible = visible_mask(
            allowed, seg_len, my_start, local_rows, block_index * block_rows, block_rows
        )
        scores = (
            jnp.einsum("qhd,khd->qhk", query_heads, key_block, preferred_element_type=jnp.float32)
            * 0.125
        )
        scores = jnp.where(visible[:, None, :], scores, masked_score)
        new_max = jnp.maximum(run_max, jnp.max(scores, axis=2))
        rescale = jnp.exp(run_max - new_max)
        exp_scores = jnp.exp(scores - new_max[:, :, None])
        run_sum = run_sum * rescale + jnp.sum(exp_scores, axis=2)
        run_acc = run_acc * rescale[:, :, None] + jnp.einsum(
            "qhk,khd->qhd",
            exp_scores.astype(jnp.bfloat16),
            value_block,
            preferred_element_type=jnp.float32,
        )
        return ((new_max, run_sum, run_acc), None)

    carried, unused = lax.scan(
        attend_block, carried, (key_blocks, value_blocks, jnp.arange(count_blocks, dtype=jnp.int32))
    )
    run_max, run_sum, run_acc = carried
    attn_exact = run_acc / run_sum[:, :, None]
    log_sum = run_max + jnp.log(run_sum)
    attended = attn_exact.reshape(local_rows, model_width).astype(jnp.bfloat16)
    hidden = inputs + jnp.dot(attended, out_full, preferred_element_type=jnp.float32)
    up_full, down_full, ffn_gain = (
        lax.all_gather(up_weight.astype(jnp.bfloat16), "shard", axis=0, tiled=True),
        lax.all_gather(down_weight.astype(jnp.bfloat16), "shard", axis=0, tiled=True),
        lax.all_gather(gain_ffn.astype(jnp.bfloat16), "shard", axis=0, tiled=True),
    )
    normed_two, inv_two = normalize(hidden)
    second = (normed_two * ffn_gain.astype(jnp.float32)).astype(jnp.bfloat16)
    pre_act = jnp.dot(second, up_full, preferred_element_type=jnp.float32)
    active = gelu_exact(pre_act).astype(jnp.bfloat16)
    output = (hidden + jnp.dot(active, down_full, preferred_element_type=jnp.float32)).astype(
        jnp.bfloat16
    )
    up_full, down_full, ffn_gain = (
        lax.all_gather(up_weight.astype(jnp.bfloat16), "shard", axis=0, tiled=True),
        lax.all_gather(down_weight.astype(jnp.bfloat16), "shard", axis=0, tiled=True),
        lax.all_gather(gain_ffn.astype(jnp.bfloat16), "shard", axis=0, tiled=True),
    )
    qkv_full, out_full, attn_gain = (
        lax.all_gather(qkv_weight.astype(jnp.bfloat16), "shard", axis=0, tiled=True),
        lax.all_gather(out_weight.astype(jnp.bfloat16), "shard", axis=0, tiled=True),
        lax.all_gather(gain_attn.astype(jnp.bfloat16), "shard", axis=0, tiled=True),
    )
    grad_down = t_times(active, cotangent)
    grad_active = times_t(cotangent, down_full).astype(jnp.bfloat16)
    grad_pre = (grad_active.astype(jnp.float32) * gelu_slope(pre_act)).astype(jnp.bfloat16)
    grad_up = t_times(second, grad_pre)
    grad_second = times_t(grad_pre, up_full)
    grad_gain_ffn = jnp.sum(grad_second * normed_two, axis=0)
    grad_hidden = cotangent.astype(jnp.float32) + norm_back(
        grad_second * ffn_gain.astype(jnp.float32), normed_two, inv_two
    )
    grad_y = grad_hidden.astype(jnp.bfloat16)
    grad_out = t_times(attended, grad_y)
    grad_attn = times_t(grad_y, out_full).astype(jnp.bfloat16)
    grad_heads = grad_attn.reshape(local_rows, HEADS, HEAD)
    row_delta = jnp.sum(grad_heads.astype(jnp.float32) * attn_exact, axis=2)
    start_back = jnp.zeros((local_rows, HEADS, HEAD), jnp.float32)
    carried = start_back
    key_piece = lax.all_gather(keys_local, "shard", axis=0, tiled=True)
    value_piece = lax.all_gather(values_local, "shard", axis=0, tiled=True)
    piece_rows = key_piece.shape[0]
    back_block_rows = block_size()
    count_blocks = piece_rows // back_block_rows
    key_blocks = key_piece.reshape(count_blocks, back_block_rows, HEADS, HEAD)
    value_blocks = value_piece.reshape(count_blocks, back_block_rows, HEADS, HEAD)

    def back_block(running, blocks):
        grad_query = running
        key_block, value_block, block_index = blocks
        block_start = block_index * back_block_rows
        visible = visible_mask(allowed, seg_len, my_start, local_rows, block_start, back_block_rows)
        part_query, part_key, part_value = pair_terms(
            query_heads, grad_heads, log_sum, row_delta, key_block, value_block, visible
        )
        joined = jnp.concatenate(
            (
                part_key.reshape(back_block_rows, model_width),
                part_value.reshape(back_block_rows, model_width),
            ),
            axis=1,
        )
        return (grad_query + part_query, joined.astype(jnp.bfloat16))

    carried, key_terms = lax.scan(
        back_block, carried, (key_blocks, value_blocks, jnp.arange(count_blocks, dtype=jnp.int32))
    )
    grad_query = carried
    key_terms = key_terms.reshape(piece_rows, 2 * model_width)
    key_grads = lax.psum_scatter(key_terms, "shard", scatter_dimension=0, tiled=True)
    grad_qkv = jnp.concatenate(
        (grad_query.reshape(local_rows, model_width), key_grads), axis=1
    ).astype(jnp.bfloat16)
    grad_qkv_weight = t_times(entered, grad_qkv)
    grad_entered = times_t(grad_qkv, qkv_full)
    grad_gain_attn = jnp.sum(grad_entered * normed_one, axis=0)
    input_grad = grad_hidden + norm_back(
        grad_entered * attn_gain.astype(jnp.float32), normed_one, inv_one
    )
    group_sums = (
        lax.psum_scatter(grad_qkv_weight.astype(jnp.bfloat16), "shard", scatter_dimension=0, tiled=True),
        lax.psum_scatter(grad_out.astype(jnp.bfloat16), "shard", scatter_dimension=0, tiled=True),
        lax.psum_scatter(grad_up.astype(jnp.bfloat16), "shard", scatter_dimension=0, tiled=True),
        lax.psum_scatter(grad_down.astype(jnp.bfloat16), "shard", scatter_dimension=0, tiled=True),
        lax.psum_scatter(grad_gain_attn, "shard", scatter_dimension=0, tiled=True),
        lax.psum_scatter(grad_gain_ffn, "shard", scatter_dimension=0, tiled=True),
    )
    totals = (
        lax.psum(group_sums[0].astype(jnp.bfloat16), "rep").astype(jnp.float32),
        lax.psum(group_sums[1].astype(jnp.bfloat16), "rep").astype(jnp.float32),
        lax.psum(group_sums[2].astype(jnp.bfloat16), "rep").astype(jnp.float32),
        lax.psum(group_sums[3].astype(jnp.bfloat16), "rep").astype(jnp.float32),
        lax.psum(group_sums[4].astype(jnp.bfloat16), "rep").astype(jnp.float32),
        lax.psum(group_sums[5].astype(jnp.bfloat16), "rep").astype(jnp.float32),
    )
    return (output, input_grad, totals[0], totals[1], totals[2], totals[3], totals[4], totals[5])


MESH = pl.DeviceIdType.MESH


def ring_place(shard):
    return (1 - shard % 2) * (shard // 2) + (shard % 2) * (7 - shard // 2)


def ring_shard(place):
    upper = place // 4
    return (1 - upper) * 2 * place + upper * (15 - 2 * place)


def remote(source, target, sent, got, device):
    return pltpu.make_async_remote_copy(
        src_ref=source,
        dst_ref=target,
        send_sem=sent,
        recv_sem=got,
        device_id=device,
        device_id_type=MESH,
    )


def around(place, offset):
    return ring_shard(lax.rem(place + offset + 8, 8))


class Where:
    def __init__(self):
        self.rep = lax.axis_index("rep")
        self.me = lax.axis_index("shard")
        self.y = self.rep // 2
        self.core = self.rep % 2
        self.rep_y = (1 - self.y) * 2 + self.core
        self.rep_core = self.y * 2 + 1 - self.core
        self.rep_far = (1 - self.y) * 2 + 1 - self.core
        self.place = ring_place(self.me)
        self.right = around(self.place, 1)
        self.left = around(self.place, -1)

    def other(self, step):
        return lax.rem(self.me + step, 8)

    def back(self, step):
        return lax.rem(self.me + 8 - step, 8)

    def greet(self):
        barrier = pltpu.get_barrier_semaphore()
        for step in range(1, 8):
            pl.semaphore_signal(
                barrier, inc=1, device_id=(self.rep, self.other(step)), device_id_type=MESH
            )
        for rep in (self.rep_y, self.rep_core, self.rep_far):
            pl.semaphore_signal(barrier, inc=1, device_id=(rep, self.me), device_id_type=MESH)
        pl.semaphore_wait(barrier, 10)


def normed_rows(values):
    average = jnp.mean(values, axis=-1, keepdims=True)
    centered = values - average
    variance = jnp.mean(centered * centered, axis=-1, keepdims=True)
    inv_std = lax.rsqrt(variance + 1e-05)
    return (centered * inv_std, inv_std)


def gain_row(gains_ref, which):
    return jnp.concatenate(
        [gains_ref[s, which * 8 : which * 8 + 1, :] for s in range(8)], axis=1
    ).astype(jnp.float32)


def head_lanes(values, head):
    lane = lax.broadcasted_iota(jnp.int32, values.shape, 1)
    return jnp.where(lane // HEAD == head, values, jnp.zeros_like(values))


def tile_masks(block, parents_ref):
    key_row = lax.broadcasted_iota(jnp.int32, (256, 256), 0)
    query_row = lax.broadcasted_iota(jnp.int32, (256, 256), 1)
    own = key_row <= query_row
    if block < 5:
        return (own, None)
    own = own & (key_row // 128 == query_row // 128)
    if block == 5:
        return (own, None)
    parent = jnp.where(query_row < 128, parents_ref[2 * block], parents_ref[2 * block + 1])
    return (own, parent == 10 + key_row // 128)


def score_parts(block, keys_ref, queries, masks):
    own_mask, branch_mask = masks
    full = 256 * block if block < 5 else 1280
    spans = [(0, full, None)] if full else []
    if branch_mask is not None:
        spans.append((1280, 256, branch_mask))
    spans.append((256 * block, 256, own_mask))
    parts = []
    for first, rows, mask in spans:
        scores = times_t(keys_ref[pl.ds(first, rows), :], queries)
        if mask is not None:
            scores = jnp.where(mask, scores, masked_score)
        parts.append((first, rows, scores))
    return parts


def summed(*parts):
    total = parts[0].astype(jnp.float32)
    for part in parts[1:]:
        total = total + part.astype(jnp.float32)
    return total


BLOCK_ORDER = [4, 3, -3, 2, -2, 1, -1, 0]


def layer_kernel(
    ids_ref, parents_ref, tok_ref, cot_ref, gain_one_ref, gain_two_ref, qkv_w, out_w, up_w, down_w,
    layer_ref, in_ref, qkv_out, out_out, up_out, down_out, gain_out, ent_hbm,
    stage, gain_ref, wq_send, slices, gains_ref, tok_all, qkv_slots, qkv, side_t, tree_rows, slot_rows,
    mixed, logs, att, out_all, w_all, xch, acts, parts, gw, rr, rr_out, cr_out, yr_out,
    do_slots, dk, dv, gq_t, qs_core, qs_half, qs_recv, qs_y, fin_up, gp, gp_recv, gp_rep,
    load_s, small_s, small_r, slc_s, slc_r, tok_s, tok_r, o_s, o_r, oy_s, oy_r, oc_s, oc_r, w_s, w_r,
    keep_s, mix_s, mix_r, cot_s, cot_r, sec_s, sec_r, part_s, part_r, do_s, do_r,
    go_s, go_r, rs_s, rs_r, ro_s, ro_r, fin_s, fin_r, ge_s, ge_r, qs_s, qs_r, qr_s, qr_r,
    gp_s, gp_r, gr_s, gr_r,
):
    low, full = jnp.bfloat16, jnp.float32
    dq_t, gq_slots = mixed, qkv.reshape(8, 256, 384)
    at = Where()
    rep, me, y, core = at.rep, at.me, at.y, at.core
    ring_device = ((rep, at.right), (rep, at.left))
    over_y, over_core = (at.rep_y, me), (at.rep_core, me)
    places = []
    for seg in range(16):
        place = jnp.int32(0)
        for slot in range(1, 16):
            place = jnp.where(ids_ref[slot] == seg, slot, place)
        places.append(place)

    loads = [
        pltpu.make_async_copy(qkv_w.at[:, pl.ds(j * 1024, 1024)], stage.at[j], load_s.at[j])
        for j in range(3)
    ]
    loads.append(pltpu.make_async_copy(out_w, stage.at[3], load_s.at[3]))
    loads.append(
        pltpu.make_async_copy(down_w.at[pl.ds(rep * 128, 128), :], stage.at[5], load_s.at[4])
    )
    for s in range(8):
        columns = pl.ds(pl.multiple_of(s * 512 + rep * 128, 128), 128)
        loads.append(
            pltpu.make_async_copy(
                up_w.at[:, columns], stage.at[4, :, pl.ds(s * 128, 128)], load_s.at[5 + s]
            )
        )
    for copy in loads:
        copy.start()
    gain_ref[0:8, :] = jnp.broadcast_to(gain_one_ref[...], (8, 128)).astype(low)
    gain_ref[8:16, :] = jnp.broadcast_to(gain_two_ref[...], (8, 128)).astype(low)
    at.greet()

    def flow_block(flow, offset):
        return around(at.place, -offset if flow else offset)

    def token_copy(flow, step, half):
        origin = flow_block(flow, -step)
        source = tok_ref if step == 0 else tok_all.at[origin]
        rows = pl.ds(half * 128, 128)
        return remote(
            source.at[rows, :],
            tok_all.at[origin, rows, :],
            tok_s.at[flow, step, half],
            tok_r.at[flow, step, half],
            ring_device[flow],
        )

    def step_halves(step):
        if step == 3:
            return [(0, 0), (1, 1)]
        return [(half, flow) for half in range(2) for flow in range(2)]

    def out_copy(flow, step):
        spot = out_all.at[flow_block(flow, -step), rep]
        return remote(spot, spot, o_s.at[flow, step], o_r.at[flow, step], ring_device[flow])

    def out_flows(step):
        return (0, 1) if step < 3 else (0,)

    def out_over_y(flow, step):
        spot = out_all.at[flow_block(flow, -step - 1), rep]
        return remote(spot, spot, oy_s.at[flow, step], oy_r.at[flow, step], over_y)

    def out_over_core(flow, step, own):
        spot = out_all.at[flow_block(flow, -step - 1), rep if own else at.rep_y]
        return remote(spot, spot, oc_s.at[own, flow, step], oc_r.at[own, flow, step], over_core)

    def w_copy(flow, step, half):
        spot = w_all.at[flow_block(flow, -step), half]
        return remote(spot, spot, w_s.at[flow, step, half], w_r.at[flow, step, half], ring_device[flow])

    def w_half(step, half):
        for flow in range(2):
            if step == 3 and flow != half:
                continue
            w_copy(flow, step, half).wait_recv()
            if step < 2 or (step == 2 and half == flow):
                w_copy(flow, step + 1, half).start()

    small = [
        remote(
            gain_ref,
            gains_ref.at[me],
            small_s.at[0, step],
            small_r.at[0, step],
            (rep, at.other(step)),
        )
        for step in range(1, 8)
    ]
    small += [
        remote(
            wq_send.at[at.other(step), :, core],
            slices.at[me, :, core],
            small_s.at[1, step],
            small_r.at[1, step],
            (rep, at.other(step)),
        )
        for step in range(1, 8)
    ]
    slice_core = remote(
        slices.at[:, :, core], slices.at[:, :, core], slc_s.at[0], slc_r.at[0], over_core
    )
    cot_y = remote(cot_ref, xch.at[6], cot_s.at[0], cot_r.at[0], over_y)
    cot_core = remote(cot_ref, xch.at[5], cot_s.at[1], cot_r.at[1], over_core)
    cot_far = remote(xch.at[6], xch.at[7], cot_s.at[2], cot_r.at[2], over_core)

    for copy in small[:7]:
        copy.start()
    for half in range(2):
        for flow in range(2):
            token_copy(flow, 0, half).start()
    cot_y.start()
    cot_core.start()
    for copy in loads[:3]:
        copy.wait()
    for s in range(8):
        for j in range(3):
            wq_send[s, :, :, :, j * 128 : j * 128 + 128] = (
                stage[j, :, s * 128 : s * 128 + 128].astype(low).reshape(2, 2, 32, 128)
            )
    for copy in small[7:]:
        copy.start()
    gains_ref[me] = gain_ref[...]
    slices[me, :, core] = wq_send[me, :, core]
    loads[3].wait()
    out_all[me] = stage[3].astype(low).reshape(4, 32, 1024)
    for flow in range(2):
        out_copy(flow, 0).start()
    for copy in loads[4:]:
        copy.wait()
    w_all[me, 0] = stage[4].astype(low)
    w_all[me, 1] = stage[5].astype(low)
    xch[4] = cot_ref[...]
    kept = {}

    def enter(rows, origin, count):
        slot = 4 + count % 2
        if count > 1:
            kept[count - 2].wait()
        normed, _ = normed_rows(rows.astype(full))
        entered = (normed * gain).astype(low)
        parts[slot] = entered
        kept[count] = pltpu.make_async_copy(parts.at[slot], ent_hbm.at[origin], keep_s.at[slot - 4])
        kept[count].start()
        weights = slices[...].reshape(1024, 384)
        made = jnp.dot(entered, weights, preferred_element_type=full).astype(low)
        qkv_slots[2 * origin] = made[:128]
        qkv_slots[2 * origin + 1] = made[128:]

    def token_step(step):
        for half, flow in step_halves(step):
            token_copy(flow, step, half).wait_recv()
            if step < 2 or (step == 2 and half == flow):
                token_copy(flow, step + 1, half).start()
        for flow in out_flows(step):
            out_copy(flow, step).wait_recv()
            if step < 2 or (step == 2 and flow == 0):
                out_copy(flow, step + 1).start()
            out_over_y(flow, step).start()
            out_over_core(flow, step, 1).start()

    token_step(0)
    for copy in small:
        copy.wait_recv()
    slice_core.start()
    slice_core.wait_recv()
    gain = gain_row(gains_ref, 0)
    enter(tok_ref[...], me, 0)
    count = 1
    for step in range(4):
        if step > 0:
            token_step(step)
        if step == W_START:
            for flow in range(2):
                w_copy(flow, 0, 0).start()
        for flow in out_flows(step):
            origin = flow_block(flow, -step - 1)
            enter(tok_all[origin], origin, count)
            count += 1
    cot_y.wait_recv()
    cot_far.start()
    kept[6].wait()
    kept[7].wait()

    for seg in range(16):
        qkv[seg * 128 : seg * 128 + 128, :] = qkv_slots[places[seg]]
    for block in range(8):
        side_t[:, block * 256 : block * 256 + 256] = qkv[block * 256 : block * 256 + 256, 256:384].T

    for block in range(8):
        masks = tile_masks(block, parents_ref)
        rows = pl.ds(block * 256, 256)

        def one_head(head, unused):
            queries = head_lanes(qkv[rows, 0:128], head) * low(0.125)
            tiles = score_parts(block, qkv.at[:, pl.ds(128, 128)], queries, masks)
            top = None
            for _, _, scores in tiles:
                part = jnp.max(scores, axis=0, keepdims=True)
                top = part if top is None else jnp.maximum(top, part)
            total = None
            mix = None
            head_rows = pl.ds(pl.multiple_of(head * HEAD, HEAD), HEAD)
            for first, number, scores in tiles:
                weights = jnp.exp(scores - top)
                part = jnp.sum(weights, axis=0, keepdims=True)
                total = part if total is None else total + part
                term = jnp.dot(
                    side_t[head_rows, pl.ds(first, number)],
                    weights.astype(low),
                    preferred_element_type=full,
                )
                mix = term if mix is None else mix + term
            mixed[head_rows, block * 256 : block * 256 + 256] = mix / total
            logs[pl.ds(pl.multiple_of(head * 8, 8), 8), block * 256 : block * 256 + 256] = (
                jnp.broadcast_to(top + jnp.log(total), (8, 256))
            )
            return unused

        lax.fori_loop(0, 2, one_head, 0)
        tree = mixed[:, block * 256 : block * 256 + 256].T.astype(low)
        tree_rows[2 * block] = tree[:128]
        tree_rows[2 * block + 1] = tree[128:]
        if block in W_BLOCKS:
            w_half(W_BLOCKS.index(block), 0)

    for slot in range(16):
        slot_rows[slot // 2, (slot % 2) * 128 : (slot % 2) * 128 + 128, :] = tree_rows[
            ids_ref[slot]
        ]
    my_columns = pl.ds(pl.multiple_of(me * 128, 128), 128)
    mix_sends = [
        remote(
            slot_rows.at[at.other(step)],
            att.at[:, my_columns],
            mix_s.at[step],
            mix_r.at[step],
            (rep, at.other(step)),
        )
        for step in range(1, 8)
    ]
    for copy in mix_sends:
        copy.start()
    for flow in range(2):
        w_copy(flow, 0, 1).start()
    att[:, my_columns] = slot_rows[me]
    for step in range(4):
        for flow in out_flows(step):
            out_over_y(flow, step).wait_recv()
            out_over_core(flow, step, 0).start()
    for step in range(4):
        for flow in out_flows(step):
            out_over_core(flow, step, 1).wait_recv()
            out_over_core(flow, step, 0).wait_recv()
    w_half(3, 0)
    for copy in mix_sends:
        copy.wait_recv()
    w_half(0, 1)

    out_full = out_all[...].reshape(1024, 1024)
    hidden = tok_ref[...].astype(full) + jnp.dot(att[...], out_full, preferred_element_type=full)
    ffn_gain = gain_row(gains_ref, 1)
    normed_two, _ = normed_rows(hidden)
    xch[0] = (normed_two * ffn_gain).astype(low)
    sec_y = remote(xch.at[0], xch.at[2], sec_s.at[0], sec_r.at[0], over_y)
    sec_core = remote(xch.at[0], xch.at[1], sec_s.at[1], sec_r.at[1], over_core)
    sec_far = remote(xch.at[2], xch.at[3], sec_s.at[2], sec_r.at[2], over_core)
    sec_y.start()
    sec_core.start()
    stage[0] = hidden[:128]
    stage[1] = hidden[128:]
    for step in range(4):
        for half, flow in step_halves(step):
            token_copy(flow, step, half).wait_send()
    w_half(1, 1)

    up = w_all[:, 0].reshape(1024, 1024)

    def ffn(first):
        second = xch[first : first + 2].reshape(512, 1024)
        pre = jnp.dot(second, up, preferred_element_type=full)
        bell = 1.0 + lax.erf(pre * 0.7071067811865476)
        acts[first : first + 2] = (0.5 * pre * bell).astype(low).reshape(2, 2, 128, 1024)
        slope = 0.5 * bell + pre * jnp.exp(-0.5 * pre * pre) * 0.3989422804014327
        acts[4 + first : 6 + first] = slope.astype(low).reshape(2, 2, 128, 1024)

    def ffn_back(first):
        cots = xch[4 + first : 6 + first].reshape(512, 1024)
        grad_act = times_t(cots, w_all[:, 1].reshape(1024, 1024)).astype(low).astype(full)
        slope = acts[4 + first : 6 + first].reshape(512, 1024).astype(full)
        grad_pre = (grad_act * slope).astype(low)
        acts[4 + first : 6 + first] = grad_pre.reshape(2, 2, 128, 1024)
        return times_t(grad_pre, w_all[:, 0].reshape(1024, 1024))

    sec_core.wait_recv()
    ffn(0)
    w_half(2, 1)
    sec_y.wait_recv()
    sec_far.start()
    cot_core.wait_recv()
    cot_far.wait_recv()
    w_half(3, 1)
    sec_far.wait_recv()
    ffn(2)

    def part_copy(kind, leg):
        index = kind * 3 + leg
        return remote(
            tok_all.at[index],
            parts.at[index],
            part_s.at[index],
            part_r.at[index],
            over_y if leg == 1 else over_core,
        )

    def weight_grads(half, offsets):
        blocks = [around(at.place, offset) for offset in offsets]
        spans = [pl.ds(pl.multiple_of(block * 128, 128), 128) for block in blocks]
        if half == 0:
            sides, other = [xch[0:4, :, span].reshape(1024, 128).T for span in spans], acts
        else:
            sides, other = [acts[0:4, :, :, span].reshape(1024, 128).T for span in spans], xch
        made = jnp.dot(
            jnp.concatenate(sides, axis=0),
            other[4:8].reshape(1024, 1024),
            preferred_element_type=full,
        ).astype(low)
        for i, block in enumerate(blocks):
            gw[block, half] = made[i * 128 : i * 128 + 128]

    def rs_copy(flow, step, half):
        return remote(
            gw.at[flow_block(flow, 4 - step), half],
            rr.at[flow, step, half],
            rs_s.at[flow, step, half],
            rs_r.at[flow, step, half],
            ring_device[flow],
        )

    def rs_half(step, half):
        for flow in range(2):
            block = flow_block(flow, 4 - step)
            if step == 0 and half != flow:
                continue
            if step > 1 or (step == 1 and half == flow):
                rs_copy(flow, step - 1, half).wait_recv()
                gw[block, half] = summed(gw[block, half], rr[flow, step - 1, half]).astype(low)
            rs_copy(flow, step, half).start()

    grad_far = ffn_back(2)
    tok_all[0] = grad_far[256:].astype(low)
    part_copy(0, 0).start()
    stage[2] = grad_far[:128]
    stage[3] = grad_far[128:256]
    part_copy(0, 0).wait_recv()
    tok_all[1] = summed(stage[2:4].reshape(256, 1024), parts[0]).astype(low)
    part_copy(0, 1).start()
    weight_grads(1, [4, 3, -3])
    rs_half(0, 1)
    grad_near = ffn_back(0)
    tok_all[2] = grad_near[256:].astype(low)
    part_copy(0, 2).start()
    stage[2] = grad_near[:128]
    stage[3] = grad_near[128:256]

    weight_grads(0, [4, 3, -3])
    rs_half(0, 0)
    rs_half(1, 1)

    def outputs(first):
        active = acts[first : first + 2].reshape(512, 1024)
        return jnp.dot(active, w_all[:, 1].reshape(1024, 1024), preferred_element_type=full)

    made = outputs(2)
    tok_all[3] = made[256:].astype(low)
    part_copy(1, 0).start()
    stage[4] = made[:128]
    stage[5] = made[128:256]
    part_copy(1, 0).wait_recv()
    tok_all[4] = summed(stage[4:6].reshape(256, 1024), parts[3]).astype(low)
    made = outputs(0)
    tok_all[5] = made[256:].astype(low)
    part_copy(1, 2).start()
    stage[0] = stage[0] + made[:128]
    stage[1] = stage[1] + made[128:256]
    part_copy(1, 1).start()

    for step in range(4):
        for half, flow in step_halves(step):
            w_copy(flow, step, half).wait_send()

    hidden = tok_ref[...].astype(full) + jnp.dot(
        att[...], out_all[...].reshape(1024, 1024), preferred_element_type=full
    )
    normed_two, inv_two = normed_rows(hidden)
    part_copy(0, 2).wait_recv()
    part_copy(0, 1).wait_recv()
    grad_second = summed(stage[2:4].reshape(256, 1024), parts[1], parts[2])
    gain_two = jnp.sum(grad_second * normed_two, axis=0, keepdims=True)
    for s in range(8):
        gp[s, 8:16, :] = jnp.broadcast_to(gain_two[:, s * 128 : s * 128 + 128], (8, 128))
    grad_hidden = cot_ref[...].astype(full) + norm_back(
        grad_second * gain_row(gains_ref, 1), normed_two, inv_two
    )
    stage[2] = grad_hidden[:128]
    stage[3] = grad_hidden[128:]
    grad_y = grad_hidden.astype(low)
    grad_attn = times_t(grad_y, out_all[...].reshape(1024, 1024)).astype(low)
    for copy in mix_sends:
        copy.wait_send()
    for s in range(8):
        slot_rows[s] = grad_attn[:, s * 128 : s * 128 + 128]
    do_sends = [
        remote(
            slot_rows.at[at.other(step)],
            do_slots.at[me],
            do_s.at[step],
            do_r.at[step],
            (rep, at.other(step)),
        )
        for step in range(1, 8)
    ]
    for copy in do_sends:
        copy.start()
    do_slots[me] = slot_rows[me]

    weight_grads(1, [2, -2, 1, -1, 0])
    rs_half(2, 1)
    rs_half(1, 0)
    weight_grads(0, [2, -2, 1, -1, 0])

    for step in range(4):
        for flow in out_flows(step):
            out_copy(flow, step).wait_send()
            out_over_y(flow, step).wait_send()
            out_over_core(flow, step, 0).wait_send()
            out_over_core(flow, step, 1).wait_send()
    for block in range(8):
        out_all[block] = (
            jnp.dot(
                att[:, block * 128 : block * 128 + 128].T, grad_y, preferred_element_type=full
            )
            .astype(low)
            .reshape(4, 32, 1024)
        )
    outs = out_all
    go_core = [
        remote(
            outs.at[:, 2 * i + 1 - core], cr_out.at[:, i], go_s.at[i], go_r.at[i], over_core
        )
        for i in range(2)
    ]
    for copy in go_core:
        copy.start()
    for copy in (cot_y, cot_core, cot_far, sec_y, sec_core, sec_far):
        copy.wait_send()
    fetch = pltpu.make_async_copy(ent_hbm, xch, load_s.at[0])
    fetch.start()
    for copy in go_core:
        copy.wait_recv()
    outs[:, at.rep_y] = summed(outs[:, at.rep_y], cr_out[:, 1 - y]).astype(low)
    go_y = remote(outs.at[:, at.rep_y], yr_out, go_s.at[2], go_r.at[2], over_y)
    go_y.start()

    def ro_copy(flow, step):
        return remote(
            outs.at[flow_block(flow, 4 - step), rep],
            rr_out.at[flow, step],
            ro_s.at[flow, step],
            ro_r.at[flow, step],
            ring_device[flow],
        )

    def ro_flows(step):
        return (0, 1) if step else (0,)

    def ro_step(step):
        for flow in ro_flows(step):
            block = flow_block(flow, 4 - step)
            if step > 0 and flow in ro_flows(step - 1):
                ro_copy(flow, step - 1).wait_recv()
                outs[block, rep] = summed(outs[block, rep], rr_out[flow, step - 1]).astype(low)
            ro_copy(flow, step).start()

    for copy in do_sends:
        copy.wait_recv()
    for seg in range(16):
        tree_rows[seg] = do_slots.reshape(16, 128, 128)[places[seg]]
    for block in range(8):
        side_t[:, block * 256 : block * 256 + 256] = qkv[block * 256 : block * 256 + 256, 128:256].T
    dk[...] = jnp.zeros_like(dk)
    dv[...] = jnp.zeros_like(dv)

    for block in range(8):
        masks = tile_masks(block, parents_ref)
        rows = pl.ds(block * 256, 256)

        def one_head_back(head, unused):
            head_rows = pl.ds(pl.multiple_of(head * HEAD, HEAD), HEAD)
            queries = head_lanes(qkv[rows, 0:128], head) * low(0.125)
            grads = tree_rows[2 * block : 2 * block + 2].reshape(256, 128)
            grad_rows = head_lanes(grads, head)
            lse = logs[pl.ds(pl.multiple_of(head * 8, 8), 8), block * 256 : block * 256 + 256][0:1]
            both = grads.T.astype(full) * mixed[:, block * 256 : block * 256 + 256]
            delta = jnp.where(
                head == 0,
                jnp.sum(both[:HEAD], axis=0, keepdims=True),
                jnp.sum(both[HEAD:], axis=0, keepdims=True),
            )
            grad_query = None
            for first, number, scores in score_parts(
                block, qkv.at[:, pl.ds(128, 128)], queries, masks
            ):
                keys = pl.ds(first, number)
                weights = jnp.exp(scores - lse)
                grad_weights = times_t(qkv[keys, 256:384], grad_rows)
                grad_scores = (weights * (grad_weights - delta)).astype(low)
                dk[keys, :] += jnp.dot(grad_scores, queries, preferred_element_type=full)
                dv[keys, :] += jnp.dot(weights.astype(low), grad_rows, preferred_element_type=full)
                term = jnp.dot(side_t[head_rows, keys], grad_scores, preferred_element_type=full)
                grad_query = term if grad_query is None else grad_query + term
            dq_t[head_rows, block * 256 : block * 256 + 256] = grad_query * 0.125
            return unused

        lax.fori_loop(0, 2, one_head_back, 0)
        if block == 0:
            rs_half(3, 1)
        if block == 1:
            rs_half(2, 0)
        if block == 5:
            rs_half(3, 0)
        if block == 4:
            outs[:, rep] = summed(outs[:, rep], cr_out[:, y]).astype(low)
            go_y.wait_recv()
            outs[:, rep] = summed(outs[:, rep], yr_out[...]).astype(low)
            ro_step(0)
        if block == 6:
            ro_step(1)

    for seg in range(16):
        rows = pl.ds(seg * 128, 128)
        qkv_slots[seg, :, 0:128] = dq_t[:, seg * 128 : seg * 128 + 128].T.astype(low)
        qkv_slots[seg, :, 128:256] = dk[rows, :].astype(low)
        qkv_slots[seg, :, 256:384] = dv[rows, :].astype(low)
    for slot in range(16):
        gq_slots[slot // 2, (slot % 2) * 128 : (slot % 2) * 128 + 128, :] = qkv_slots[ids_ref[slot]]

    def ge_copy(flow, step, half):
        return remote(
            acts.at[flow * 4 + step, half],
            w_all.at[flow * 4 + step, half],
            ge_s.at[flow, step, half],
            ge_r.at[flow, step, half],
            ring_device[flow],
        )

    def ge_part(block):
        return times_t(gq_slots[block], slices[...].reshape(1024, 384))

    def ge_step(step):
        made = [ge_part(flow_block(flow, 4 - step)) for flow in range(2)]
        for half in range(2):
            for flow in range(2):
                if step == 0 and half != flow:
                    continue
                rows = made[flow][half * 128 : half * 128 + 128]
                if step > 1 or (step == 1 and half == flow):
                    ge_copy(flow, step - 1, half).wait_recv()
                    rows = rows + w_all[flow * 4 + step - 1, half].astype(full)
                acts[flow * 4 + step, half] = rows.astype(low)
                ge_copy(flow, step, half).start()

    ge_step(0)
    ro_step(2)
    for block in range(8):
        gq_t[:, block * 256 : block * 256 + 256] = gq_slots[block].T
    fetch.wait()
    for copy in small:
        copy.wait_send()
    for s in range(8):
        made = jnp.dot(
            gq_t[...],
            xch[:, :, s * 128 : s * 128 + 128].reshape(2048, 128),
            preferred_element_type=full,
        )
        wq_send[s] = made.T.astype(low).reshape(2, 2, 32, 384)
    qs_over_core = remote(wq_send.at[:, :, 1 - core], qs_core, qr_s.at[0], qr_r.at[0], over_core)
    qs_over_core.start()
    ge_step(1)
    qs_over_core.wait_recv()
    qs_half[...] = summed(wq_send[:, :, core], qs_core[...]).astype(low)
    qs_over_y = remote(qs_half.at[:, 1 - y], qs_y, qr_s.at[1], qr_r.at[1], over_y)
    qs_over_y.start()
    ro_step(3)
    ge_step(2)
    qs_over_y.wait_recv()
    qs_half[:, y] = summed(qs_half[:, y], qs_y[...]).astype(low)
    qs_sends = [
        remote(
            qs_half.at[at.other(step), y],
            qs_recv.at[me],
            qs_s.at[step],
            qs_r.at[step],
            (rep, at.other(step)),
        )
        for step in range(1, 8)
    ]
    for copy in qs_sends:
        copy.start()
    qs_recv[me] = qs_half[me, y]

    def final_copy(kind, leg):
        quarter = at.rep_y if leg == 2 else rep
        if kind == 0:
            spot = fin_up.at[quarter]
        elif kind == 1:
            spot = down_out.at[pl.ds(quarter * 128, 128), :]
        elif kind == 2:
            spot = out_out.at[pl.ds(quarter * 32, 32), :]
        else:
            spot = qkv_out.at[pl.ds(quarter * 32, 32), :]
        device = over_y if leg == 0 else over_core
        return remote(spot, spot, fin_s.at[kind, leg], fin_r.at[kind, leg], device)

    for half in range(2):
        for flow in range(2):
            rs_copy(flow, 3, half).wait_recv()
        total = summed(gw[me, half], rr[0, 3, half], rr[1, 3, half]).astype(low)
        if half == 0:
            fin_up[rep] = total
        else:
            down_out[pl.ds(rep * 128, 128), :] = total
        final_copy(half, 0).start()
        final_copy(half, 1).start()
    for flow in range(2):
        ro_copy(flow, 3).wait_recv()
    out_out[pl.ds(rep * 32, 32), :] = summed(outs[me, rep], rr_out[0, 3], rr_out[1, 3]).astype(low)
    final_copy(2, 0).start()
    final_copy(2, 1).start()
    ge_step(3)
    part_copy(1, 1).wait_recv()
    part_copy(1, 2).wait_recv()
    tok_all[6] = summed(stage[0:2].reshape(256, 1024), parts[4], parts[5]).astype(low)
    layer_write = pltpu.make_async_copy(tok_all.at[6], layer_ref, load_s.at[1])
    layer_write.start()
    for copy in qs_sends:
        copy.wait_recv()
    quarter_rows = pl.ds(rep * 32, 32)
    for s in range(8):
        total = qs_recv[s]
        for j in range(3):
            first = j * 1024 + s * 128
            qkv_out[quarter_rows, first : first + 128] = total[:, j * 128 : j * 128 + 128]
    final_copy(3, 0).start()
    final_copy(3, 1).start()
    for kind in range(4):
        final_copy(kind, 0).wait_recv()
        final_copy(kind, 2).start()

    grad_entered = ge_part(me)
    for flow in range(2):
        ge_copy(flow, 3, 0).wait_recv()
        ge_copy(flow, 3, 1).wait_recv()
        grad_entered = grad_entered + w_all[flow * 4 + 3].reshape(256, 1024).astype(full)
    normed, inv_std = normed_rows(tok_ref[...].astype(full))
    gain_one = jnp.sum(grad_entered * normed, axis=0, keepdims=True)
    for s in range(8):
        gp[s, 0:8, :] = jnp.broadcast_to(gain_one[:, s * 128 : s * 128 + 128], (8, 128))
    gain_sends = [
        remote(
            gp.at[at.other(step)],
            gp_recv.at[me],
            gp_s.at[step],
            gp_r.at[step],
            (rep, at.other(step)),
        )
        for step in range(1, 8)
    ]
    for copy in gain_sends:
        copy.start()
    gp_recv[me] = gp[me]
    in_grad = stage[2:4].reshape(256, 1024) + norm_back(
        grad_entered * gain_row(gains_ref, 0), normed, inv_std
    )
    stage[4] = in_grad[:128]
    stage[5] = in_grad[128:]
    in_write = pltpu.make_async_copy(stage.at[4:6], in_ref, load_s.at[2])
    in_write.start()
    for copy in gain_sends:
        copy.wait_recv()
    total = gp_recv[0]
    for s in range(1, 8):
        total = total + gp_recv[s]
    gp_rep[rep] = total
    rep_sends = [
        remote(gp_rep.at[rep], gp_rep.at[rep], gr_s.at[i], gr_r.at[i], (to, me))
        for i, to in enumerate((at.rep_y, at.rep_core, at.rep_far))
    ]
    for copy in rep_sends:
        copy.start()
    for kind in range(4):
        final_copy(kind, 1).wait_recv()
        final_copy(kind, 2).wait_recv()
    for quarter in range(4):
        for s in range(8):
            first = s * 512 + quarter * 128
            up_out[:, first : first + 128] = fin_up[quarter, :, s * 128 : s * 128 + 128]
    for copy in rep_sends:
        copy.wait()
    gain_out[...] = gp_rep[0] + gp_rep[1] + gp_rep[2] + gp_rep[3]

    layer_write.wait()
    in_write.wait()
    for kind in range(4):
        for leg in range(3):
            final_copy(kind, leg).wait_send()
    qs_over_y.wait_send()
    qs_over_core.wait_send()
    go_y.wait_send()
    for copy in go_core + qs_sends + gain_sends + do_sends:
        copy.wait_send()
    slice_core.wait_send()
    for kind in range(2):
        for leg in range(3):
            part_copy(kind, leg).wait_send()
    for step in range(4):
        for flow in range(2):
            for half in range(2):
                if step > 0 or half == flow:
                    ge_copy(flow, step, half).wait_send()
                    rs_copy(flow, step, half).wait_send()
        for flow in ro_flows(step):
            ro_copy(flow, step).wait_send()


def widen_kernel(*refs):
    for source, target in zip(refs[:6], refs[7:13]):
        target[...] = source[...].astype(target.dtype)
    refs[13][...] = refs[6][0:1, :]
    refs[14][...] = refs[6][8:9, :]


W_START = 2
W_BLOCKS = [0, 4, 7]


def fast_shards(
    tokens, cotangent, qkv_weight, out_weight, up_weight, down_weight, gain_attn, gain_ffn, parents, slot_ids
):
    low, full = jnp.bfloat16, jnp.float32
    smem = pl.BlockSpec(memory_space=pltpu.SMEM)
    vmem = pl.BlockSpec(memory_space=pltpu.VMEM)
    anywhere = pl.BlockSpec(memory_space=pl.ANY)

    def dma(*shape):
        return pltpu.SemaphoreType.DMA(shape)

    v = pltpu.VMEM
    scratch = [
        v((6, 128, 1024), full),
        v((16, 128), low),
        v((8, 2, 2, 32, 384), low),
        v((8, 2, 2, 32, 384), low),
        v((8, 16, 128), low),
        v((8, 256, 1024), low),
        v((16, 128, 384), low),
        v((2048, 384), low),
        v((128, 2048), low),
        v((16, 128, 128), low),
        v((8, 256, 128), low),
        v((128, 2048), full),
        v((16, 2048), full),
        v((256, 1024), low),
        v((8, 4, 32, 1024), low),
        v((8, 2, 128, 1024), low),
        v((8, 256, 1024), low),
        v((8, 2, 128, 1024), low),
        v((6, 256, 1024), low),
        v((8, 2, 128, 1024), low),
        v((2, 4, 2, 128, 1024), low),
        v((2, 4, 32, 1024), low),
        v((8, 2, 32, 1024), low),
        v((8, 32, 1024), low),
        v((8, 256, 128), low),
        v((2048, 128), full),
        v((2048, 128), full),
        v((384, 2048), low),
        v((8, 2, 32, 384), low),
        v((8, 2, 32, 384), low),
        v((8, 32, 384), low),
        v((8, 32, 384), low),
        v((4, 128, 1024), low),
        v((8, 16, 128), full),
        v((8, 16, 128), full),
        v((4, 16, 128), full),
        dma(13), dma(2, 8), dma(2, 8), dma(1), dma(1), dma(2, 4, 2), dma(2, 4, 2),
        dma(2, 4), dma(2, 4), dma(2, 4), dma(2, 4), dma(2, 2, 4), dma(2, 2, 4),
        dma(2, 4, 2), dma(2, 4, 2), dma(2), dma(8), dma(8), dma(3), dma(3), dma(3), dma(3),
        dma(6), dma(6), dma(8), dma(8), dma(3), dma(3), dma(2, 4, 2), dma(2, 4, 2),
        dma(2, 4), dma(2, 4), dma(4, 3), dma(4, 3), dma(2, 4, 2), dma(2, 4, 2), dma(8), dma(8),
        dma(2), dma(2), dma(8), dma(8), dma(3), dma(3),
    ]
    made = pl.pallas_call(
        layer_kernel,
        out_shape=[
            jax.ShapeDtypeStruct((256, 1024), low),
            jax.ShapeDtypeStruct((2, 128, 1024), full),
            jax.ShapeDtypeStruct((128, 3072), low),
            jax.ShapeDtypeStruct((128, 1024), low),
            jax.ShapeDtypeStruct((128, 4096), low),
            jax.ShapeDtypeStruct((512, 1024), low),
            jax.ShapeDtypeStruct((16, 128), full),
            jax.ShapeDtypeStruct((8, 256, 1024), low),
        ],
        in_specs=[smem] * 2 + [vmem] * 4 + [anywhere] * 4,
        out_specs=[anywhere] * 2 + [vmem] * 5 + [anywhere],
        scratch_shapes=scratch,
        compiler_params=pltpu.CompilerParams(
            collective_id=1, has_side_effects=True, vmem_limit_bytes=VMEM_LIMIT
        ),
    )(
        slot_ids, parents.reshape(16), tokens, cotangent, gain_attn.reshape(1, 128), gain_ffn.reshape(1, 128), qkv_weight, out_weight, up_weight,
        down_weight,
    )
    shapes = [(256, 1024), (256, 1024), (128, 3072), (128, 1024), (128, 4096), (512, 1024)]
    results = [made[0], made[1].reshape(256, 1024)] + list(made[2:7])

    def spec(shape):
        return pl.BlockSpec((shape[0] // 4, shape[1]), lambda i: (i, 0))

    gain_spec = pl.BlockSpec((1, 128), lambda i: (0, 0))
    last = pl.pallas_call(
        widen_kernel,
        grid=(4,),
        out_shape=[jax.ShapeDtypeStruct(shapes[0], low)]
        + [jax.ShapeDtypeStruct(shape, full) for shape in shapes[1:]]
        + [jax.ShapeDtypeStruct((1, 128), full)] * 2,
        in_specs=[spec(shape) for shape in shapes] + [pl.BlockSpec((16, 128), lambda i: (0, 0))],
        out_specs=[spec(shape) for shape in shapes] + [gain_spec] * 2,
    )(*results)
    return tuple(last[:6]) + (last[6].reshape(128), last[7].reshape(128))


VMEM_LIMIT = 61 * 2**20


def solution(mesh):
    in_specs = (
        P(("rep", "shard"), None),
        P(("rep", "shard"), None),
        P("shard", None),
        P("shard", None),
        P("shard", None),
        P("shard", None),
        P("shard"),
        P("shard"),
        P("rep", None),
        P("rep"),
    )
    out_specs = (
        P(("rep", "shard"), None),
        P(("rep", "shard"), None),
        P("shard", None),
        P("shard", None),
        P("shard", None),
        P("shard", None),
        P("shard"),
        P("shard"),
    )

    def fits(*args):
        shapes = [a.shape for a in args]
        return shapes[0] == (8192, 1024) and shapes[4] == (1024, 4096) and shapes[8] == (4, 16)

    small = mesh.shape["rep"] == 4 and mesh.shape["shard"] == 8

    def whole(*args):
        run = fast_shards if small and fits(*args) else shards
        return jax.shard_map(
            run, mesh=mesh, in_specs=in_specs, out_specs=out_specs, check_vma=False
        )(*args)

    return whole
```
